32 devices in a mesh: gz: 2 (over y), xy: 16 (over z, x, core).
Axes of the slice: x: 2, y: 2, z: 4, core: 2. Of those that a mesh axis runs over, the one named last changes fastest.
Arguments:
- velocity_free: float32 [2, 16, 6, 512], P('gz', 'xy'), may hold values from -6 to 6
- inverse_mass: float32 [2, 16, 2, 512], P('gz', 'xy'), may hold values from 0.25 to 4
- jacobian: float32 [2, 16, 36, 2048], P('gz', 'xy'), may hold values from -1.75 to 1.75
- impulses: float32 [2, 16, 3, 2048], P('gz', 'xy'), may hold values from -6 to 6
- previous_impulses: float32 [2, 16, 3, 2048], P('gz', 'xy'), may hold values from -6 to 6
- compliance: float32 [2, 16, 2048], P('gz', 'xy'), may hold values from 0.05 to 0.5
- offset: float32 [2, 16, 2048], P('gz', 'xy'), may hold values from -6 to 6
- friction: float32 [2, 16, 2048], P('gz', 'xy'), may hold values from 0.2 to 0.8
- body_near: int32 [2, 16, 2048], P('gz', 'xy'), may hold values from 0 to 511
- body_far: int32 [2, 16, 2048], P('gz', 'xy'), may hold values from 0 to 1023
- block_counts: int32 [2, 16, 16], P('gz', 'xy'), may hold values from 0 to 128, as said below
- layer_send: int32 [2, 16, 128], P('gz', 'xy'), may hold values from 0 to 511
- side_send: int32 [2, 16, 2, 192], P('gz', 'xy'), may hold values from 0 to 639
Outputs:
- impulses_out: float32 [2, 16, 3, 2048], P('gz', 'xy')
- velocity_out: float32 [2, 16, 6, 512], P('gz', 'xy')
The draws below stay inside these ranges and needn't reach their ends.
Inputs may be any that keep to these rules, and one draw needn't show every extreme that they name: `block_counts`: on each device the blocks that hold live contacts come first, every one of them but the last full; some device holds 2048 live contacts. `body_far`: entries of 512 or more name received rows: 512 + i is the row received as the i-th from the layer above, then 192 rows from the lower-side and 192 from the higher-side neighbour. `side_send`: entries of 512 or more name rows received from the layer above.
All inputs are finite; a program needn't handle non-finite values.
Results may differ from the reference program's by a relative error of at most 0.0003.
Values sent between devices are 32-bit elements; how exact they have to be, the bound alone decides.
No kernel may reach another device: no remote copies, remote signals or barrier semaphores. Data moves between devices by JAX's collectives and lax.ppermute only.
A program may use at most 64 MiB of HBM per device.

```python
import math
import jax
import jax.numpy as jnp
from jax import lax

CB = 16
BLOCK = 128
ITERS = 2
LAYERS = 2
CELLS = 16
CON = 2048
SPH = 512
GZS = 128
XS = 192
EXT = 1024


def draw_block_counts(key, part):
    factor_key, chosen_key = jax.random.split(key, 2)
    layer_index = jnp.arange(LAYERS, dtype=jnp.int32)[:, None]
    cell_index = jnp.arange(CELLS, dtype=jnp.int32)[None, :]
    layer_total = CON * (3 * (LAYERS - 1) - 2 * layer_index) // (3 * (LAYERS - 1))
    random_root = jax.random.randint(factor_key, (LAYERS, CELLS), 0, 17)
    live_total = layer_total * (256 + 3 * random_root * random_root) // 1024
    chosen_cell = jax.random.randint(chosen_key, (), 0, CELLS)
    live_total = jnp.where((layer_index == 0) & (cell_index == chosen_cell), CON, live_total)
    slot_excess = live_total[:, :, None] - BLOCK * jnp.arange(CB, dtype=jnp.int32)[None, None, :]
    return jnp.clip(slot_excess, 0, BLOCK).astype(jnp.int32)


def plant(values, stream_key, low, top_value):
    shape = values.shape
    index_at = [jax.random.randint(jax.random.fold_in(stream_key, axis), (), 0, shape[axis]) for axis in range(len(shape))]
    values = values.at[tuple(index_at)].set(low)
    longest = shape.index(max(shape))
    index_at[longest] = (index_at[longest] + 1) % shape[longest]
    return values.at[tuple(index_at)].set(top_value)


def block_scale(rng, dims, cuts, least, top_value):
    gain = 1.0
    for dim, shards_of in cuts:
        steps = jax.random.uniform(jax.random.fold_in(jax.random.fold_in(rng, 6), dim), (shards_of,), jnp.float32, least / len(cuts), top_value / len(cuts))
        gain = gain * jnp.repeat(jnp.exp(steps), dims[dim] // shards_of).reshape((-1,) + (1,) * (len(dims) - 1 - dim))
    return gain


def scatter_about(stream_key, shape, width, most, pieces=(), kind=jnp.bfloat16):
    loudness = block_scale(stream_key, shape, pieces, -0.22, 0.18) if pieces else 1.0
    values = jax.random.normal(stream_key, shape, jnp.float32) * width * loudness
    return jnp.minimum(jnp.maximum(values, -most), most).astype(kind)


def setup_inputs(seed: int = 0) -> dict:
    splits = jax.random.split(jax.random.key(seed), 14)
    velocity_free = scatter_about(splits[0], (LAYERS, CELLS, 6, SPH), 1.0, 6.0, ((0, 2), (1, 16)), jnp.float32)
    inverse_mass = jnp.clip(jnp.exp(math.log(4.0) - 2.7725887 * jax.random.uniform(splits[1], (LAYERS, CELLS, 2, SPH), jnp.float32) ** block_scale(splits[1], (LAYERS, CELLS, 2, SPH), ((0, 2), (1, 16)), -0.2, 0.2)), 0.25, 4.0)
    jacobian = scatter_about(splits[2], (LAYERS, CELLS, 36, CON), 12 ** -0.5, 1.75, ((0, 2), (1, 16)), jnp.float32)
    impulses = scatter_about(splits[3], (LAYERS, CELLS, 3, CON), 1.0, 6.0, ((0, 2), (1, 16)), jnp.float32)
    previous_impulses = scatter_about(splits[4], (LAYERS, CELLS, 3, CON), 1.0, 6.0, ((0, 2), (1, 16)), jnp.float32)
    compliance = jnp.clip(jnp.exp(math.log(0.5) - 2.3025851 * jax.random.uniform(splits[5], (LAYERS, CELLS, CON), jnp.float32) ** block_scale(splits[5], (LAYERS, CELLS, CON), ((0, 2), (1, 16)), -0.2, 0.2)), 0.05, 0.5)
    offset = scatter_about(splits[6], (LAYERS, CELLS, CON), 1.0, 6.0, ((0, 2), (1, 16)), jnp.float32)
    friction = jnp.clip(jnp.exp(math.log(0.8) - 1.3862944 * jax.random.uniform(splits[7], (LAYERS, CELLS, CON), jnp.float32) ** block_scale(splits[7], (LAYERS, CELLS, CON), ((0, 2), (1, 16)), -0.2, 0.2)), 0.2, 0.8)
    body_near = plant(jax.random.randint(splits[8], (LAYERS, CELLS, CON), 0, SPH), jax.random.fold_in(splits[8], 1), 0, SPH - 1).astype(jnp.int32)
    body_far = plant(jax.random.randint(splits[9], (LAYERS, CELLS, CON), 0, EXT), jax.random.fold_in(splits[9], 1), 0, EXT - 1).astype(jnp.int32)
    block_counts = draw_block_counts(jax.random.fold_in(splits[13], 71), 0)
    layer_send = plant(jax.random.randint(splits[11], (LAYERS, CELLS, GZS), 0, SPH), jax.random.fold_in(splits[11], 1), 0, SPH - 1).astype(jnp.int32)
    side_send = plant(jax.random.randint(splits[12], (LAYERS, CELLS, 2, XS), 0, SPH + GZS), jax.random.fold_in(splits[12], 1), 0, (SPH + GZS) - 1).astype(jnp.int32)
    return {"velocity_free": velocity_free, "inverse_mass": inverse_mass, "jacobian": jacobian, "impulses": impulses, "previous_impulses": previous_impulses, "compliance": compliance, "offset": offset, "friction": friction, "body_near": body_near, "body_far": body_far, "block_counts": block_counts, "layer_send": layer_send, "side_send": side_send}


EPSILON = 1e-06
THETA_START = 0.3

def theta_after(theta_value):
    return 0.5 * (-theta_value * theta_value + theta_value * math.sqrt(theta_value * theta_value + 4.0))

def momentum_factors(iteration_count):
    thetas = [THETA_START]
    for iteration in range(iteration_count):
        thetas.append(theta_after(thetas[-1]))
    return [thetas[position] * (1.0 - thetas[position]) / (thetas[position] * thetas[position] + thetas[position + 1]) for position in range(iteration_count)]

def contact_rows(jacobian_dev, extended, near_index, far_index):
    blocks = jacobian_dev.reshape(3, 12, -1)
    near_rows = extended[:, near_index]
    far_rows = extended[:, far_index]
    return lax.optimization_barrier(jnp.sum(blocks[:, :6] * near_rows[None], axis=1)) + lax.optimization_barrier(jnp.sum(blocks[:, 6:] * far_rows[None], axis=1))

def sphere_terms(jacobian_dev, impulse, near_index, far_index, base_terms):
    blocks = jacobian_dev.reshape(3, 12, -1)
    spread = lax.optimization_barrier(jnp.sum(blocks * impulse[:, None], axis=0))
    return base_terms.at[:, near_index].add(spread[:6]).at[:, far_index].add(spread[6:])

def cone_project(impulse_value, cone_friction):
    normal = impulse_value[0]
    tangent = impulse_value[1:]
    slide_norm = jnp.sqrt(tangent[0] * tangent[0] + tangent[1] * tangent[1])
    inside_cone = slide_norm <= cone_friction * normal
    polar_cone = cone_friction * slide_norm <= -normal
    outside_both = jnp.logical_not(jnp.logical_or(inside_cone, polar_cone))
    onto_normal = (cone_friction * slide_norm + normal) / (cone_friction * cone_friction + 1.0)
    tangent_scale = cone_friction * onto_normal / jnp.where(outside_both, slide_norm, 1.0)
    new_normal = jnp.where(inside_cone, normal, jnp.where(polar_cone, 0.0, onto_normal))
    new_tangent = jnp.where(inside_cone[None], tangent, jnp.where(polar_cone[None], 0.0, tangent_scale[None] * tangent))
    return jnp.concatenate([new_normal[None], new_tangent], axis=0)

def take_columns(field, index_list):
    return field[:, index_list]

def add_columns(base_terms, values, index_list):
    return base_terms.at[:, index_list].add(values)

def spread_field(field, layer_send, side_send):
    take = jax.vmap(jax.vmap(take_columns))
    upper_rows = take(field, layer_send)
    upper_rows = jnp.concatenate([upper_rows[1:], jnp.zeros_like(upper_rows[:1])], axis=0)
    first_section = jnp.concatenate([field, upper_rows], axis=3)
    to_lower = take(first_section, side_send[:, :, 0])
    to_higher = take(first_section, side_send[:, :, 1])
    from_lower = jnp.concatenate([jnp.zeros_like(to_higher[:, :1]), to_higher[:, :-1]], axis=1)
    from_higher = jnp.concatenate([to_lower[:, 1:], jnp.zeros_like(to_lower[:, :1])], axis=1)
    return jnp.concatenate([first_section, from_lower, from_higher], axis=3)

def collect_terms(terms, layer_send, side_send):
    place = jax.vmap(jax.vmap(add_columns))
    section_rows = SPH + GZS
    first_section = terms[..., :section_rows]
    lower_part = terms[..., section_rows:section_rows + XS]
    higher_part = terms[..., section_rows + XS:]
    from_higher_cell = jnp.concatenate([lower_part[:, 1:], jnp.zeros_like(lower_part[:, :1])], axis=1)
    from_lower_cell = jnp.concatenate([jnp.zeros_like(higher_part[:, :1]), higher_part[:, :-1]], axis=1)
    first_section = place(first_section, from_higher_cell, side_send[:, :, 1])
    first_section = place(first_section, from_lower_cell, side_send[:, :, 0])
    layer_part = first_section[..., SPH:]
    from_below = jnp.concatenate([jnp.zeros_like(layer_part[:1]), layer_part[:-1]], axis=0)
    return place(first_section[..., :SPH], from_below, layer_send)

def reference(velocity_free, inverse_mass, jacobian, impulses, previous_impulses, compliance, offset, friction, body_near, body_far, block_counts, layer_send, side_send):
    device_count = LAYERS * CELLS

    def per_device(function, *arrays):
        flat = tuple((array.reshape((device_count,) + array.shape[2:]) for array in arrays))
        result = lax.map(lambda parts: function(*parts), flat)
        return result.reshape((LAYERS, CELLS) + result.shape[1:])

    def terms_dev(jacobian_dev, impulse_dev, near_dev, far_dev):
        return sphere_terms(jacobian_dev, impulse_dev, near_dev, far_dev, jnp.zeros((6, EXT), jnp.float32))
    weights = jnp.concatenate([jnp.repeat(inverse_mass[:, :, 0:1], 3, axis=2), jnp.repeat(inverse_mass[:, :, 1:2], 3, axis=2)], axis=2)
    slot_index = (jnp.arange(CON, dtype=jnp.int32) % BLOCK)[None, None, :]
    alive = (slot_index < jnp.repeat(block_counts, BLOCK, axis=2)).astype(jnp.float32)[:, :, None]
    zeros_rows = jnp.zeros_like(offset)
    offset_rows = jnp.stack([offset, zeros_rows, zeros_rows], axis=2)
    softness = compliance[:, :, None]

    def velocity_of(impulse):
        terms = per_device(terms_dev, jacobian, impulse, body_near, body_far)
        return velocity_free + weights * collect_terms(terms, layer_send, side_send)
    factors = momentum_factors(ITERS)
    current = alive * impulses
    earlier = alive * previous_impulses
    guess = alive * (current + factors[0] * (current - earlier))
    for iteration in range(ITERS):
        extended = spread_field(velocity_of(guess), layer_send, side_send)
        rows_now = per_device(contact_rows, jacobian, extended, body_near, body_far)
        gradient = alive * (rows_now + offset_rows + softness * guess)
        sphere_sums = collect_terms(per_device(terms_dev, jacobian, gradient, body_near, body_far), layer_send, side_send)
        norm_sq = jnp.sum(gradient * gradient)
        curvature = jnp.sum(weights * sphere_sums * sphere_sums) + jnp.sum(softness * gradient * gradient)
        step_size = norm_sq / (curvature + EPSILON)
        updated = alive * per_device(cone_project, guess - step_size * gradient, friction)
        if iteration + 1 < ITERS:
            guess = alive * (updated + factors[iteration + 1] * (updated - current))
        current = updated
    return (current, velocity_of(current))
```

```python
import math

import jax
import jax.numpy as jnp
from jax import lax
from jax.experimental import pallas as pl
from jax.experimental.pallas import tpu as pltpu
from jax.sharding import PartitionSpec as P

ITERS = 2
EPSILON = 1e-06
THETA_START = 0.3
LANES = 128
WIDE = 256
F32 = jnp.float32
BF16 = jnp.bfloat16
I32 = jnp.int32


def theta_after(theta_value):
    return 0.5 * (
        -theta_value * theta_value + theta_value * math.sqrt(theta_value * theta_value + 4.0)
    )


def momentum_factors(iteration_count):
    thetas = [THETA_START]
    for iteration in range(iteration_count):
        thetas.append(theta_after(thetas[-1]))
    return [
        thetas[position]
        * (1.0 - thetas[position])
        / (thetas[position] * thetas[position] + thetas[position + 1])
        for position in range(iteration_count)
    ]


def pair_swaps(count, parity):
    target = list(range(count))
    for cell in range(parity, count - 1, 2):
        target[cell], target[cell + 1] = cell + 1, cell
    return list(enumerate(target))


class Sizes:
    def __init__(self, contacts, own, layer, side, slots, cells):
        self.contacts, self.own, self.layer, self.side = contacts, own, layer, side
        self.slots, self.cells = slots, cells
        self.blocks = contacts // LANES
        self.section = own + layer
        self.total = self.section + 2 * side
        self.window = -(-side // LANES) * LANES
        self.own_groups = own // LANES
        self.section_groups = self.section // LANES
        self.total_groups = self.total // LANES
        self.window_groups = self.window // LANES
        assert contacts % LANES == own % WIDE == layer % LANES == 2 * side % LANES == 0
        self.tile_row = 48 * self.blocks
        self.misc_row = self.tile_row + 12 * self.blocks
        self.weight_group = self.own_groups
        self.layer_group = 2 * self.own_groups
        self.side_group = self.layer_group + layer // LANES
        self.misc_groups = self.side_group + self.window_groups
        self.rows = self.misc_row + 8 * self.misc_groups


NEAR, FAR, ALIVE, FRICTION, SOFTNESS, OFFSET, CURRENT, GUESS = 0, 1, 2, 3, 4, 5, 6, 9


class Packed:
    def __init__(self, ref, sizes):
        self.ref, self.sizes = ref, sizes

    def near_part(self, block, row):
        return self.ref[pl.ds(block * 48 + row * 16, 8), :]

    def far_part(self, block, row):
        return self.ref[pl.ds(block * 48 + row * 16 + 8, 8), :]

    def tile(self, which):
        blocks = self.sizes.blocks
        return self.ref[pl.ds(self.sizes.tile_row + which * blocks, blocks), :]

    def misc(self, group):
        return self.ref[pl.ds(self.sizes.misc_row + group * 8, 8), :]

    def free(self, group):
        return self.misc(group)

    def weight(self, group):
        return self.misc(self.sizes.weight_group + group)

    def layer_list(self, group):
        return self.misc(self.sizes.layer_group + group)[0:1].astype(I32)

    def side_list(self, which, group):
        return self.misc(self.sizes.side_group + group)[which : which + 1].astype(I32)


def gather(groups, index):
    lane = jnp.broadcast_to(index & (LANES - 1), (8, LANES))
    which = jnp.broadcast_to(index >> 7, (8, LANES))
    out = jnp.zeros((8, LANES), F32)
    for number, group in enumerate(groups):
        picked = jnp.take_along_axis(group, lane, axis=1, mode="promise_in_bounds")
        out = jnp.where(which == number, picked, out)
    return out


def put_columns(pieces, columns, spread_ref, hot_ref):
    wide_groups = -(-columns // WIDE)
    row_number = lax.broadcasted_iota(I32, (WIDE, LANES), 0)
    for at, (values, index) in enumerate(pieces):
        lanes = pl.ds(at * LANES, LANES)
        upper = values.astype(BF16).astype(F32)
        both = jnp.concatenate([upper, values - upper], axis=0)
        which = jnp.broadcast_to(index >> 8, (16, LANES))
        for number in range(wide_groups):
            part = jnp.where(which == number, both, 0.0)
            spread_ref[pl.ds(number * 16, 16), lanes] = part.astype(BF16)
        low = jnp.broadcast_to(index & (WIDE - 1), (WIDE, LANES))
        hot_ref[:, lanes] = jnp.where(row_number == low, 1.0, 0.0).astype(BF16)
    length = len(pieces) * LANES
    out = lax.dot_general(
        spread_ref[pl.ds(0, wide_groups * 16), pl.ds(0, length)],
        hot_ref[:, pl.ds(0, length)],
        (((1,), (1,)), ((), ())),
        preferred_element_type=F32,
    )
    return [out[g * 16 : g * 16 + 8] + out[g * 16 + 8 : g * 16 + 16] for g in range(wide_groups)]


def halves(wide):
    return [piece for w in wide for piece in (w[:, :LANES], w[:, LANES:])]


def contact_terms(packed, impulse, sizes, spread_ref, hot_ref):
    near, far = packed.tile(NEAR).astype(I32), packed.tile(FAR).astype(I32)
    near_pieces, far_pieces = [], []
    for block in range(sizes.blocks):
        near_value = far_value = None
        for row in range(3):
            value = impulse[row][block : block + 1]
            n, f = packed.near_part(block, row) * value, packed.far_part(block, row) * value
            near_value = n if near_value is None else near_value + n
            far_value = f if far_value is None else far_value + f
        near_pieces.append((near_value, near[block : block + 1]))
        far_pieces.append((far_value, far[block : block + 1]))
    far_groups = halves(put_columns(far_pieces, sizes.total, spread_ref, hot_ref))
    near_groups = halves(put_columns(near_pieces, sizes.own, spread_ref, hot_ref))
    for number, group in enumerate(near_groups):
        far_groups[number] = far_groups[number] + group
    return far_groups[: sizes.total_groups]


def store_terms(groups, slot, sizes, flags, section_ref, first_ref, second_ref):
    even = flags[0] == 0
    for group in range(sizes.section_groups):
        section_ref[slot, :, pl.ds(group * LANES, LANES)] = groups[group]
    for group in range(sizes.window_groups):
        lower = groups[sizes.section_groups + group]
        higher = groups[sizes.total_groups - sizes.window_groups + group]
        lanes = pl.ds(group * LANES, LANES)
        first_ref[slot, :, lanes] = jnp.where(even, higher, lower)
        second_ref[slot, :, lanes] = jnp.where(even, lower, higher)


def received(slot, group, flags, first_ref, second_ref):
    even = flags[0] == 0
    lanes = pl.ds(group * LANES, LANES)
    first, second = first_ref[slot, :, lanes], second_ref[slot, :, lanes]
    lower = jnp.where(flags[1] != 0, jnp.where(even, second, first), 0.0)
    higher = jnp.where(flags[2] != 0, jnp.where(even, first, second), 0.0)
    return lower, higher


def collect(packs, sizes, flags, section_ref, first_ref, second_ref, spread_ref, hot_ref, only=None):
    slots = sizes.slots
    sections = []
    for slot in range(slots):
        pieces = []
        for group in range(sizes.window_groups):
            lower, higher = received(slot, group, flags, first_ref, second_ref)
            pieces.append((higher, packs[slot].side_list(1, group)))
            pieces.append((lower, packs[slot].side_list(0, group)))
        added = halves(put_columns(pieces, sizes.section, spread_ref, hot_ref))
        sections.append(
            [
                section_ref[slot, :, pl.ds(group * LANES, LANES)] + added[group]
                for group in range(sizes.section_groups)
            ]
        )
    result = []
    for slot in range(slots):
        own = sections[slot][: sizes.own_groups]
        if slots > 1:
            below = (slot + slots - 1) % slots
            under = flags[3 + below] != 0
            pieces = [
                (
                    jnp.where(under, sections[below][sizes.own_groups + group], 0.0),
                    packs[slot].layer_list(group),
                )
                for group in range(sizes.layer // LANES)
            ]
            added = halves(put_columns(pieces, sizes.own, spread_ref, hot_ref))
            own = [a + b for a, b in zip(own, added)]
        result.append(own)
    return result


def gradient_rows(packed, table, sizes, rows_ref):
    near, far = packed.tile(NEAR).astype(I32), packed.tile(FAR).astype(I32)
    own = table[: sizes.own_groups]
    for block in range(sizes.blocks):
        near_value = gather(own, near[block : block + 1])
        far_value = gather(table, far[block : block + 1])
        for row in range(3):
            terms = packed.near_part(block, row) * near_value + packed.far_part(block, row) * far_value
            rows_ref[row, pl.ds(block, 1), :] = jnp.sum(terms, axis=0, keepdims=True)


def cone_project(impulse_value, cone_friction):
    normal, first, second = impulse_value
    slide_norm = jnp.sqrt(first * first + second * second)
    inside_cone = slide_norm <= cone_friction * normal
    polar_cone = cone_friction * slide_norm <= -normal
    outside_both = jnp.logical_not(jnp.logical_or(inside_cone, polar_cone))
    onto_normal = (cone_friction * slide_norm + normal) / (cone_friction * cone_friction + 1.0)
    tangent_scale = cone_friction * onto_normal / jnp.where(outside_both, slide_norm, 1.0)
    scale = jnp.where(inside_cone, 1.0, jnp.where(polar_cone, 0.0, tangent_scale))
    new_normal = jnp.where(inside_cone, normal, jnp.where(polar_cone, 0.0, onto_normal))
    return [new_normal, scale * first, scale * second]


def call(body, out_shape, operands, scratch=(), smem=1):
    specs = [pl.BlockSpec(memory_space=pltpu.SMEM)] * smem
    specs += [pl.BlockSpec(memory_space=pltpu.VMEM)] * (len(operands) - smem)
    return pl.pallas_call(
        body,
        out_shape=[jax.ShapeDtypeStruct(shape, F32) for shape in out_shape],
        in_specs=specs,
        out_specs=[pl.BlockSpec(memory_space=pltpu.VMEM)] * len(out_shape),
        scratch_shapes=list(scratch),
        compiler_params=pltpu.CompilerParams(vmem_limit_bytes=40 * 1024 * 1024),
    )(*operands)


def on_device(
    velocity_free,
    inverse_mass,
    jacobian,
    impulses,
    previous_impulses,
    compliance,
    offset,
    friction,
    body_near,
    body_far,
    block_counts,
    layer_send,
    side_send,
):
    slots, cells = lax.axis_size("gz"), lax.axis_size("xy")
    layer_at, cell_at = lax.axis_index("gz"), lax.axis_index("xy")
    sizes = Sizes(
        jacobian.shape[3], velocity_free.shape[3], layer_send.shape[2], side_send.shape[3], slots, cells
    )
    blocks, window = sizes.blocks, sizes.window
    factors = momentum_factors(ITERS)

    flags = jnp.stack(
        [cell_at % 2, (cell_at > 0).astype(I32), (cell_at < cells - 1).astype(I32)]
        + [((layer_at + slot) % slots != slots - 1).astype(I32) for slot in range(slots)]
    ).astype(I32)

    def tiles(array):
        return array.reshape(-1, blocks, LANES)

    def pack_body(
        counts, free_ref, mass_ref, jac_ref, imp_ref, prev_ref, soft_ref, off_ref, fric_ref, near_ref,
        far_ref, layer_ref, side_ref, out_ref,
    ):
        gap = jnp.zeros((2, LANES), F32)
        for block in range(blocks):
            lanes = pl.ds(block * LANES, LANES)
            for part in range(6):
                rows = jac_ref[pl.ds(part * 6, 6), lanes]
                out_ref[pl.ds(block * 48 + part * 8, 8), :] = jnp.concatenate([rows, gap], axis=0)

        def put(which, value):
            out_ref[pl.ds(sizes.tile_row + which * blocks, blocks), :] = value

        put(NEAR, near_ref[0].astype(F32))
        put(FAR, far_ref[0].astype(F32))
        put(FRICTION, fric_ref[0])
        put(SOFTNESS, soft_ref[0])
        put(OFFSET, off_ref[0])
        lane = lax.broadcasted_iota(I32, (1, LANES), 1)
        rows = [jnp.where(lane < counts[block], 1.0, 0.0) for block in range(blocks)]
        alive = jnp.concatenate(rows, axis=0)
        put(ALIVE, alive)
        for row in range(3):
            current = alive * imp_ref[row]
            earlier = alive * prev_ref[row]
            put(CURRENT + row, current)
            put(GUESS + row, alive * (current + factors[0] * (current - earlier)))

        def misc(group, value):
            out_ref[pl.ds(sizes.misc_row + group * 8, 8), :] = value

        for group in range(sizes.own_groups):
            lanes = pl.ds(group * LANES, LANES)
            misc(group, jnp.concatenate([free_ref[:, lanes], gap], axis=0))
            mass = mass_ref[:, lanes]
            linear = jnp.broadcast_to(mass[0:1], (3, LANES))
            angular = jnp.broadcast_to(mass[1:2], (3, LANES))
            misc(sizes.weight_group + group, jnp.concatenate([linear, angular, gap], axis=0))
        for group in range(sizes.layer // LANES):
            lanes = pl.ds(group * LANES, LANES)
            rows = jnp.broadcast_to(layer_ref[:, lanes], (8, LANES))
            misc(sizes.layer_group + group, rows.astype(F32))
        for group in range(sizes.window_groups):
            lanes = pl.ds(group * LANES, LANES)
            rows = jnp.concatenate([side_ref[:, lanes]] * 4, axis=0)
            misc(sizes.side_group + group, rows.astype(F32))

    lists = side_send[0, 0]
    margin = window - sizes.side
    side_lists = jnp.stack(
        [
            jnp.pad(lists[0], (margin, 0), constant_values=-1),
            jnp.pad(lists[1], (0, margin), constant_values=-1),
        ]
    )
    (own_pack,) = call(
        pack_body,
        [(sizes.rows, LANES)],
        [
            block_counts[0, 0],
            velocity_free[0, 0],
            inverse_mass[0, 0],
            jacobian[0, 0],
            tiles(impulses[0, 0]),
            tiles(previous_impulses[0, 0]),
            tiles(compliance[0, 0]),
            tiles(offset[0, 0]),
            tiles(friction[0, 0]),
            tiles(body_near[0, 0]),
            tiles(body_far[0, 0]),
            layer_send[0],
            side_lists,
        ],
    )
    packs = [own_pack] + [
        lax.ppermute(own_pack, "gz", [((i + step) % slots, i) for i in range(slots)])
        for step in range(1, slots)
    ]

    side_shape = (slots, 8, window)
    section_shape = (slots, 8, sizes.section)
    tile_shape = (slots, 3, blocks, LANES)
    wide_groups = -(-sizes.total // WIDE)
    work = [
        pltpu.VMEM((wide_groups * 16, sizes.contacts), BF16),
        pltpu.VMEM((WIDE, sizes.contacts), BF16),
    ]
    to_first, to_second = pair_swaps(cells, 0), pair_swaps(cells, 1)

    def swap(first, second):
        return lax.ppermute(first, "xy", to_first), lax.ppermute(second, "xy", to_second)

    def wrap(refs):
        return [Packed(ref, sizes) for ref in refs]

    def first_terms():
        def body(flags, *refs):
            pack_refs, (section_ref, first_ref, second_ref, spread_ref, hot_ref) = refs[:slots], refs[slots:]
            for slot, pack in enumerate(wrap(pack_refs)):
                value = [pack.tile(GUESS + row) for row in range(3)]
                groups = contact_terms(pack, value, sizes, spread_ref, hot_ref)
                store_terms(groups, slot, sizes, flags, section_ref, first_ref, second_ref)

        return call(body, [section_shape, side_shape, side_shape], [flags, *packs], work)

    def spheres(section, first, second):
        def body(flags, section_ref, first_ref, second_ref, *refs):
            pack_refs, (out_ref, to_first_ref, to_second_ref, spread_ref, hot_ref) = refs[:slots], refs[slots:]
            pack = wrap(pack_refs)
            sums = collect(pack, sizes, flags, section_ref, first_ref, second_ref, spread_ref, hot_ref)
            velocity = [
                [pack[s].free(g) + pack[s].weight(g) * sums[s][g] for g in range(sizes.own_groups)]
                for s in range(slots)
            ]
            even = flags[0] == 0
            for slot in range(slots):
                above = (slot + 1) % slots
                table = list(velocity[slot])
                for group in range(sizes.layer // LANES):
                    upper = jnp.zeros((8, LANES), F32)
                    if slots > 1:
                        upper = gather(velocity[above], pack[above].layer_list(group))
                        upper = jnp.where(flags[3 + slot] != 0, upper, 0.0)
                    table.append(upper)
                for group, value in enumerate(table):
                    out_ref[slot, :, pl.ds(group * LANES, LANES)] = value
                for group in range(sizes.window_groups):
                    lanes = pl.ds(group * LANES, LANES)
                    to_lower = gather(table, pack[slot].side_list(0, group))
                    to_higher = gather(table, pack[slot].side_list(1, group))
                    to_first_ref[slot, :, lanes] = jnp.where(even, to_higher, to_lower)
                    to_second_ref[slot, :, lanes] = jnp.where(even, to_lower, to_higher)

        return call(
            body, [section_shape, side_shape, side_shape], [flags, section, first, second, *packs], work
        )

    def gradients(section, first, second, state):
        held = [] if state is None else [state]

        def body(flags, section_ref, first_ref, second_ref, *refs):
            pack_refs, refs = refs[:slots], refs[slots:]
            state_ref, refs = (refs[0], refs[1:]) if held else (None, refs)
            grad_ref, norm_ref, out_ref, to_first_ref, to_second_ref, spread_ref, hot_ref, rows_ref = refs
            lane = lax.broadcasted_iota(I32, (8, LANES), 1)
            edge = sizes.side % LANES
            norm = soft = jnp.zeros((blocks, LANES), F32)
            for slot, pack in enumerate(wrap(pack_refs)):
                table = [
                    section_ref[slot, :, pl.ds(g * LANES, LANES)] for g in range(sizes.section_groups)
                ]
                got = [
                    received(slot, g, flags, first_ref, second_ref) for g in range(sizes.window_groups)
                ]
                lower, higher = [a for a, b in got], [b for a, b in got]
                if edge:
                    table += lower[:-1]
                    table.append(jnp.where(lane < edge, lower[-1], higher[0]))
                    table += higher[1:]
                else:
                    table += lower + higher
                gradient_rows(pack, table, sizes, rows_ref)
                alive, softness = pack.tile(ALIVE), pack.tile(SOFTNESS)
                grad = []
                for row in range(3):
                    guess = pack.tile(GUESS + row) if state_ref is None else state_ref[slot, row]
                    value = rows_ref[row] + softness * guess
                    if row == 0:
                        value = value + pack.tile(OFFSET)
                    value = alive * value
                    grad_ref[slot, row] = value
                    grad.append(value)
                    norm = norm + value * value
                    soft = soft + softness * value * value
                groups = contact_terms(pack, grad, sizes, spread_ref, hot_ref)
                store_terms(groups, slot, sizes, flags, out_ref, to_first_ref, to_second_ref)
            norm_ref[0] = norm
            norm_ref[1] = soft

        return call(
            body,
            [tile_shape, (2, blocks, LANES), section_shape, side_shape, side_shape],
            [flags, section, first, second, *packs, *held],
            work + [pltpu.VMEM((3, blocks, LANES), F32)],
        )

    def curvatures(section, first, second, norms):
        def body(flags, section_ref, first_ref, second_ref, norm_ref, *refs):
            pack_refs, (out_ref, spread_ref, hot_ref) = refs[:slots], refs[slots:]
            pack = wrap(pack_refs)
            sums = collect(pack, sizes, flags, section_ref, first_ref, second_ref, spread_ref, hot_ref)
            curve = jnp.sum(norm_ref[1], axis=0, keepdims=True)
            norm = jnp.sum(norm_ref[0], axis=0, keepdims=True)
            total = jnp.zeros((8, LANES), F32)
            for slot in range(slots):
                for group in range(sizes.own_groups):
                    value = sums[slot][group]
                    total = total + pack[slot].weight(group) * value * value
            curve = curve + jnp.sum(total, axis=0, keepdims=True)
            both = jnp.concatenate([norm, curve, jnp.zeros((6, LANES), F32)], axis=0)
            for cell in range(cells):
                out_ref[cell] = both

        return call(body, [(cells, 8, LANES)], [flags, section, first, second, norms, *packs], work)[0]

    def updates(parts, grad, state, earlier, factor):
        held = [] if state is None else [state, earlier]
        last = factor is None

        def body(flags, part_ref, grad_ref, *refs):
            pack_refs, refs = refs[:slots], refs[slots:]
            if held:
                (state_ref, earlier_ref), refs = refs[:2], refs[2:]
            if last:
                result_ref, out_ref, to_first_ref, to_second_ref, spread_ref, hot_ref = refs
            else:
                result_ref, guess_ref, out_ref, to_first_ref, to_second_ref, spread_ref, hot_ref = refs
            total = part_ref[0]
            for cell in range(1, cells):
                total = total + part_ref[cell]
            sums = jnp.sum(total, axis=1, keepdims=True)
            step = sums[0:1] / (sums[1:2] + EPSILON)
            for slot, pack in enumerate(wrap(pack_refs)):
                alive = pack.tile(ALIVE)
                moved, before = [], []
                for row in range(3):
                    guess = state_ref[slot, row] if held else pack.tile(GUESS + row)
                    before.append(earlier_ref[slot, row] if held else pack.tile(CURRENT + row))
                    moved.append(guess - step * grad_ref[slot, row])
                value = [alive * v for v in cone_project(moved, pack.tile(FRICTION))]
                if last:
                    if slot == 0:
                        for row in range(3):
                            for block in range(blocks):
                                lanes = pl.ds(block * LANES, LANES)
                                result_ref[pl.ds(row, 1), lanes] = value[row][block : block + 1]
                else:
                    guess = [alive * (v + factor * (v - b)) for v, b in zip(value, before)]
                    for row in range(3):
                        result_ref[slot, row] = value[row]
                        guess_ref[slot, row] = guess[row]
                    value = guess
                groups = contact_terms(pack, value, sizes, spread_ref, hot_ref)
                store_terms(groups, slot, sizes, flags, out_ref, to_first_ref, to_second_ref)

        shapes = [(3, sizes.contacts)] if last else [tile_shape, tile_shape]
        return call(
            body,
            shapes + [section_shape, side_shape, side_shape],
            [flags, parts, grad, *packs, *held],
            work,
        )

    def last_spheres(section, first, second):
        def body(flags, section_ref, first_ref, second_ref, *refs):
            pack_refs, (out_ref, spread_ref, hot_ref) = refs[:slots], refs[slots:]
            pack = wrap(pack_refs)
            sums = collect(pack, sizes, flags, section_ref, first_ref, second_ref, spread_ref, hot_ref)
            for group in range(sizes.own_groups):
                value = pack[0].free(group) + pack[0].weight(group) * sums[0][group]
                out_ref[:, pl.ds(group * LANES, LANES)] = value[:6]

        return call(body, [(6, sizes.own)], [flags, section, first, second, *packs], work)[0]

    state = earlier = None
    section, first, second = first_terms()
    for iteration in range(ITERS):
        section, first, second = spheres(section, *swap(first, second))
        grad, norms, section, first, second = gradients(section, *swap(first, second), state)
        parts = curvatures(section, *swap(first, second), norms)
        parts = lax.all_to_all(parts, "xy", 0, 0, tiled=True)
        if iteration + 1 < ITERS:
            earlier, state, section, first, second = updates(
                parts, grad, state, earlier, factors[iteration + 1]
            )
        else:
            result, section, first, second = updates(parts, grad, state, earlier, None)
    velocity = last_spheres(section, *swap(first, second))
    return (result[None, None], velocity[None, None])


def solution(mesh):
    placed = (
        P("gz", "xy", None, None),
        P("gz", "xy", None, None),
        P("gz", "xy", None, None),
        P("gz", "xy", None, None),
        P("gz", "xy", None, None),
        P("gz", "xy", None),
        P("gz", "xy", None),
        P("gz", "xy", None),
        P("gz", "xy", None),
        P("gz", "xy", None),
        P("gz", "xy", None),
        P("gz", "xy", None),
        P("gz", "xy", None, None),
    )
    return jax.shard_map(
        on_device,
        mesh=mesh,
        in_specs=placed,
        out_specs=(P("gz", "xy", None, None), P("gz", "xy", None, None)),
        check_vma=False,
    )
```

```python
import math

import jax
import jax.numpy as jnp
from jax import lax
from jax.experimental import pallas as pl
from jax.experimental.pallas import tpu as pltpu
from jax.sharding import PartitionSpec as P

ITERS = 2
EPSILON = 1e-06
THETA_START = 0.3
LANES = 128
WIDE = 256
F32 = jnp.float32
BF16 = jnp.bfloat16
I32 = jnp.int32


def theta_after(theta_value):
    return 0.5 * (
        -theta_value * theta_value + theta_value * math.sqrt(theta_value * theta_value + 4.0)
    )


def momentum_factors(iteration_count):
    thetas = [THETA_START]
    for iteration in range(iteration_count):
        thetas.append(theta_after(thetas[-1]))
    return [
        thetas[position]
        * (1.0 - thetas[position])
        / (thetas[position] * thetas[position] + thetas[position + 1])
        for position in range(iteration_count)
    ]


def pair_swaps(count, parity):
    target = list(range(count))
    for cell in range(parity, count - 1, 2):
        target[cell], target[cell + 1] = cell + 1, cell
    return list(enumerate(target))


class Sizes:
    def __init__(self, contacts, own, layer, side, slots, cells):
        self.contacts, self.own, self.layer, self.side = contacts, own, layer, side
        self.slots, self.cells = slots, cells
        self.blocks = contacts // LANES
        self.section = own + layer
        self.total = self.section + 2 * side
        self.window = -(-side // LANES) * LANES
        self.margin = self.window - side
        self.own_groups = own // LANES
        self.layer_groups = layer // LANES
        self.section_groups = self.section // LANES
        self.total_groups = self.total // LANES
        self.window_groups = self.window // LANES
        self.contact_rows = 48 * self.blocks
        self.layer_at = 2 * self.own_groups
        self.side_at = self.layer_at + self.layer_groups
        self.sphere_rows = 8 * (self.side_at + self.window_groups)
        self.sent = own + self.window
        assert contacts % LANES == own % LANES == layer % LANES == 2 * side % LANES == 0
        assert 8 >= 6 and self.blocks % 8 == 0


SPARE = [half * 8 + 16 * row + 6 + at for row in range(3) for half in range(2) for at in range(2)]
NEAR, FAR, ALIVE, FRICTION, SOFTNESS, OFFSET, CURRENT, GUESS = 0, 1, 2, 3, 4, 5, 6, 9


class Contacts:
    def __init__(self, ref, sizes):
        self.ref, self.sizes = ref, sizes

    def near_part(self, block, row):
        return self.ref[pl.ds(block * 48 + row * 16, 8), :]

    def far_part(self, block, row):
        return self.ref[pl.ds(block * 48 + row * 16 + 8, 8), :]

    def tile(self, which):
        return self.ref[pl.ds(SPARE[which], self.sizes.blocks, stride=48), :]


class Spheres:
    def __init__(self, ref, sizes):
        self.ref, self.sizes = ref, sizes

    def misc(self, group):
        return self.ref[pl.ds(group * 8, 8), :]

    def free(self, group):
        return self.misc(group)

    def weight(self, group):
        return self.misc(self.sizes.own_groups + group)

    def layer_list(self, group):
        return self.misc(self.sizes.layer_at + group)[0:1].astype(I32)

    def side_list(self, which, group):
        return self.misc(self.sizes.side_at + group)[which : which + 1].astype(I32)


def gather(groups, index):
    lane = jnp.broadcast_to(index & (LANES - 1), (8, LANES))
    which = jnp.broadcast_to(index >> 7, (8, LANES))
    out = jnp.zeros((8, LANES), groups[0].dtype)
    for number, group in enumerate(groups):
        picked = jnp.take_along_axis(group, lane, axis=1, mode="promise_in_bounds")
        out = jnp.where(which == number, picked, out)
    return out


def look_up(lists, index):
    groups = [jnp.broadcast_to(row, (8, LANES)) for row in lists]
    pieces = [gather(groups, index[at : at + 8]) for at in range(0, index.shape[0], 8)]
    return jnp.concatenate(pieces, axis=0) - 1


def spread_out(values, index, groups, at, spread_ref, hot_ref):
    lanes = pl.ds(at * LANES, LANES)
    upper = values.astype(BF16).astype(F32)
    both = jnp.concatenate([upper, values - upper], axis=0).astype(BF16)
    which = jnp.broadcast_to((index >> 7).astype(F32), (16, LANES)).astype(BF16)
    low = jnp.broadcast_to((index & (LANES - 1)).astype(F32), (16, LANES)).astype(BF16)
    for number in range(groups):
        part = jnp.where(which == jnp.asarray(number, BF16), both, jnp.zeros((16, LANES), BF16))
        spread_ref[pl.ds(number * 16, 16), lanes] = part
    row_number = lax.broadcasted_iota(I32, (LANES, LANES), 0).astype(F32).astype(BF16)
    for part in range(LANES // 16):
        rows = slice(part * 16, part * 16 + 16)
        hot = jnp.where(row_number[rows] == low, jnp.ones((16, LANES), BF16), jnp.zeros((16, LANES), BF16))
        hot_ref[pl.ds(part * 16, 16), lanes] = hot


def summed(groups, spread_ref, hot_ref):
    out = lax.dot_general(
        spread_ref[...], hot_ref[...], (((1,), (1,)), ((), ())), preferred_element_type=F32
    )
    return [out[g * 16 : g * 16 + 8] + out[g * 16 + 8 : g * 16 + 16] for g in range(groups)]


class Maps:
    def __init__(self, spheres, sizes, flags):
        self.spheres, self.sizes, self.flags = spheres, sizes, flags

    def upper(self, slot):
        above = self.spheres[(slot + 1) % self.sizes.slots]
        return [above.layer_list(group) for group in range(self.sizes.layer_groups)]

    def side(self, slot, which):
        picks = []
        for group in range(self.sizes.window_groups):
            to_lower = self.spheres[slot].side_list(0, group)
            to_higher = self.spheres[slot].side_list(1, group)
            higher = (self.flags[0] == 0) == (which == 1)
            picks.append(jnp.where(higher, to_higher, to_lower))
        return picks

    def window_index(self, far, which):
        sizes = self.sizes
        higher = (self.flags[0] == 0) == (which == 1)
        return far - jnp.where(higher, sizes.section, sizes.section + sizes.side - sizes.margin)

    def resolved(self, slot, which, far):
        sizes = self.sizes
        if which == 0:
            row = jnp.where(far < sizes.section, far, -1)
        else:
            row = look_up(self.side(slot, which), self.window_index(far, which))
            row = jnp.where(self.flags[which] != 0, row, -1)
        above = look_up(self.upper(slot), row - sizes.own) + sizes.own
        above = jnp.where(self.flags[3 + slot] != 0, above, -1)
        return jnp.where(row < sizes.own, row, above)


def collected(sets, values, maps, sizes, work):
    slots, own_groups = sizes.slots, sizes.own_groups
    spans = 2 * own_groups if slots > 1 else own_groups
    result = [[None] * own_groups for _ in range(slots)]

    def add(slot, group, value):
        held = result[slot][group]
        result[slot][group] = value if held is None else held + value

    for slot in range(slots):
        near_ref, near_hot, far_ref, far_hot = work[(slot % 2) * 4 : (slot % 2) * 4 + 4]
        for which in range(3):
            pack, value = sets[slot][which], values[slot][which]
            far = maps.resolved(slot, which, pack.tile(FAR).astype(I32))
            near = pack.tile(NEAR).astype(I32) if which == 0 else None
            for block in range(sizes.blocks):
                far_value = near_value = None
                for row in range(3):
                    line = value[row][block : block + 1]
                    term = pack.far_part(block, row) * line
                    far_value = term if far_value is None else far_value + term
                    if which == 0:
                        term = pack.near_part(block, row) * line
                        near_value = term if near_value is None else near_value + term
                at = which * sizes.blocks + block
                spread_out(far_value, far[block : block + 1], spans, at, far_ref, far_hot)
                if which == 0:
                    spread_out(near_value, near[block : block + 1], own_groups, block, near_ref, near_hot)
        for group, value in enumerate(summed(own_groups, near_ref, near_hot)):
            add(slot, group, value)
        for group, value in enumerate(summed(spans, far_ref, far_hot)):
            add((slot + group // own_groups) % slots, group % own_groups, value)
    return result


def rows_of(pack, own, table, index, sizes, rows_ref):
    near = pack.tile(NEAR).astype(I32)
    for block in range(sizes.blocks):
        near_value = gather(own, near[block : block + 1])
        far_value = gather(table, index[block : block + 1])
        for row in range(3):
            terms = pack.near_part(block, row) * near_value + pack.far_part(block, row) * far_value
            rows_ref[row, pl.ds(block, 1), :] = jnp.sum(terms, axis=0, keepdims=True)


def cone_project(impulse_value, cone_friction):
    normal, first, second = impulse_value
    slide_norm = jnp.sqrt(first * first + second * second)
    inside_cone = slide_norm <= cone_friction * normal
    polar_cone = cone_friction * slide_norm <= -normal
    outside_both = jnp.logical_not(jnp.logical_or(inside_cone, polar_cone))
    onto_normal = (cone_friction * slide_norm + normal) / (cone_friction * cone_friction + 1.0)
    tangent_scale = cone_friction * onto_normal / jnp.where(outside_both, slide_norm, 1.0)
    scale = jnp.where(inside_cone, 1.0, jnp.where(polar_cone, 0.0, tangent_scale))
    new_normal = jnp.where(inside_cone, normal, jnp.where(polar_cone, 0.0, onto_normal))
    return [new_normal, scale * first, scale * second]


def call(body, out_shape, operands, scratch=(), smem=1):
    specs = [pl.BlockSpec(memory_space=pltpu.SMEM)] * smem
    specs += [pl.BlockSpec(memory_space=pltpu.VMEM)] * (len(operands) - smem)
    return pl.pallas_call(
        body,
        out_shape=[jax.ShapeDtypeStruct(shape, F32) for shape in out_shape],
        in_specs=specs,
        out_specs=[pl.BlockSpec(memory_space=pltpu.VMEM)] * len(out_shape),
        scratch_shapes=list(scratch),
        compiler_params=pltpu.CompilerParams(vmem_limit_bytes=40 * 1024 * 1024),
    )(*operands)


def on_device(
    velocity_free,
    inverse_mass,
    jacobian,
    impulses,
    previous_impulses,
    compliance,
    offset,
    friction,
    body_near,
    body_far,
    block_counts,
    layer_send,
    side_send,
):
    slots, cells = lax.axis_size("gz"), lax.axis_size("xy")
    layer_at, cell_at = lax.axis_index("gz"), lax.axis_index("xy")
    sizes = Sizes(
        jacobian.shape[3], velocity_free.shape[3], layer_send.shape[2], side_send.shape[3], slots, cells
    )
    blocks, window = sizes.blocks, sizes.window
    factors = momentum_factors(ITERS)

    odd = cell_at % 2
    lower, higher = cell_at > 0, cell_at < cells - 1
    flags = jnp.stack(
        [odd, jnp.where(odd == 0, higher, lower), jnp.where(odd == 0, lower, higher)]
        + [(layer_at + slot) % slots != slots - 1 for slot in range(slots)]
    ).astype(I32)

    def tiles(array):
        return array.reshape(-1, blocks, LANES)

    def pack_body(
        counts, free_ref, mass_ref, jac_ref, imp_ref, prev_ref, soft_ref, off_ref, fric_ref, near_ref,
        far_ref, layer_ref, side_ref, out_ref, sphere_ref,
    ):
        lane = lax.broadcasted_iota(I32, (1, LANES), 1)
        for block in range(blocks):
            lanes = pl.ds(block * LANES, LANES)
            one = slice(block, block + 1)
            alive = jnp.where(lane < counts[block], 1.0, 0.0)
            spare = [
                near_ref[0, one].astype(F32), far_ref[0, one].astype(F32), alive,
                fric_ref[0, one], soft_ref[0, one], off_ref[0, one],
            ]
            current = [alive * imp_ref[row, one] for row in range(3)]
            earlier = [alive * prev_ref[row, one] for row in range(3)]
            spare += current
            spare += [alive * (c + factors[0] * (c - e)) for c, e in zip(current, earlier)]
            for part in range(6):
                rows = jac_ref[pl.ds(part * 6, 6), lanes]
                both = jnp.concatenate([rows, spare[2 * part], spare[2 * part + 1]], axis=0)
                out_ref[pl.ds(block * 48 + part * 8, 8), :] = both

        gap = jnp.zeros((2, LANES), F32)

        def misc(group, value):
            sphere_ref[pl.ds(group * 8, 8), :] = value

        for group in range(sizes.own_groups):
            lanes = pl.ds(group * LANES, LANES)
            misc(group, jnp.concatenate([free_ref[:, lanes], gap], axis=0))
            mass = mass_ref[:, lanes]
            linear = jnp.broadcast_to(mass[0:1], (3, LANES))
            angular = jnp.broadcast_to(mass[1:2], (3, LANES))
            misc(sizes.own_groups + group, jnp.concatenate([linear, angular, gap], axis=0))
        for group in range(sizes.layer_groups):
            lanes = pl.ds(group * LANES, LANES)
            rows = jnp.broadcast_to(layer_ref[:, lanes] + 1, (8, LANES))
            misc(sizes.layer_at + group, rows.astype(F32))
        for group in range(sizes.window_groups):
            lanes = pl.ds(group * LANES, LANES)
            rows = jnp.concatenate([side_ref[:, lanes] + 1] * 4, axis=0)
            misc(sizes.side_at + group, rows.astype(F32))

    lists = side_send[0, 0]
    side_lists = jnp.stack(
        [
            jnp.pad(lists[0], (sizes.margin, 0), constant_values=-1),
            jnp.pad(lists[1], (0, sizes.margin), constant_values=-1),
        ]
    )
    own_contacts, own_spheres = call(
        pack_body,
        [(sizes.contact_rows, LANES), (sizes.sphere_rows, LANES)],
        [
            block_counts[0, 0],
            velocity_free[0, 0],
            inverse_mass[0, 0],
            jacobian[0, 0],
            tiles(impulses[0, 0]),
            tiles(previous_impulses[0, 0]),
            tiles(compliance[0, 0]),
            tiles(offset[0, 0]),
            tiles(friction[0, 0]),
            tiles(body_near[0, 0]),
            tiles(body_far[0, 0]),
            layer_send[0],
            side_lists,
        ],
    )
    to_first, to_second = pair_swaps(cells, 0), pair_swaps(cells, 1)

    def swap(first, second):
        return lax.ppermute(first, "xy", to_first), lax.ppermute(second, "xy", to_second)

    def turned(array, step):
        return lax.ppermute(array, "gz", [((i + step) % slots, i) for i in range(slots)])

    sphere_arrays = [own_spheres] + [turned(own_spheres, step) for step in range(1, slots)]
    contact_arrays = []
    for slot in range(slots):
        held = own_contacts if slot == 0 else turned(own_contacts, slot)
        contact_arrays += [held, *swap(held, held)]
    inputs = [*contact_arrays, *sphere_arrays]

    def views(refs):
        sets = [[Contacts(refs[3 * s + w], sizes) for w in range(3)] for s in range(slots)]
        spheres = [Spheres(ref, sizes) for ref in refs[3 * slots : 4 * slots]]
        return sets, spheres, refs[4 * slots :]

    def chosen(*arrays):
        return [array for array in arrays if array is not None]

    state_shape = (slots, 3, 3, blocks, LANES)
    section_shape, sent_shape = (slots, 8, sizes.section), (slots, 8, sizes.sent)
    spans = (2 if slots > 1 else 1) * sizes.own_groups
    work = [
        pltpu.VMEM((sizes.own_groups * 16, sizes.contacts), BF16),
        pltpu.VMEM((LANES, sizes.contacts), BF16),
        pltpu.VMEM((spans * 16, 3 * sizes.contacts), BF16),
        pltpu.VMEM((LANES, 3 * sizes.contacts), BF16),
    ] * 2

    def put_velocities(sums, spheres, maps, flags, section_ref, first_ref, second_ref):
        velocity = [
            [spheres[s].free(g) + spheres[s].weight(g) * sums[s][g] for g in range(sizes.own_groups)]
            for s in range(slots)
        ]
        for slot in range(slots):
            table = list(velocity[slot])
            for rows in maps.upper(slot):
                upper = gather(velocity[(slot + 1) % slots], rows - 1)
                table.append(jnp.where(flags[3 + slot] != 0, upper, 0.0))
            for group, value in enumerate(table):
                section_ref[slot, :, pl.ds(group * LANES, LANES)] = value
            for which, sent_ref in ((1, first_ref), (2, second_ref)):
                for group, value in enumerate(velocity[slot]):
                    sent_ref[slot, :, pl.ds(group * LANES, LANES)] = value
                for group, rows in enumerate(maps.side(slot, which)):
                    lanes = pl.ds(sizes.own + group * LANES, LANES)
                    sent_ref[slot, :, lanes] = gather(table, rows - 1)

    def first_velocities():
        def body(flags, *refs):
            sets, spheres, refs = views(refs)
            section_ref, first_ref, second_ref, *scratch = refs
            maps = Maps(spheres, sizes, flags)
            values = [[[c.tile(GUESS + row) for row in range(3)] for c in row_sets] for row_sets in sets]
            sums = collected(sets, values, maps, sizes, scratch)
            put_velocities(sums, spheres, maps, flags, section_ref, first_ref, second_ref)

        return call(body, [section_shape, sent_shape, sent_shape], [flags, *inputs], work)

    def gradients(section, sent, got, state):
        def body(flags, section_ref, sent_first, sent_second, got_first, got_second, *refs):
            sets, spheres, refs = views(refs)
            if state is None:
                state_ref = None
            else:
                state_ref, *refs = refs
            grad_ref, parts_ref, rows_ref, *scratch = refs
            maps = Maps(spheres, sizes, flags)
            even = flags[0] == 0
            norm = soft = jnp.zeros((blocks, LANES), F32)
            lane = lax.broadcasted_iota(I32, (8, LANES), 1)
            edge = sizes.side % LANES

            def groups(ref, slot, start, count):
                return [ref[slot, :, pl.ds(start + g * LANES, LANES)] for g in range(count)]

            values = []
            for slot in range(slots):
                table = groups(section_ref, slot, 0, sizes.section_groups)
                first = groups(got_first, slot, sizes.own, sizes.window_groups)
                second = groups(got_second, slot, sizes.own, sizes.window_groups)
                first = [jnp.where(flags[1] != 0, value, 0.0) for value in first]
                second = [jnp.where(flags[2] != 0, value, 0.0) for value in second]
                low = [jnp.where(even, b, a) for a, b in zip(first, second)]
                high = [jnp.where(even, a, b) for a, b in zip(first, second)]
                if edge:
                    table += low[:-1] + [jnp.where(lane < edge, low[-1], high[0])] + high[1:]
                else:
                    table += low + high
                slot_values = []
                for which, pack in enumerate(sets[slot]):
                    far = pack.tile(FAR).astype(I32)
                    if which == 0:
                        rows_of(pack, table[: sizes.own_groups], table, far, sizes, rows_ref.at[slot, which])
                    else:
                        sent_ref = (sent_first, sent_second)[which - 1]
                        got_ref = (got_first, got_second)[which - 1]
                        own = groups(got_ref, slot, 0, sizes.own_groups)
                        listed = groups(sent_ref, slot, sizes.own, sizes.window_groups)
                        index = maps.window_index(far, which)
                        rows_of(pack, own, listed, index, sizes, rows_ref.at[slot, which])
                    alive, softness = pack.tile(ALIVE), pack.tile(SOFTNESS)
                    grad = []
                    for row in range(3):
                        guess = pack.tile(GUESS + row) if state_ref is None else state_ref[slot, which, row]
                        value = rows_ref[slot, which, row] + softness * guess
                        if row == 0:
                            value = value + pack.tile(OFFSET)
                        value = alive * value
                        grad_ref[slot, which, row] = value
                        grad.append(value)
                        if which == 0:
                            norm = norm + value * value
                            soft = soft + softness * value * value
                    slot_values.append(grad)
                values.append(slot_values)
            sums = collected(sets, values, maps, sizes, scratch)
            curve = jnp.sum(soft, axis=0, keepdims=True)
            norm = jnp.sum(norm, axis=0, keepdims=True)
            total = jnp.zeros((8, LANES), F32)
            for slot in range(slots):
                for group in range(sizes.own_groups):
                    value = sums[slot][group]
                    total = total + spheres[slot].weight(group) * value * value
            curve = curve + jnp.sum(total, axis=0, keepdims=True)
            both = jnp.concatenate([norm, curve, jnp.zeros((6, LANES), F32)], axis=0)
            for cell in range(cells):
                parts_ref[cell] = both

        return call(
            body,
            [state_shape, (cells, 8, LANES)],
            chosen(flags, section, *sent, *got, *inputs, state),
            [pltpu.VMEM(state_shape, F32), *work],
        )

    def updates(parts, grad, state, earlier, factor):
        last = factor is None

        def body(flags, part_ref, grad_ref, *refs):
            sets, spheres, refs = views(refs)
            if state is not None:
                state_ref, earlier_ref, *refs = refs
            if last:
                result_ref, velocity_ref, *scratch = refs
            else:
                result_ref, guess_ref, section_ref, first_ref, second_ref, *scratch = refs
            maps = Maps(spheres, sizes, flags)
            total = part_ref[0]
            for cell in range(1, cells):
                total = total + part_ref[cell]
            sums = jnp.sum(total, axis=1, keepdims=True)
            step = sums[0:1] / (sums[1:2] + EPSILON)
            values = []
            for slot in range(slots):
                slot_values = []
                for which, pack in enumerate(sets[slot]):
                    alive = pack.tile(ALIVE)
                    moved, before = [], []
                    for row in range(3):
                        if state is None:
                            guess, old = pack.tile(GUESS + row), pack.tile(CURRENT + row)
                        else:
                            guess, old = state_ref[slot, which, row], earlier_ref[slot, which, row]
                        before.append(old)
                        moved.append(guess - step * grad_ref[slot, which, row])
                    value = [alive * v for v in cone_project(moved, pack.tile(FRICTION))]
                    if not last:
                        guess = [alive * (v + factor * (v - b)) for v, b in zip(value, before)]
                        for row in range(3):
                            result_ref[slot, which, row] = value[row]
                            guess_ref[slot, which, row] = guess[row]
                        value = guess
                    elif slot == which == 0:
                        for row in range(3):
                            for block in range(blocks):
                                lanes = pl.ds(block * LANES, LANES)
                                result_ref[pl.ds(row, 1), lanes] = value[row][block : block + 1]
                    slot_values.append(value)
                values.append(slot_values)
            sums = collected(sets, values, maps, sizes, scratch)
            if last:
                for group in range(sizes.own_groups):
                    value = spheres[0].free(group) + spheres[0].weight(group) * sums[0][group]
                    velocity_ref[:, pl.ds(group * LANES, LANES)] = value[:6]
            else:
                put_velocities(sums, spheres, maps, flags, section_ref, first_ref, second_ref)

        if last:
            shapes = [(3, sizes.contacts), (6, sizes.own)]
        else:
            shapes = [state_shape, state_shape, section_shape, sent_shape, sent_shape]
        return call(body, shapes, chosen(flags, parts, grad, *inputs, state, earlier), work)

    state = earlier = None
    section, *sent = first_velocities()
    for iteration in range(ITERS):
        grad, parts = gradients(section, sent, swap(*sent), state)
        parts = lax.all_to_all(parts, "xy", 0, 0, tiled=True)
        if iteration + 1 < ITERS:
            earlier, state, section, *sent = updates(parts, grad, state, earlier, factors[iteration + 1])
    result, velocity = updates(parts, grad, state, earlier, None)
    return (result[None, None], velocity[None, None])


def solution(mesh):
    placed = (
        P("gz", "xy", None, None),
        P("gz", "xy", None, None),
        P("gz", "xy", None, None),
        P("gz", "xy", None, None),
        P("gz", "xy", None, None),
        P("gz", "xy", None),
        P("gz", "xy", None),
        P("gz", "xy", None),
        P("gz", "xy", None),
        P("gz", "xy", None),
        P("gz", "xy", None),
        P("gz", "xy", None),
        P("gz", "xy", None, None),
    )
    return jax.shard_map(
        on_device,
        mesh=mesh,
        in_specs=placed,
        out_specs=(P("gz", "xy", None, None), P("gz", "xy", None, None)),
        check_vma=False,
    )
```

```python
import math

import jax
import jax.numpy as jnp
from jax import lax
from jax.experimental import pallas as pl
from jax.experimental.pallas import tpu as pltpu
from jax.sharding import PartitionSpec as P

ITERS = 2
EPSILON = 1e-06
THETA_START = 0.3
LANES = 128
WIDE = 256
F32 = jnp.float32
BF16 = jnp.bfloat16
I32 = jnp.int32


def theta_after(theta_value):
    return 0.5 * (
        -theta_value * theta_value + theta_value * math.sqrt(theta_value * theta_value + 4.0)
    )


def momentum_factors(iteration_count):
    thetas = [THETA_START]
    for iteration in range(iteration_count):
        thetas.append(theta_after(thetas[-1]))
    return [
        thetas[position]
        * (1.0 - thetas[position])
        / (thetas[position] * thetas[position] + thetas[position + 1])
        for position in range(iteration_count)
    ]


def pair_swaps(count, parity):
    target = list(range(count))
    for cell in range(parity, count - 1, 2):
        target[cell], target[cell + 1] = cell + 1, cell
    return list(enumerate(target))


class Sizes:
    def __init__(self, contacts, own, layer, side, slots, cells):
        self.contacts, self.own, self.layer, self.side = contacts, own, layer, side
        self.slots, self.cells = slots, cells
        self.blocks = contacts // LANES
        self.section = own + layer
        self.window = -(-side // LANES) * LANES
        self.margin = self.window - side
        self.own_groups = own // LANES
        self.layer_groups = layer // LANES
        self.section_groups = self.section // LANES
        self.total_groups = (self.section + 2 * side) // LANES
        self.window_groups = self.window // LANES
        self.layer_at = 2 * self.own_groups
        self.side_at = self.layer_at + self.layer_groups
        self.sphere_groups = self.side_at + self.window_groups
        self.mail_groups = self.section_groups + self.sphere_groups
        self.sent = own + self.window
        assert contacts % LANES == own % LANES == layer % LANES == 2 * side % LANES == 0
        assert self.blocks % 8 == 0


NEAR, FAR, ALIVE, FRICTION, SOFTNESS, OFFSET, CURRENT, GUESS = 36, 37, 38, 39, 40, 41, 42, 45
TILES = 48


class Contacts:
    def __init__(self, ref):
        self.ref = ref

    def tile(self, which):
        return self.ref[which]

    def entry(self, row, part, body, rows=slice(None)):
        return self.ref[12 * row + 6 * part + body, rows, :]


class Spheres:
    def __init__(self, ref, sizes, start=0):
        self.ref, self.sizes, self.start = ref, sizes, start

    def misc(self, group):
        return self.ref[:, pl.ds((self.start + group) * LANES, LANES)]

    def free(self, group):
        return self.misc(group)

    def weight(self, group):
        return self.misc(self.sizes.own_groups + group)

    def layer_list(self, group):
        return self.misc(self.sizes.layer_at + group)[0:1].astype(I32)

    def side_list(self, which, group):
        return self.misc(self.sizes.side_at + group)[which : which + 1].astype(I32)


def places(index, groups):
    index = jnp.broadcast_to(index, (8, LANES))
    which = index >> 7
    return index & (LANES - 1), [which == number for number in range(groups)]


def gather(groups, place):
    lane, inside = place
    out = jnp.zeros((8, LANES), groups[0].dtype)
    for group, here in zip(groups, inside):
        group = jnp.broadcast_to(group, (8, LANES))
        out = jnp.where(here, jnp.take_along_axis(group, lane, axis=1, mode="promise_in_bounds"), out)
    return out


def look_up(lists, index):
    pieces = [
        gather(lists, places(index[at : at + 8], len(lists))) for at in range(0, index.shape[0], 8)
    ]
    return jnp.concatenate(pieces, axis=0) - 1


def lay_hot(index, hot_ref):
    lane_of = (index & (LANES - 1)).astype(F32)
    row_number = lax.broadcasted_iota(I32, (LANES, LANES), 0).astype(F32).astype(BF16)
    zeros, ones = jnp.zeros((16, LANES), BF16), jnp.ones((16, LANES), BF16)
    for block in range(index.shape[0]):
        low = jnp.broadcast_to(lane_of[block : block + 1], (16, LANES)).astype(BF16)
        for piece in range(LANES // 16):
            rows = slice(piece * 16, piece * 16 + 16)
            hot = jnp.where(row_number[rows] == low, ones, zeros)
            hot_ref[pl.ds(piece * 16, 16), pl.ds(block * LANES, LANES)] = hot


def lay_terms(terms, index, groups, parts_ref, spread_ref):
    blocks = terms[0].shape[0]
    for body, term in enumerate(terms):
        upper = term.astype(BF16).astype(F32)
        parts_ref[pl.ds(body * blocks, blocks), :] = upper
        parts_ref[pl.ds((8 + body) * blocks, blocks), :] = term - upper
    group_of = (index >> 7).astype(F32)
    zeros = jnp.zeros((16, LANES), BF16)
    for block in range(blocks):
        both = parts_ref[pl.ds(block, 16, stride=blocks), :].astype(BF16)
        which = jnp.broadcast_to(group_of[block : block + 1], (16, LANES)).astype(BF16)
        for at, number in enumerate(groups):
            part = jnp.where(which == jnp.asarray(number, BF16), both, zeros)
            spread_ref[pl.ds(at * 16, 16), pl.ds(block * LANES, LANES)] = part


def summed(spread, hot):
    out = lax.dot_general(spread, hot, (((1,), (1,)), ((), ())), preferred_element_type=F32)
    return [out[at : at + 8] + out[at + 8 : at + 16] for at in range(0, out.shape[0], 16)]


def put_columns(values, lists, groups):
    result = [jnp.zeros((8, LANES), F32)] * groups
    row_number = lax.broadcasted_iota(I32, (LANES, LANES), 0)
    for value, index in zip(values, lists):
        upper = value.astype(BF16).astype(F32)
        both = jnp.concatenate([upper, value - upper], axis=0)
        which = jnp.broadcast_to(index >> 7, (16, LANES))
        spread = jnp.concatenate([jnp.where(which == g, both, 0.0) for g in range(groups)], axis=0)
        low = jnp.broadcast_to(index & (LANES - 1), (LANES, LANES))
        hot = jnp.where(row_number == low, 1.0, 0.0).astype(BF16)
        result = [a + b for a, b in zip(result, summed(spread.astype(BF16), hot))]
    return result


class Maps:
    def __init__(self, spheres, sizes, flags):
        self.spheres, self.sizes, self.flags = spheres, sizes, flags

    def upper(self, slot):
        above = self.spheres[(slot + 1) % self.sizes.slots]
        return [above.layer_list(group) for group in range(self.sizes.layer_groups)]

    def side(self, slot, which):
        picks = []
        for group in range(self.sizes.window_groups):
            to_lower = self.spheres[slot].side_list(0, group)
            to_higher = self.spheres[slot].side_list(1, group)
            higher = (self.flags[0] == 0) == (which == 1)
            picks.append(jnp.where(higher, to_higher, to_lower))
        return picks

    def window_index(self, far, which):
        sizes = self.sizes
        higher = (self.flags[0] == 0) == (which == 1)
        return far - jnp.where(higher, sizes.section, sizes.section + sizes.side - sizes.margin)

    def section_row(self, slot, which, far):
        if which == 0:
            return jnp.where(far < self.sizes.section, far, -1)
        row = look_up(self.side(slot, which), self.window_index(far, which))
        return jnp.where(self.flags[which] != 0, row, -1)


def set_terms(slot, which, pack, value, maps, sizes, hots, scratch, groups, new_hots=False):
    far_hot, near_hot = hots
    parts_ref, spread_ref, near_parts, near_spread = scratch
    far = maps.section_row(slot, which, pack.tile(FAR).astype(I32))
    own = [group for group in groups if group < sizes.own_groups] if which == 0 else []
    todo = [(1, far, groups, far_hot, parts_ref, spread_ref)]
    if own:
        todo.append((0, pack.tile(NEAR).astype(I32), own, near_hot, near_parts, near_spread))
    result = {}
    for part, index, wanted, hot_ref, to_parts, to_spread in todo:
        terms = [
            pack.entry(0, part, body) * value[0]
            + pack.entry(1, part, body) * value[1]
            + pack.entry(2, part, body) * value[2]
            for body in range(6)
        ]
        if new_hots:
            lay_hot(index, hot_ref)
        lay_terms(terms, index, wanted, to_parts, to_spread)
        sums = summed(to_spread[pl.ds(0, 16 * len(wanted)), :], hot_ref[...])
        for group, total in zip(wanted, sums):
            result[group] = result[group] + total if group in result else total
    return [result[group] for group in groups]


def added(lists):
    return [sum(values[1:], values[0]) for values in zip(*lists)]


def joined(sections, spheres, sizes, flags, slot):
    own = sections[slot][: sizes.own_groups]
    if sizes.slots > 1:
        below = (slot + sizes.slots - 1) % sizes.slots
        upper = [jnp.where(flags[3 + below] != 0, v, 0.0) for v in sections[below][-sizes.layer_groups :]]
        lists = [spheres[slot].layer_list(group) - 1 for group in range(sizes.layer_groups)]
        own = added([own, put_columns(upper, lists, sizes.own_groups)])
    return own


def rows_of(pack, near_rows, far_rows, far_index):
    near_index = pack.tile(NEAR).astype(I32)
    near_groups, far_groups = len(near_rows(0)), len(far_rows(0))
    halves = []
    for at in range(0, near_index.shape[0], 8):
        rows = slice(at, at + 8)
        totals = [None] * 3
        for part, table, place in (
            (0, near_rows, places(near_index[rows], near_groups)),
            (1, far_rows, places(far_index[rows], far_groups)),
        ):
            for body in range(6):
                picked = gather(table(body), place)
                for row in range(3):
                    term = pack.entry(row, part, body, rows) * picked
                    totals[row] = term if totals[row] is None else totals[row] + term
        halves.append(totals)
    return [jnp.concatenate([half[row] for half in halves], axis=0) for row in range(3)]


def cone_project(impulse_value, cone_friction):
    normal, first, second = impulse_value
    slide_norm = jnp.sqrt(first * first + second * second)
    inside_cone = slide_norm <= cone_friction * normal
    polar_cone = cone_friction * slide_norm <= -normal
    outside_both = jnp.logical_not(jnp.logical_or(inside_cone, polar_cone))
    onto_normal = (cone_friction * slide_norm + normal) / (cone_friction * cone_friction + 1.0)
    tangent_scale = cone_friction * onto_normal / jnp.where(outside_both, slide_norm, 1.0)
    scale = jnp.where(inside_cone, 1.0, jnp.where(polar_cone, 0.0, tangent_scale))
    new_normal = jnp.where(inside_cone, normal, jnp.where(polar_cone, 0.0, onto_normal))
    return [new_normal, scale * first, scale * second]


def call(body, out_shape, operands, scratch=(), space=pltpu.VMEM, room=40):
    specs = [pl.BlockSpec(memory_space=pltpu.SMEM)]
    specs += [pl.BlockSpec(memory_space=space)] * (len(operands) - 1)
    return pl.pallas_call(
        body,
        out_shape=[
            jax.ShapeDtypeStruct(*shape) if isinstance(shape[0], tuple) else jax.ShapeDtypeStruct(shape, F32)
            for shape in out_shape
        ],
        in_specs=specs,
        out_specs=[pl.BlockSpec(memory_space=pltpu.VMEM)] * len(out_shape),
        scratch_shapes=list(scratch),
        compiler_params=pltpu.CompilerParams(vmem_limit_bytes=room * 1024 * 1024),
    )(*operands)


def on_device(
    velocity_free,
    inverse_mass,
    jacobian,
    impulses,
    previous_impulses,
    compliance,
    offset,
    friction,
    body_near,
    body_far,
    block_counts,
    layer_send,
    side_send,
):
    slots, cells = lax.axis_size("gz"), lax.axis_size("xy")
    layer_at, cell_at = lax.axis_index("gz"), lax.axis_index("xy")
    sizes = Sizes(
        jacobian.shape[3], velocity_free.shape[3], layer_send.shape[2], side_send.shape[3], slots, cells
    )
    blocks, window = sizes.blocks, sizes.window
    factors = momentum_factors(ITERS)

    odd = cell_at % 2
    lower, higher = cell_at > 0, cell_at < cells - 1
    flags = jnp.stack(
        [odd, jnp.where(odd == 0, higher, lower), jnp.where(odd == 0, lower, higher)]
        + [(layer_at + slot) % slots != slots - 1 for slot in range(slots)]
    ).astype(I32)

    def tiles(array):
        return array.reshape(-1, blocks, LANES)

    def pack_body(counts, *refs):
        inputs, (out_ref, sphere_ref, *held, semaphores) = refs[:12], refs[12:]
        targets = [*held[:2], out_ref.at[pl.ds(0, 36)], *held[2:]]
        copies = [
            pltpu.make_async_copy(source, target, semaphores.at[at])
            for at, (source, target) in enumerate(zip(inputs, targets))
        ]
        for copy in copies:
            copy.start()
        for copy in copies:
            copy.wait()
        (free_ref, mass_ref, imp_ref, prev_ref, soft_ref, off_ref, fric_ref, near_ref, far_ref,
         layer_ref, side_ref) = held
        lane = lax.broadcasted_iota(I32, (1, LANES), 1)
        rows = [jnp.where(lane < counts[block], 1.0, 0.0) for block in range(blocks)]
        alive = jnp.concatenate(rows, axis=0)
        out_ref[NEAR] = near_ref[0].astype(F32)
        out_ref[FAR] = far_ref[0].astype(F32)
        out_ref[ALIVE] = alive
        out_ref[FRICTION] = fric_ref[0]
        out_ref[SOFTNESS] = soft_ref[0]
        out_ref[OFFSET] = off_ref[0]
        for row in range(3):
            current = alive * imp_ref[row]
            earlier = alive * prev_ref[row]
            out_ref[CURRENT + row] = current
            out_ref[GUESS + row] = alive * (current + factors[0] * (current - earlier))

        gap = jnp.zeros((2, LANES), F32)

        def misc(group, value):
            sphere_ref[:, pl.ds(group * LANES, LANES)] = value

        for group in range(sizes.own_groups):
            lanes = pl.ds(group * LANES, LANES)
            free = [free_ref[body, pl.ds(group, 1), :] for body in range(6)]
            misc(group, jnp.concatenate(free + [gap], axis=0))
            mass = mass_ref[:, lanes]
            linear = jnp.broadcast_to(mass[0:1], (3, LANES))
            angular = jnp.broadcast_to(mass[1:2], (3, LANES))
            misc(sizes.own_groups + group, jnp.concatenate([linear, angular, gap], axis=0))
        for group in range(sizes.layer_groups):
            lanes = pl.ds(group * LANES, LANES)
            rows = jnp.broadcast_to(layer_ref[:, lanes] + 1, (8, LANES))
            misc(sizes.layer_at + group, rows.astype(F32))
        side = side_ref[...] + 1
        if sizes.margin:
            none = jnp.zeros((1, sizes.margin), I32)
            to_lower = jnp.concatenate([none, side[0:1]], axis=1)
            to_higher = jnp.concatenate([side[1:2], none], axis=1)
            side = jnp.concatenate([to_lower, to_higher], axis=0)
        for group in range(sizes.window_groups):
            rows = jnp.concatenate([side[:, group * LANES : (group + 1) * LANES]] * 4, axis=0)
            misc(sizes.side_at + group, rows.astype(F32))

    loaded = [
        velocity_free[0, 0].reshape(6, sizes.own_groups, LANES),
        inverse_mass[0, 0],
        tiles(jacobian[0, 0]),
        tiles(impulses[0, 0]),
        tiles(previous_impulses[0, 0]),
        tiles(compliance[0, 0]),
        tiles(offset[0, 0]),
        tiles(friction[0, 0]),
        tiles(body_near[0, 0]),
        tiles(body_far[0, 0]),
        layer_send[0],
        side_send[0, 0],
    ]
    own_contacts, own_spheres = call(
        pack_body,
        [(TILES, blocks, LANES), (8, sizes.sphere_groups * LANES)],
        [block_counts[0, 0], *loaded],
        [pltpu.VMEM(array.shape, array.dtype) for at, array in enumerate(loaded) if at != 2]
        + [pltpu.SemaphoreType.DMA((len(loaded),))],
        pl.ANY,
        62,
    )
    to_first, to_second = pair_swaps(cells, 0), pair_swaps(cells, 1)

    def swap(first, second):
        return lax.ppermute(first, "xy", to_first), lax.ppermute(second, "xy", to_second)

    def turned(array, step):
        return lax.ppermute(array, "gz", [((i + step) % slots, i) for i in range(slots)])

    contact_arrays = []
    for slot in range(slots):
        held = own_contacts if slot == 0 else turned(own_contacts, slot)
        contact_arrays.append([held, *swap(held, held)])

    def views(refs):
        sets = [[Contacts(refs[3 * s + w]) for w in range(3)] for s in range(slots)]
        refs = refs[3 * slots :]
        spheres = [Spheres(ref, sizes, sizes.section_groups) for ref in refs[:slots]]
        refs = refs[slots:]
        hots = [
            [(refs[4 * s + 1 + w], refs[4 * s] if w == 0 else None) for w in range(3)] for s in range(slots)
        ]
        return sets, spheres, hots, refs[4 * slots :]

    def chosen(*arrays):
        return [array for array in arrays if array is not None]

    state_shape = (slots, 3, 3, blocks, LANES)
    section_shape, sent_shape = (slots, 8, sizes.section), (slots, 8, sizes.sent)
    hot_shape = ((LANES, sizes.contacts), BF16)

    def scratch_of(own):
        split = pltpu.VMEM((16 * blocks, LANES), F32)
        spread = [pltpu.VMEM((16 * n, sizes.contacts), BF16) for n in (sizes.section_groups, sizes.own_groups)]
        return [split, spread[0]] + ([split, spread[1]] if own else [])

    work = scratch_of(True) + scratch_of(False) * 2

    def places_of(scratch, slot, which):
        base = (slot % 2) * len(work)
        if which == 0:
            return scratch[base : base + 4]
        return [*scratch[base + 2 + 2 * which : base + 4 + 2 * which], None, None]

    def clear(scratch):
        gap = jnp.zeros((2 * blocks, LANES), F32)
        for ref in scratch[::2]:
            ref[pl.ds(6 * blocks, 2 * blocks), :] = gap
            ref[pl.ds(14 * blocks, 2 * blocks), :] = gap

    def slot_sections(sets, values, maps, hots, scratch, wanted):
        clear(scratch)
        return [
            added(
                [
                    set_terms(
                        s, w, sets[s][w], values[s][w], maps, sizes, hots[s][w], places_of(scratch, s, w), groups
                    )
                    for w in range(3)
                ]
            )
            if groups
            else None
            for s, groups in enumerate(wanted)
        ]

    every = list(range(sizes.section_groups))

    def put_velocities(sums, spheres, maps, flags, section_ref, first_ref, second_ref):
        velocity = [
            [spheres[s].free(g) + spheres[s].weight(g) * sums[s][g] for g in range(sizes.own_groups)]
            for s in range(slots)
        ]
        for slot in range(slots):
            table = list(velocity[slot])
            for rows in maps.upper(slot):
                upper = gather(velocity[(slot + 1) % slots], places(rows - 1, sizes.own_groups))
                table.append(jnp.where(flags[3 + slot] != 0, upper, 0.0))
            for group, value in enumerate(table):
                section_ref[slot, :, pl.ds(group * LANES, LANES)] = value
            for which, sent_ref in ((1, first_ref), (2, second_ref)):
                for group, value in enumerate(velocity[slot]):
                    sent_ref[slot, :, pl.ds(group * LANES, LANES)] = value
                for group, rows in enumerate(maps.side(slot, which)):
                    lanes = pl.ds(sizes.own + group * LANES, LANES)
                    sent_ref[slot, :, lanes] = gather(table, places(rows - 1, sizes.section_groups))

    def first_terms():
        def guess_of(pack):
            return [pack.tile(GUESS + row) for row in range(3)]

        def early(flags, own_ref, first_ref, sphere_ref, out_ref, near_hot, far_hot, first_hot, *scratch):
            clear(scratch)
            maps = Maps([Spheres(sphere_ref, sizes)], sizes, flags)
            sets = [Contacts(own_ref), Contacts(first_ref)]
            hots = [(far_hot, near_hot), (first_hot, None)]
            sums = added(
                [
                    set_terms(
                        0, w, sets[w], guess_of(sets[w]), maps, sizes, hots[w], places_of(scratch, 0, w),
                        every, True,
                    )
                    for w in range(2)
                ]
            )
            for group, value in enumerate(sums):
                out_ref[:, pl.ds(group * LANES, LANES)] = value

        def late(flags, part_ref, second_ref, sphere_ref, out_ref, hot_ref, *scratch):
            clear(scratch)
            maps = Maps([Spheres(sphere_ref, sizes)], sizes, flags)
            pack = Contacts(second_ref)
            sums = set_terms(
                0, 2, pack, guess_of(pack), maps, sizes, (hot_ref, None), [*scratch, None, None], every, True
            )
            for group, value in enumerate(sums):
                lanes = pl.ds(group * LANES, LANES)
                out_ref[:, lanes] = part_ref[:, lanes] + value
            out_ref[:, pl.ds(sizes.section, sizes.sphere_groups * LANES)] = sphere_ref[...]

        own, first, second = contact_arrays[0]
        part, near_hot, far_hot, first_hot = call(
            early, [(8, sizes.section), hot_shape, hot_shape, hot_shape], [flags, own, first, own_spheres], work[:6]
        )
        mail, second_hot = call(
            late,
            [(8, sizes.mail_groups * LANES), hot_shape],
            [flags, part, second, own_spheres],
            work[4:6],
        )
        return mail, [near_hot, far_hot, first_hot, second_hot]

    def one_hots(slot, mail):
        def body(flags, own_ref, first_ref, second_ref, mail_ref, near_hot, *hot_refs):
            spheres = {slot: Spheres(mail_ref, sizes, sizes.section_groups)}
            maps = Maps(spheres, sizes, flags)
            packs = [Contacts(ref) for ref in (own_ref, first_ref, second_ref)]
            lay_hot(packs[0].tile(NEAR).astype(I32), near_hot)
            for which, pack in enumerate(packs):
                lay_hot(maps.section_row(slot, which, pack.tile(FAR).astype(I32)), hot_refs[which])

        return call(body, [hot_shape] * 4, [flags, *contact_arrays[slot], mail])

    mail, hots = first_terms()
    mails = [mail] + [turned(mail, step) for step in range(1, slots)]
    for slot in range(1, slots):
        hots = [*hots, *one_hots(slot, mails[slot])]
    inputs = [*sum(contact_arrays, []), *mails, *hots]

    def first_velocities():
        def body(flags, *refs):
            mail_refs, refs = refs[:slots], refs[slots:]
            spheres = [Spheres(ref, sizes, sizes.section_groups) for ref in mail_refs]
            maps = Maps(spheres, sizes, flags)
            sections = [[ref[:, pl.ds(group * LANES, LANES)] for group in every] for ref in mail_refs]
            sums = [joined(sections, spheres, sizes, flags, slot) for slot in range(slots)]
            put_velocities(sums, spheres, maps, flags, *refs)

        return call(body, [section_shape, sent_shape, sent_shape], [flags, *mails])

    def gradients(section, sent, got, state):
        def body(flags, section_ref, sent_first, sent_second, got_first, got_second, *refs):
            sets, spheres, hots, refs = views(refs)
            if state is None:
                state_ref = None
            else:
                state_ref, *refs = refs
            grad_ref, parts_ref, table_ref, *scratch = refs
            maps = Maps(spheres, sizes, flags)
            even = flags[0] == 0
            norm = soft = jnp.zeros((blocks, LANES), F32)
            lane = lax.broadcasted_iota(I32, (8, LANES), 1)
            edge = sizes.side % LANES

            def rows_from(ref, slot, start, count):
                def rows(body):
                    return [ref[slot, pl.ds(body, 1), pl.ds(start + g * LANES, LANES)] for g in range(count)]

                return rows

            values = []
            for slot in range(slots):
                low, high = [], []
                for group in range(sizes.window_groups):
                    lanes = pl.ds(sizes.own + group * LANES, LANES)
                    first = jnp.where(flags[1] != 0, got_first[slot, :, lanes], 0.0)
                    second = jnp.where(flags[2] != 0, got_second[slot, :, lanes], 0.0)
                    low.append(jnp.where(even, second, first))
                    high.append(jnp.where(even, first, second))
                if edge:
                    extended = low[:-1] + [jnp.where(lane < edge, low[-1], high[0])] + high[1:]
                else:
                    extended = low + high
                table_ref[slot, :, pl.ds(0, sizes.section)] = section_ref[slot]
                for group, value in enumerate(extended):
                    table_ref[slot, :, pl.ds(sizes.section + group * LANES, LANES)] = value
                slot_values = []
                for which, pack in enumerate(sets[slot]):
                    far = pack.tile(FAR).astype(I32)
                    if which == 0:
                        near_rows = rows_from(table_ref, slot, 0, sizes.own_groups)
                        far_rows = rows_from(table_ref, slot, 0, sizes.total_groups)
                    else:
                        got_ref = (got_first, got_second)[which - 1]
                        sent_ref = (sent_first, sent_second)[which - 1]
                        near_rows = rows_from(got_ref, slot, 0, sizes.own_groups)
                        far_rows = rows_from(sent_ref, slot, sizes.own, sizes.window_groups)
                        far = maps.window_index(far, which)
                    contact_rows = rows_of(pack, near_rows, far_rows, far)
                    alive, softness = pack.tile(ALIVE), pack.tile(SOFTNESS)
                    grad = []
                    for row in range(3):
                        guess = pack.tile(GUESS + row) if state_ref is None else state_ref[slot, which, row]
                        value = contact_rows[row] + softness * guess
                        if row == 0:
                            value = value + pack.tile(OFFSET)
                        value = alive * value
                        grad_ref[slot, which, row] = value
                        grad.append(value)
                        if which == 0:
                            norm = norm + value * value
                            soft = soft + softness * value * value
                    slot_values.append(grad)
                values.append(slot_values)
            sections = slot_sections(sets, values, maps, hots, scratch, [every] * slots)
            sums = [joined(sections, spheres, sizes, flags, slot) for slot in range(slots)]
            curve = jnp.sum(soft, axis=0, keepdims=True)
            norm = jnp.sum(norm, axis=0, keepdims=True)
            total = jnp.zeros((8, LANES), F32)
            for slot in range(slots):
                for group in range(sizes.own_groups):
                    value = sums[slot][group]
                    total = total + spheres[slot].weight(group) * value * value
            curve = curve + jnp.sum(total, axis=0, keepdims=True)
            half = LANES // 2
            norm = norm + pltpu.roll(norm, half, 1)
            curve = curve + pltpu.roll(curve, half, 1)
            both = jnp.where(lax.broadcasted_iota(I32, (1, LANES), 1) < half, norm, curve)
            for cell in range(cells):
                parts_ref[cell] = both

        return call(
            body,
            [state_shape, (cells, 1, LANES)],
            chosen(flags, section, *sent, *got, *inputs, state),
            [pltpu.VMEM((slots, 8, sizes.total_groups * LANES), F32), *work, *work],
        )

    def updates(parts, grad, state, earlier, factor):
        last = factor is None

        def body(flags, part_ref, grad_ref, *refs):
            sets, spheres, hots, refs = views(refs)
            if state is not None:
                state_ref, earlier_ref, *refs = refs
            if last:
                result_ref, velocity_ref, *scratch = refs
            else:
                result_ref, guess_ref, section_ref, first_ref, second_ref, *scratch = refs
            maps = Maps(spheres, sizes, flags)
            total = part_ref[0]
            for cell in range(1, cells):
                total = total + part_ref[cell]
            lane = lax.broadcasted_iota(I32, (1, LANES), 1)
            norm = jnp.sum(jnp.where(lane < LANES // 2, total, 0.0), axis=1, keepdims=True)
            curve = jnp.sum(jnp.where(lane < LANES // 2, 0.0, total), axis=1, keepdims=True)
            step = norm / (curve + EPSILON)
            values = []
            for slot in range(slots):
                slot_values = []
                for which, pack in enumerate(sets[slot]):
                    alive = pack.tile(ALIVE)
                    moved, before = [], []
                    for row in range(3):
                        if state is None:
                            guess, old = pack.tile(GUESS + row), pack.tile(CURRENT + row)
                        else:
                            guess, old = state_ref[slot, which, row], earlier_ref[slot, which, row]
                        before.append(old)
                        moved.append(guess - step * grad_ref[slot, which, row])
                    value = [alive * v for v in cone_project(moved, pack.tile(FRICTION))]
                    if not last:
                        guess = [alive * (v + factor * (v - b)) for v, b in zip(value, before)]
                        for row in range(3):
                            result_ref[slot, which, row] = value[row]
                            guess_ref[slot, which, row] = guess[row]
                        value = guess
                    elif slot == which == 0:
                        for row in range(3):
                            result_ref[row] = value[row]
                    slot_values.append(value)
                values.append(slot_values)
            wanted = [every] * slots
            if last:
                wanted = [[] for _ in range(slots)]
                wanted[-1] = every[sizes.own_groups :]
                wanted[0] = every[: sizes.own_groups]
            sections = slot_sections(sets, values, maps, hots, scratch, wanted)
            if last:
                total = joined(sections, spheres, sizes, flags, 0)
                for group in range(sizes.own_groups):
                    value = spheres[0].free(group) + spheres[0].weight(group) * total[group]
                    for body_row in range(6):
                        velocity_ref[body_row, pl.ds(group, 1), :] = value[body_row : body_row + 1]
            else:
                sums = [joined(sections, spheres, sizes, flags, slot) for slot in range(slots)]
                put_velocities(sums, spheres, maps, flags, section_ref, first_ref, second_ref)

        if last:
            shapes = [(3, blocks, LANES), (6, sizes.own_groups, LANES)]
        else:
            shapes = [state_shape, state_shape, section_shape, sent_shape, sent_shape]
        return call(body, shapes, chosen(flags, parts, grad, *inputs, state, earlier), [*work, *work])

    state = earlier = None
    section, *sent = first_velocities()
    for iteration in range(ITERS):
        grad, parts = gradients(section, sent, swap(*sent), state)
        parts = lax.all_to_all(parts, "xy", 0, 0, tiled=True)
        if iteration + 1 < ITERS:
            earlier, state, section, *sent = updates(parts, grad, state, earlier, factors[iteration + 1])
    result, velocity = updates(parts, grad, state, earlier, None)
    return (
        result.reshape(1, 1, 3, sizes.contacts),
        velocity.reshape(1, 1, 6, sizes.own),
    )


def solution(mesh):
    placed = (
        P("gz", "xy", None, None),
        P("gz", "xy", None, None),
        P("gz", "xy", None, None),
        P("gz", "xy", None, None),
        P("gz", "xy", None, None),
        P("gz", "xy", None),
        P("gz", "xy", None),
        P("gz", "xy", None),
        P("gz", "xy", None),
        P("gz", "xy", None),
        P("gz", "xy", None),
        P("gz", "xy", None),
        P("gz", "xy", None, None),
    )
    return jax.shard_map(
        on_device,
        mesh=mesh,
        in_specs=placed,
        out_specs=(P("gz", "xy", None, None), P("gz", "xy", None, None)),
        check_vma=False,
    )
```

```python
import math

import jax
import jax.numpy as jnp
from jax import lax
from jax.experimental import pallas as pl
from jax.experimental.pallas import tpu as pltpu
from jax.sharding import PartitionSpec as P

ITERS = 2
EPSILON = 1e-06
THETA_START = 0.3
LANES = 128
WIDE = 256
F32 = jnp.float32
BF16 = jnp.bfloat16
I32 = jnp.int32


def theta_after(theta_value):
    return 0.5 * (
        -theta_value * theta_value + theta_value * math.sqrt(theta_value * theta_value + 4.0)
    )


def momentum_factors(iteration_count):
    thetas = [THETA_START]
    for iteration in range(iteration_count):
        thetas.append(theta_after(thetas[-1]))
    return [
        thetas[position]
        * (1.0 - thetas[position])
        / (thetas[position] * thetas[position] + thetas[position + 1])
        for position in range(iteration_count)
    ]


def pair_swaps(count, parity):
    target = list(range(count))
    for cell in range(parity, count - 1, 2):
        target[cell], target[cell + 1] = cell + 1, cell
    return list(enumerate(target))


class Sizes:
    def __init__(self, contacts, own, layer, side, slots, cells):
        self.contacts, self.own, self.layer, self.side = contacts, own, layer, side
        self.slots, self.cells = slots, cells
        self.blocks = contacts // LANES
        self.section = own + layer
        self.window = -(-side // LANES) * LANES
        self.margin = self.window - side
        self.own_groups = own // LANES
        self.layer_groups = layer // LANES
        self.section_groups = self.section // LANES
        self.total_groups = (self.section + 2 * side) // LANES
        self.window_groups = self.window // LANES
        self.layer_at = 2 * self.own_groups
        self.side_at = self.layer_at + self.layer_groups
        self.sphere_groups = self.side_at + self.window_groups
        self.mail_groups = self.section_groups + self.sphere_groups
        self.sent = own + self.window
        assert contacts % LANES == own % LANES == layer % LANES == 2 * side % LANES == 0
        assert self.blocks % 8 == 0


NEAR, FAR, ALIVE, FRICTION, SOFTNESS, OFFSET, CURRENT, GUESS = 36, 37, 38, 39, 40, 41, 42, 45
TILES = 48


class Contacts:
    def __init__(self, ref):
        self.ref = ref

    def tile(self, which):
        return self.ref[which]

    def entry(self, row, part, body, rows=slice(None)):
        return self.ref[12 * row + 6 * part + body, rows, :]


class Spheres:
    def __init__(self, ref, sizes, start=0):
        self.ref, self.sizes, self.start = ref, sizes, start

    def misc(self, group):
        return self.ref[:, pl.ds((self.start + group) * LANES, LANES)]

    def free(self, group):
        return self.misc(group)

    def weight(self, group):
        return self.misc(self.sizes.own_groups + group)

    def layer_list(self, group):
        return self.misc(self.sizes.layer_at + group)[0:1].astype(I32)

    def side_list(self, which, group):
        return self.misc(self.sizes.side_at + group)[which : which + 1].astype(I32)


def places(index, groups):
    index = jnp.broadcast_to(index, (8, LANES))
    which = index >> 7
    return index & (LANES - 1), [which == number for number in range(groups)]


def gather(groups, place):
    lane, inside = place
    out = jnp.zeros((8, LANES), groups[0].dtype)
    for group, here in zip(groups, inside):
        group = jnp.broadcast_to(group, (8, LANES))
        out = jnp.where(here, jnp.take_along_axis(group, lane, axis=1, mode="promise_in_bounds"), out)
    return out


def look_up(lists, index):
    pieces = [
        gather(lists, places(index[at : at + 8], len(lists))) for at in range(0, index.shape[0], 8)
    ]
    return jnp.concatenate(pieces, axis=0) - 1


def lay_hot(index, hot_ref):
    lane_of = (index & (LANES - 1)).astype(F32)
    row_number = lax.broadcasted_iota(I32, (LANES, LANES), 0).astype(F32).astype(BF16)
    zeros, ones = jnp.zeros((16, LANES), BF16), jnp.ones((16, LANES), BF16)
    for block in range(index.shape[0]):
        low = jnp.broadcast_to(lane_of[block : block + 1], (16, LANES)).astype(BF16)
        for piece in range(LANES // 16):
            rows = slice(piece * 16, piece * 16 + 16)
            hot = jnp.where(row_number[rows] == low, ones, zeros)
            hot_ref[pl.ds(piece * 16, 16), pl.ds(block * LANES, LANES)] = hot


def lay_terms(terms, index, groups, parts_ref, spread_ref):
    blocks = terms[0].shape[0]
    for body, term in enumerate(terms):
        upper = term.astype(BF16).astype(F32)
        parts_ref[pl.ds(body * blocks, blocks), :] = upper
        parts_ref[pl.ds((8 + body) * blocks, blocks), :] = term - upper
    group_of = (index >> 7).astype(F32)
    zeros = jnp.zeros((16, LANES), BF16)
    for block in range(blocks):
        both = parts_ref[pl.ds(block, 16, stride=blocks), :].astype(BF16)
        which = jnp.broadcast_to(group_of[block : block + 1], (16, LANES)).astype(BF16)
        for at, number in enumerate(groups):
            part = jnp.where(which == jnp.asarray(number, BF16), both, zeros)
            spread_ref[pl.ds(at * 16, 16), pl.ds(block * LANES, LANES)] = part


def summed(spread, hot):
    out = lax.dot_general(spread, hot, (((1,), (1,)), ((), ())), preferred_element_type=F32)
    return [out[at : at + 8] + out[at + 8 : at + 16] for at in range(0, out.shape[0], 16)]


def put_columns(values, lists, groups):
    result = [jnp.zeros((8, LANES), F32)] * groups
    row_number = lax.broadcasted_iota(I32, (LANES, LANES), 0)
    for value, index in zip(values, lists):
        upper = value.astype(BF16).astype(F32)
        both = jnp.concatenate([upper, value - upper], axis=0)
        which = jnp.broadcast_to(index >> 7, (16, LANES))
        spread = jnp.concatenate([jnp.where(which == g, both, 0.0) for g in range(groups)], axis=0)
        low = jnp.broadcast_to(index & (LANES - 1), (LANES, LANES))
        hot = jnp.where(row_number == low, 1.0, 0.0).astype(BF16)
        result = [a + b for a, b in zip(result, summed(spread.astype(BF16), hot))]
    return result


class Maps:
    def __init__(self, spheres, sizes, flags):
        self.spheres, self.sizes, self.flags = spheres, sizes, flags

    def upper(self, slot):
        above = self.spheres[(slot + 1) % self.sizes.slots]
        return [above.layer_list(group) for group in range(self.sizes.layer_groups)]

    def side(self, slot, which):
        picks = []
        for group in range(self.sizes.window_groups):
            to_lower = self.spheres[slot].side_list(0, group)
            to_higher = self.spheres[slot].side_list(1, group)
            higher = (self.flags[0] == 0) == (which == 1)
            picks.append(jnp.where(higher, to_higher, to_lower))
        return picks

    def window_index(self, far, which):
        sizes = self.sizes
        higher = (self.flags[0] == 0) == (which == 1)
        return far - jnp.where(higher, sizes.section, sizes.section + sizes.side - sizes.margin)

    def section_row(self, slot, which, far):
        if which == 0:
            return jnp.where(far < self.sizes.section, far, -1)
        row = look_up(self.side(slot, which), self.window_index(far, which))
        return jnp.where(self.flags[which] != 0, row, -1)


def set_terms(slot, which, pack, value, maps, sizes, hots, scratch, groups, new_hots=False):
    far_hot, near_hot = hots
    parts_ref, spread_ref, near_parts, near_spread = scratch
    far = maps.section_row(slot, which, pack.tile(FAR).astype(I32))
    own = [group for group in groups if group < sizes.own_groups] if which == 0 else []
    todo = [(1, far, groups, far_hot, parts_ref, spread_ref)]
    if own:
        todo.append((0, pack.tile(NEAR).astype(I32), own, near_hot, near_parts, near_spread))
    result = {}
    for part, index, wanted, hot_ref, to_parts, to_spread in todo:
        terms = [
            pack.entry(0, part, body) * value[0]
            + pack.entry(1, part, body) * value[1]
            + pack.entry(2, part, body) * value[2]
            for body in range(6)
        ]
        if new_hots:
            lay_hot(index, hot_ref)
        lay_terms(terms, index, wanted, to_parts, to_spread)
        sums = summed(to_spread[pl.ds(0, 16 * len(wanted)), :], hot_ref[...])
        for group, total in zip(wanted, sums):
            result[group] = result[group] + total if group in result else total
    return [result[group] for group in groups]


def added(lists):
    return [sum(values[1:], values[0]) for values in zip(*lists)]


def joined(sections, spheres, sizes, flags, slot):
    own = sections[slot][: sizes.own_groups]
    if sizes.slots > 1:
        below = (slot + sizes.slots - 1) % sizes.slots
        upper = [jnp.where(flags[3 + below] != 0, v, 0.0) for v in sections[below][-sizes.layer_groups :]]
        lists = [spheres[slot].layer_list(group) - 1 for group in range(sizes.layer_groups)]
        own = added([own, put_columns(upper, lists, sizes.own_groups)])
    return own


def rows_of(pack, near_rows, far_rows, far_index):
    near_index = pack.tile(NEAR).astype(I32)
    near_groups, far_groups = len(near_rows(0)), len(far_rows(0))
    halves = []
    for at in range(0, near_index.shape[0], 8):
        rows = slice(at, at + 8)
        totals = [None] * 3
        for part, table, place in (
            (0, near_rows, places(near_index[rows], near_groups)),
            (1, far_rows, places(far_index[rows], far_groups)),
        ):
            for body in range(6):
                picked = gather(table(body), place)
                for row in range(3):
                    term = pack.entry(row, part, body, rows) * picked
                    totals[row] = term if totals[row] is None else totals[row] + term
        halves.append(totals)
    return [jnp.concatenate([half[row] for half in halves], axis=0) for row in range(3)]


def cone_project(impulse_value, cone_friction):
    normal, first, second = impulse_value
    slide_norm = jnp.sqrt(first * first + second * second)
    inside_cone = slide_norm <= cone_friction * normal
    polar_cone = cone_friction * slide_norm <= -normal
    outside_both = jnp.logical_not(jnp.logical_or(inside_cone, polar_cone))
    onto_normal = (cone_friction * slide_norm + normal) / (cone_friction * cone_friction + 1.0)
    tangent_scale = cone_friction * onto_normal / jnp.where(outside_both, slide_norm, 1.0)
    scale = jnp.where(inside_cone, 1.0, jnp.where(polar_cone, 0.0, tangent_scale))
    new_normal = jnp.where(inside_cone, normal, jnp.where(polar_cone, 0.0, onto_normal))
    return [new_normal, scale * first, scale * second]


def call(body, out_shape, operands, scratch=(), space=pltpu.VMEM, room=40, out_space=pltpu.VMEM):
    return pl.pallas_call(
        body,
        out_shape=[
            jax.ShapeDtypeStruct(*shape) if isinstance(shape[0], tuple) else jax.ShapeDtypeStruct(shape, F32)
            for shape in out_shape
        ],
        in_specs=[pl.BlockSpec(memory_space=space)] * len(operands),
        out_specs=[pl.BlockSpec(memory_space=out_space)] * len(out_shape),
        scratch_shapes=list(scratch),
        compiler_params=pltpu.CompilerParams(vmem_limit_bytes=room * 1024 * 1024),
    )(*operands)


def on_device(
    velocity_free,
    inverse_mass,
    jacobian,
    impulses,
    previous_impulses,
    compliance,
    offset,
    friction,
    body_near,
    body_far,
    block_counts,
    layer_send,
    side_send,
):
    slots, cells = lax.axis_size("gz"), lax.axis_size("xy")
    sizes = Sizes(
        jacobian.shape[3], velocity_free.shape[3], layer_send.shape[2], side_send.shape[3], slots, cells
    )
    blocks, window = sizes.blocks, sizes.window
    factors = momentum_factors(ITERS)

    def flags_here():
        layer_at, cell_at = lax.axis_index("gz"), lax.axis_index("xy")
        odd = cell_at % 2
        lower, higher = cell_at > 0, cell_at < cells - 1
        places = [odd, jnp.where(odd == 0, higher, lower), jnp.where(odd == 0, lower, higher)]
        places += [(layer_at + slot) % slots != slots - 1 for slot in range(slots)]
        return [place.astype(I32) for place in places]

    def tiles(array):
        return array.reshape(-1, blocks, LANES)

    def pack_body(*refs):
        inputs, (contact_out, sphere_out, *held, out_ref, sphere_ref, semaphores) = refs[:13], refs[13:]
        targets = [*held[:2], out_ref.at[pl.ds(0, NEAR)], *held[2:]]
        copies = [
            pltpu.make_async_copy(source, target, semaphores.at[at])
            for at, (source, target) in enumerate(zip(inputs, targets))
        ]
        for copy in copies:
            copy.start()
        jacobian_out = pltpu.make_async_copy(
            out_ref.at[pl.ds(0, NEAR)], contact_out.at[pl.ds(0, NEAR)], semaphores.at[15]
        )
        copies[2].wait()
        jacobian_out.start()
        for at, copy in enumerate(copies):
            if at != 2:
                copy.wait()
        (free_ref, mass_ref, imp_ref, prev_ref, soft_ref, off_ref, fric_ref, near_ref, far_ref,
         layer_ref, side_ref, counts) = held
        lane = lax.broadcasted_iota(I32, (1, LANES), 1)
        rows = [jnp.where(lane < counts[block], 1.0, 0.0) for block in range(blocks)]
        alive = jnp.concatenate(rows, axis=0)
        out_ref[NEAR] = near_ref[0].astype(F32)
        out_ref[FAR] = far_ref[0].astype(F32)
        out_ref[ALIVE] = alive
        out_ref[FRICTION] = fric_ref[0]
        out_ref[SOFTNESS] = soft_ref[0]
        out_ref[OFFSET] = off_ref[0]
        for row in range(3):
            current = alive * imp_ref[row]
            earlier = alive * prev_ref[row]
            out_ref[CURRENT + row] = current
            out_ref[GUESS + row] = alive * (current + factors[0] * (current - earlier))

        gap = jnp.zeros((2, LANES), F32)

        def misc(group, value):
            sphere_ref[:, pl.ds(group * LANES, LANES)] = value

        for group in range(sizes.own_groups):
            lanes = pl.ds(group * LANES, LANES)
            free = [free_ref[body, pl.ds(group, 1), :] for body in range(6)]
            misc(group, jnp.concatenate(free + [gap], axis=0))
            mass = mass_ref[:, lanes]
            linear = jnp.broadcast_to(mass[0:1], (3, LANES))
            angular = jnp.broadcast_to(mass[1:2], (3, LANES))
            misc(sizes.own_groups + group, jnp.concatenate([linear, angular, gap], axis=0))
        for group in range(sizes.layer_groups):
            lanes = pl.ds(group * LANES, LANES)
            rows = jnp.broadcast_to(layer_ref[:, lanes] + 1, (8, LANES))
            misc(sizes.layer_at + group, rows.astype(F32))
        side = side_ref[...] + 1
        if sizes.margin:
            none = jnp.zeros((1, sizes.margin), I32)
            to_lower = jnp.concatenate([none, side[0:1]], axis=1)
            to_higher = jnp.concatenate([side[1:2], none], axis=1)
            side = jnp.concatenate([to_lower, to_higher], axis=0)
        for group in range(sizes.window_groups):
            rows = jnp.concatenate([side[:, group * LANES : (group + 1) * LANES]] * 4, axis=0)
            misc(sizes.side_at + group, rows.astype(F32))
        last = [
            pltpu.make_async_copy(
                out_ref.at[pl.ds(NEAR, TILES - NEAR)],
                contact_out.at[pl.ds(NEAR, TILES - NEAR)],
                semaphores.at[13],
            ),
            pltpu.make_async_copy(sphere_ref, sphere_out, semaphores.at[14]),
        ]
        for copy in last:
            copy.start()
        for copy in (jacobian_out, *last):
            copy.wait()

    loaded = [
        velocity_free[0, 0].reshape(6, sizes.own_groups, LANES),
        inverse_mass[0, 0],
        tiles(jacobian[0, 0]),
        tiles(impulses[0, 0]),
        tiles(previous_impulses[0, 0]),
        tiles(compliance[0, 0]),
        tiles(offset[0, 0]),
        tiles(friction[0, 0]),
        tiles(body_near[0, 0]),
        tiles(body_far[0, 0]),
        layer_send[0],
        side_send[0, 0],
        block_counts[0, 0],
    ]
    own_contacts, own_spheres = call(
        pack_body,
        [(TILES, blocks, LANES), (8, sizes.sphere_groups * LANES)],
        loaded,
        [pltpu.VMEM(array.shape, array.dtype) for at, array in enumerate(loaded[:-1]) if at != 2]
        + [
            pltpu.SMEM(block_counts.shape[2:], I32),
            pltpu.VMEM((TILES, blocks, LANES), F32),
            pltpu.VMEM((8, sizes.sphere_groups * LANES), F32),
            pltpu.SemaphoreType.DMA((len(loaded) + 3,)),
        ],
        pl.ANY,
        62,
        pl.ANY,
    )
    to_first, to_second = pair_swaps(cells, 0), pair_swaps(cells, 1)

    def swap(first, second):
        return lax.ppermute(first, "xy", to_first), lax.ppermute(second, "xy", to_second)

    def turned(array, step):
        return lax.ppermute(array, "gz", [((i + step) % slots, i) for i in range(slots)])

    contact_arrays = [[own_contacts, *swap(own_contacts, own_contacts)]]
    above_contacts = [turned(own_contacts, slot) for slot in range(1, slots)]

    def views(refs):
        sets = [[Contacts(refs[3 * s + w]) for w in range(3)] for s in range(slots)]
        refs = refs[3 * slots :]
        spheres = [Spheres(ref, sizes, sizes.section_groups) for ref in refs[:slots]]
        refs = refs[slots:]
        hots = [
            [(refs[4 * s + 1 + w], refs[4 * s] if w == 0 else None) for w in range(3)] for s in range(slots)
        ]
        return sets, spheres, hots, refs[4 * slots :]

    def chosen(*arrays):
        return [array for array in arrays if array is not None]

    state_shape = (slots, 3, 3, blocks, LANES)
    section_shape, sent_shape = (slots, 8, sizes.section), (slots, 8, sizes.sent)
    hot_shape = ((LANES, sizes.contacts), BF16)

    def scratch_of(own):
        split = pltpu.VMEM((16 * blocks, LANES), F32)
        spread = [pltpu.VMEM((16 * n, sizes.contacts), BF16) for n in (sizes.section_groups, sizes.own_groups)]
        return [split, spread[0]] + ([split, spread[1]] if own else [])

    work = scratch_of(True) + scratch_of(False) * 2

    def places_of(scratch, slot, which):
        base = (slot % 2) * len(work)
        if which == 0:
            return scratch[base : base + 4]
        return [*scratch[base + 2 + 2 * which : base + 4 + 2 * which], None, None]

    def clear(scratch):
        gap = jnp.zeros((2 * blocks, LANES), F32)
        for ref in scratch[::2]:
            ref[pl.ds(6 * blocks, 2 * blocks), :] = gap
            ref[pl.ds(14 * blocks, 2 * blocks), :] = gap

    def slot_sections(sets, values, maps, hots, scratch, wanted):
        clear(scratch)
        return [
            added(
                [
                    set_terms(
                        s, w, sets[s][w], values[s][w], maps, sizes, hots[s][w], places_of(scratch, s, w), groups
                    )
                    for w in range(3)
                ]
            )
            if groups
            else None
            for s, groups in enumerate(wanted)
        ]

    every = list(range(sizes.section_groups))

    def put_velocities(sums, spheres, maps, flags, section_ref, first_ref, second_ref):
        velocity = [
            [spheres[s].free(g) + spheres[s].weight(g) * sums[s][g] for g in range(sizes.own_groups)]
            for s in range(slots)
        ]
        for slot in range(slots):
            table = list(velocity[slot])
            for rows in maps.upper(slot):
                upper = gather(velocity[(slot + 1) % slots], places(rows - 1, sizes.own_groups))
                table.append(jnp.where(flags[3 + slot] != 0, upper, 0.0))
            for group, value in enumerate(table):
                section_ref[slot, :, pl.ds(group * LANES, LANES)] = value
            for which, sent_ref in ((1, first_ref), (2, second_ref)):
                for group, value in enumerate(velocity[slot]):
                    sent_ref[slot, :, pl.ds(group * LANES, LANES)] = value
                for group, rows in enumerate(maps.side(slot, which)):
                    lanes = pl.ds(sizes.own + group * LANES, LANES)
                    sent_ref[slot, :, lanes] = gather(table, places(rows - 1, sizes.section_groups))

    def first_terms():
        def guess_of(pack):
            return [pack.tile(GUESS + row) for row in range(3)]

        def early(own_ref, first_ref, sphere_ref, out_ref, near_hot, far_hot, first_hot, *scratch):
            flags = flags_here()
            clear(scratch)
            maps = Maps([Spheres(sphere_ref, sizes)], sizes, flags)
            sets = [Contacts(own_ref), Contacts(first_ref)]
            hots = [(far_hot, near_hot), (first_hot, None)]
            sums = added(
                [
                    set_terms(
                        0, w, sets[w], guess_of(sets[w]), maps, sizes, hots[w], places_of(scratch, 0, w),
                        every, True,
                    )
                    for w in range(2)
                ]
            )
            for group, value in enumerate(sums):
                out_ref[:, pl.ds(group * LANES, LANES)] = value

        def late(part_ref, second_ref, sphere_ref, out_ref, hot_ref, *scratch):
            flags = flags_here()
            clear(scratch)
            maps = Maps([Spheres(sphere_ref, sizes)], sizes, flags)
            pack = Contacts(second_ref)
            sums = set_terms(
                0, 2, pack, guess_of(pack), maps, sizes, (hot_ref, None), [*scratch, None, None], every, True
            )
            for group, value in enumerate(sums):
                lanes = pl.ds(group * LANES, LANES)
                out_ref[:, lanes] = part_ref[:, lanes] + value
            out_ref[:, pl.ds(sizes.section, sizes.sphere_groups * LANES)] = sphere_ref[...]

        own, first, second = contact_arrays[0]
        part, near_hot, far_hot, first_hot = call(
            early, [(8, sizes.section), hot_shape, hot_shape, hot_shape], [own, first, own_spheres], work[:6]
        )
        part, *others = lax.optimization_barrier((part, *above_contacts))
        seconds = [lax.ppermute(held, "xy", to_second) for held in others]
        mail, second_hot = call(
            late,
            [(8, sizes.mail_groups * LANES), hot_shape],
            [part, second, own_spheres],
            work[4:6],
        )
        mail, *others = lax.optimization_barrier((mail, *others))
        for held, got in zip(others, seconds):
            contact_arrays.append([held, lax.ppermute(held, "xy", to_first), got])
        return mail, [near_hot, far_hot, first_hot, second_hot]

    def one_hots(slot, mail):
        def body(own_ref, first_ref, second_ref, mail_ref, near_hot, *hot_refs):
            flags = flags_here()
            spheres = {slot: Spheres(mail_ref, sizes, sizes.section_groups)}
            maps = Maps(spheres, sizes, flags)
            packs = [Contacts(ref) for ref in (own_ref, first_ref, second_ref)]
            lay_hot(packs[0].tile(NEAR).astype(I32), near_hot)
            for which, pack in enumerate(packs):
                lay_hot(maps.section_row(slot, which, pack.tile(FAR).astype(I32)), hot_refs[which])

        return call(body, [hot_shape] * 4, [*contact_arrays[slot], mail])

    mail, hots = first_terms()
    mails = [mail] + [turned(mail, step) for step in range(1, slots)]
    for slot in range(1, slots):
        hots = [*hots, *one_hots(slot, mails[slot])]
    inputs = [*sum(contact_arrays, []), *mails, *hots]

    def first_velocities():
        def body(*refs):
            flags = flags_here()
            mail_refs, refs = refs[:slots], refs[slots:]
            spheres = [Spheres(ref, sizes, sizes.section_groups) for ref in mail_refs]
            maps = Maps(spheres, sizes, flags)
            sections = [[ref[:, pl.ds(group * LANES, LANES)] for group in every] for ref in mail_refs]
            sums = [joined(sections, spheres, sizes, flags, slot) for slot in range(slots)]
            put_velocities(sums, spheres, maps, flags, *refs)

        return call(body, [section_shape, sent_shape, sent_shape], [*mails])

    def gradients(section, sent, got, state):
        def body(section_ref, sent_first, sent_second, got_first, got_second, *refs):
            flags = flags_here()
            sets, spheres, hots, refs = views(refs)
            if state is None:
                state_ref = None
            else:
                state_ref, *refs = refs
            grad_ref, parts_ref, table_ref, *scratch = refs
            maps = Maps(spheres, sizes, flags)
            even = flags[0] == 0
            norm = soft = jnp.zeros((blocks, LANES), F32)
            lane = lax.broadcasted_iota(I32, (8, LANES), 1)
            edge = sizes.side % LANES

            def rows_from(ref, slot, start, count):
                def rows(body):
                    return [ref[slot, pl.ds(body, 1), pl.ds(start + g * LANES, LANES)] for g in range(count)]

                return rows

            values = []
            for slot in range(slots):
                low, high = [], []
                for group in range(sizes.window_groups):
                    lanes = pl.ds(sizes.own + group * LANES, LANES)
                    first = jnp.where(flags[1] != 0, got_first[slot, :, lanes], 0.0)
                    second = jnp.where(flags[2] != 0, got_second[slot, :, lanes], 0.0)
                    low.append(jnp.where(even, second, first))
                    high.append(jnp.where(even, first, second))
                if edge:
                    extended = low[:-1] + [jnp.where(lane < edge, low[-1], high[0])] + high[1:]
                else:
                    extended = low + high
                table_ref[slot, :, pl.ds(0, sizes.section)] = section_ref[slot]
                for group, value in enumerate(extended):
                    table_ref[slot, :, pl.ds(sizes.section + group * LANES, LANES)] = value
                slot_values = []
                for which, pack in enumerate(sets[slot]):
                    far = pack.tile(FAR).astype(I32)
                    if which == 0:
                        near_rows = rows_from(table_ref, slot, 0, sizes.own_groups)
                        far_rows = rows_from(table_ref, slot, 0, sizes.total_groups)
                    else:
                        got_ref = (got_first, got_second)[which - 1]
                        sent_ref = (sent_first, sent_second)[which - 1]
                        near_rows = rows_from(got_ref, slot, 0, sizes.own_groups)
                        far_rows = rows_from(sent_ref, slot, sizes.own, sizes.window_groups)
                        far = maps.window_index(far, which)
                    contact_rows = rows_of(pack, near_rows, far_rows, far)
                    alive, softness = pack.tile(ALIVE), pack.tile(SOFTNESS)
                    grad = []
                    for row in range(3):
                        guess = pack.tile(GUESS + row) if state_ref is None else state_ref[slot, which, row]
                        value = contact_rows[row] + softness * guess
                        if row == 0:
                            value = value + pack.tile(OFFSET)
                        value = alive * value
                        grad_ref[slot, which, row] = value
                        grad.append(value)
                        if which == 0:
                            norm = norm + value * value
                            soft = soft + softness * value * value
                    slot_values.append(grad)
                values.append(slot_values)
            sections = slot_sections(sets, values, maps, hots, scratch, [every] * slots)
            sums = [joined(sections, spheres, sizes, flags, slot) for slot in range(slots)]
            curve = jnp.sum(soft, axis=0, keepdims=True)
            norm = jnp.sum(norm, axis=0, keepdims=True)
            total = jnp.zeros((8, LANES), F32)
            for slot in range(slots):
                for group in range(sizes.own_groups):
                    value = sums[slot][group]
                    total = total + spheres[slot].weight(group) * value * value
            curve = curve + jnp.sum(total, axis=0, keepdims=True)
            half = LANES // 2
            norm = norm + pltpu.roll(norm, half, 1)
            curve = curve + pltpu.roll(curve, half, 1)
            both = jnp.where(lax.broadcasted_iota(I32, (1, LANES), 1) < half, norm, curve)
            for cell in range(cells):
                parts_ref[cell] = both

        return call(
            body,
            [state_shape, (cells, 1, LANES)],
            chosen(section, *sent, *got, *inputs, state),
            [pltpu.VMEM((slots, 8, sizes.total_groups * LANES), F32), *work, *work],
        )

    def updates(parts, grad, state, earlier, factor):
        last = factor is None

        def body(part_ref, grad_ref, *refs):
            flags = flags_here()
            sets, spheres, hots, refs = views(refs)
            if state is not None:
                state_ref, earlier_ref, *refs = refs
            if last:
                result_ref, velocity_ref, *scratch = refs
            else:
                result_ref, guess_ref, section_ref, first_ref, second_ref, *scratch = refs
            maps = Maps(spheres, sizes, flags)
            total = part_ref[0]
            for cell in range(1, cells):
                total = total + part_ref[cell]
            lane = lax.broadcasted_iota(I32, (1, LANES), 1)
            norm = jnp.sum(jnp.where(lane < LANES // 2, total, 0.0), axis=1, keepdims=True)
            curve = jnp.sum(jnp.where(lane < LANES // 2, 0.0, total), axis=1, keepdims=True)
            step = norm / (curve + EPSILON)
            values = []
            for slot in range(slots):
                slot_values = []
                for which, pack in enumerate(sets[slot]):
                    alive = pack.tile(ALIVE)
                    moved, before = [], []
                    for row in range(3):
                        if state is None:
                            guess, old = pack.tile(GUESS + row), pack.tile(CURRENT + row)
                        else:
                            guess, old = state_ref[slot, which, row], earlier_ref[slot, which, row]
                        before.append(old)
                        moved.append(guess - step * grad_ref[slot, which, row])
                    value = [alive * v for v in cone_project(moved, pack.tile(FRICTION))]
                    if not last:
                        guess = [alive * (v + factor * (v - b)) for v, b in zip(value, before)]
                        for row in range(3):
                            result_ref[slot, which, row] = value[row]
                            guess_ref[slot, which, row] = guess[row]
                        value = guess
                    elif slot == which == 0:
                        for row in range(3):
                            result_ref[row] = value[row]
                    slot_values.append(value)
                values.append(slot_values)
            wanted = [every] * slots
            if last:
                wanted = [[] for _ in range(slots)]
                wanted[-1] = every[sizes.own_groups :]
                wanted[0] = every[: sizes.own_groups]
            sections = slot_sections(sets, values, maps, hots, scratch, wanted)
            if last:
                total = joined(sections, spheres, sizes, flags, 0)
                for group in range(sizes.own_groups):
                    value = spheres[0].free(group) + spheres[0].weight(group) * total[group]
                    for body_row in range(6):
                        velocity_ref[body_row, pl.ds(group, 1), :] = value[body_row : body_row + 1]
            else:
                sums = [joined(sections, spheres, sizes, flags, slot) for slot in range(slots)]
                put_velocities(sums, spheres, maps, flags, section_ref, first_ref, second_ref)

        if last:
            shapes = [(3, blocks, LANES), (6, sizes.own_groups, LANES)]
        else:
            shapes = [state_shape, state_shape, section_shape, sent_shape, sent_shape]
        return call(body, shapes, chosen(parts, grad, *inputs, state, earlier), [*work, *work])

    state = earlier = None
    section, *sent = first_velocities()
    for iteration in range(ITERS):
        grad, parts = gradients(section, sent, swap(*sent), state)
        parts = lax.all_to_all(parts, "xy", 0, 0, tiled=True)
        if iteration + 1 < ITERS:
            earlier, state, section, *sent = updates(parts, grad, state, earlier, factors[iteration + 1])
    result, velocity = updates(parts, grad, state, earlier, None)
    return (
        result.reshape(1, 1, 3, sizes.contacts),
        velocity.reshape(1, 1, 6, sizes.own),
    )


def solution(mesh):
    placed = (
        P("gz", "xy", None, None),
        P("gz", "xy", None, None),
        P("gz", "xy", None, None),
        P("gz", "xy", None, None),
        P("gz", "xy", None, None),
        P("gz", "xy", None),
        P("gz", "xy", None),
        P("gz", "xy", None),
        P("gz", "xy", None),
        P("gz", "xy", None),
        P("gz", "xy", None),
        P("gz", "xy", None),
        P("gz", "xy", None, None),
    )
    return jax.shard_map(
        on_device,
        mesh=mesh,
        in_specs=placed,
        out_specs=(P("gz", "xy", None, None), P("gz", "xy", None, None)),
        check_vma=False,
    )
```

```python
import math

import jax
import jax.numpy as jnp
from jax import lax
from jax.experimental import pallas as pl
from jax.experimental.pallas import tpu as pltpu
from jax.sharding import PartitionSpec as P

ITERS = 2
EPSILON = 1e-06
THETA_START = 0.3
LANES = 128
WIDE = 256
F32 = jnp.float32
BF16 = jnp.bfloat16
I32 = jnp.int32


def theta_after(theta_value):
    return 0.5 * (
        -theta_value * theta_value + theta_value * math.sqrt(theta_value * theta_value + 4.0)
    )


def momentum_factors(iteration_count):
    thetas = [THETA_START]
    for iteration in range(iteration_count):
        thetas.append(theta_after(thetas[-1]))
    return [
        thetas[position]
        * (1.0 - thetas[position])
        / (thetas[position] * thetas[position] + thetas[position + 1])
        for position in range(iteration_count)
    ]


def pair_swaps(count, parity):
    target = list(range(count))
    for cell in range(parity, count - 1, 2):
        target[cell], target[cell + 1] = cell + 1, cell
    return list(enumerate(target))


class Sizes:
    def __init__(self, contacts, own, layer, side, slots, cells):
        self.contacts, self.own, self.layer, self.side = contacts, own, layer, side
        self.slots, self.cells = slots, cells
        self.blocks = contacts // LANES
        self.section = own + layer
        self.window = -(-side // LANES) * LANES
        self.margin = self.window - side
        self.own_groups = own // LANES
        self.layer_groups = layer // LANES
        self.section_groups = self.section // LANES
        self.total_groups = (self.section + 2 * side) // LANES
        self.window_groups = self.window // LANES
        self.layer_at = 2 * self.own_groups
        self.side_at = self.layer_at + self.layer_groups
        self.sphere_groups = self.side_at + self.window_groups
        self.mail_groups = self.section_groups + self.sphere_groups
        self.sent_rows = 3 * self.blocks + 8 * self.window_groups
        assert contacts % LANES == own % LANES == layer % LANES == 2 * side % LANES == 0
        assert self.blocks % 8 == 0


FAR, ALIVE, FRICTION, SOFTNESS, CURRENT, GUESS, NEAR_PART, NEAR, OFFSET = 18, 19, 20, 21, 22, 25, 28, 46, 47
SHARED, TILES = 28, 48


class Contacts:
    def __init__(self, ref):
        self.ref = ref

    def tile(self, which):
        return self.ref[which]

    def entry(self, row, part, body, rows=slice(None)):
        return self.ref[6 * row + body + (0 if part else NEAR_PART), rows, :]


class Spheres:
    def __init__(self, ref, sizes, start=0):
        self.ref, self.sizes, self.start = ref, sizes, start

    def misc(self, group):
        return self.ref[:, pl.ds((self.start + group) * LANES, LANES)]

    def free(self, group):
        return self.misc(group)

    def weight(self, group):
        return self.misc(self.sizes.own_groups + group)

    def layer_list(self, group):
        return self.misc(self.sizes.layer_at + group)[0:1].astype(I32)

    def side_list(self, which, group):
        return self.misc(self.sizes.side_at + group)[which : which + 1].astype(I32)


def places(index, groups):
    index = jnp.broadcast_to(index, (8, LANES))
    which = index >> 7
    return index & (LANES - 1), [which == number for number in range(groups)]


def gather(groups, place):
    lane, inside = place
    out = jnp.zeros((8, LANES), groups[0].dtype)
    for group, here in zip(groups, inside):
        group = jnp.broadcast_to(group, (8, LANES))
        out = jnp.where(here, jnp.take_along_axis(group, lane, axis=1, mode="promise_in_bounds"), out)
    return out


def look_up(lists, index):
    pieces = [
        gather(lists, places(index[at : at + 8], len(lists))) for at in range(0, index.shape[0], 8)
    ]
    return jnp.concatenate(pieces, axis=0) - 1


def lay_hot(index, hot_ref):
    lane_of = (index & (LANES - 1)).astype(F32)
    row_number = lax.broadcasted_iota(I32, (LANES, LANES), 0).astype(F32).astype(BF16)
    zeros, ones = jnp.zeros((16, LANES), BF16), jnp.ones((16, LANES), BF16)
    for block in range(index.shape[0]):
        low = jnp.broadcast_to(lane_of[block : block + 1], (16, LANES)).astype(BF16)
        for piece in range(LANES // 16):
            rows = slice(piece * 16, piece * 16 + 16)
            hot = jnp.where(row_number[rows] == low, ones, zeros)
            hot_ref[pl.ds(piece * 16, 16), pl.ds(block * LANES, LANES)] = hot


def lay_terms(terms, index, groups, parts_ref, spread_ref):
    blocks = terms[0].shape[0]
    for body, term in enumerate(terms):
        upper = term.astype(BF16).astype(F32)
        parts_ref[pl.ds(body * blocks, blocks), :] = upper
        parts_ref[pl.ds((8 + body) * blocks, blocks), :] = term - upper
    gap = jnp.zeros((2 * blocks, LANES), F32)
    parts_ref[pl.ds(6 * blocks, 2 * blocks), :] = gap
    parts_ref[pl.ds(14 * blocks, 2 * blocks), :] = gap
    group_of = (index >> 7).astype(F32)
    zeros = jnp.zeros((16, LANES), BF16)
    for block in range(blocks):
        both = parts_ref[pl.ds(block, 16, stride=blocks), :].astype(BF16)
        which = jnp.broadcast_to(group_of[block : block + 1], (16, LANES)).astype(BF16)
        for at, number in enumerate(groups):
            part = jnp.where(which == jnp.asarray(number, BF16), both, zeros)
            spread_ref[pl.ds(at * 16, 16), pl.ds(block * LANES, LANES)] = part


def summed(spread, hot):
    out = lax.dot_general(spread, hot, (((1,), (1,)), ((), ())), preferred_element_type=F32)
    return [out[at : at + 8] + out[at + 8 : at + 16] for at in range(0, out.shape[0], 16)]


def put_columns(values, lists, groups):
    result = [jnp.zeros((8, LANES), F32)] * groups
    row_number = lax.broadcasted_iota(I32, (LANES, LANES), 0)
    for value, index in zip(values, lists):
        upper = value.astype(BF16).astype(F32)
        both = jnp.concatenate([upper, value - upper], axis=0)
        which = jnp.broadcast_to(index >> 7, (16, LANES))
        spread = jnp.concatenate([jnp.where(which == g, both, 0.0) for g in range(groups)], axis=0)
        low = jnp.broadcast_to(index & (LANES - 1), (LANES, LANES))
        hot = jnp.where(row_number == low, 1.0, 0.0).astype(BF16)
        result = [a + b for a, b in zip(result, summed(spread.astype(BF16), hot))]
    return result


class Maps:
    def __init__(self, spheres, sizes, flags):
        self.spheres, self.sizes, self.flags = spheres, sizes, flags

    def upper(self, slot):
        above = self.spheres[(slot + 1) % self.sizes.slots]
        return [above.layer_list(group) for group in range(self.sizes.layer_groups)]

    def side(self, slot, which):
        picks = []
        for group in range(self.sizes.window_groups):
            to_lower = self.spheres[slot].side_list(0, group)
            to_higher = self.spheres[slot].side_list(1, group)
            higher = (self.flags[0] == 0) == (which == 1)
            picks.append(jnp.where(higher, to_higher, to_lower))
        return picks

    def window_index(self, far, which):
        sizes = self.sizes
        higher = (self.flags[0] == 0) == (which == 1)
        return far - jnp.where(higher, sizes.section, sizes.section + sizes.side - sizes.margin)

    def section_row(self, slot, which, far):
        if which == 0:
            return jnp.where(far < self.sizes.section, far, -1)
        row = look_up(self.side(slot, which), self.window_index(far, which))
        return jnp.where(self.flags[which] != 0, row, -1)


def set_terms(slot, which, pack, value, maps, sizes, hots, scratch, groups, new_hots=False, live=None):
    rows = slice(0, live)
    columns = pl.ds(0, (live or sizes.blocks) * LANES)
    value = [v[rows] for v in value]
    far_hot, near_hot = hots
    parts_ref, spread_ref, near_parts, near_spread = scratch
    far = maps.section_row(slot, which, pack.tile(FAR).astype(I32))
    own = [group for group in groups if group < sizes.own_groups] if which == 0 else []
    todo = [(1, far, groups, far_hot, parts_ref, spread_ref)]
    if own:
        todo.append((0, pack.tile(NEAR).astype(I32), own, near_hot, near_parts, near_spread))
    result = {}
    for part, index, wanted, hot_ref, to_parts, to_spread in todo:
        terms = [
            pack.entry(0, part, body, rows) * value[0]
            + pack.entry(1, part, body, rows) * value[1]
            + pack.entry(2, part, body, rows) * value[2]
            for body in range(6)
        ]
        if new_hots:
            lay_hot(index, hot_ref)
        lay_terms(terms, index[rows], wanted, to_parts, to_spread)
        sums = summed(to_spread[pl.ds(0, 16 * len(wanted)), columns], hot_ref[:, columns])
        for group, total in zip(wanted, sums):
            result[group] = result[group] + total if group in result else total
    return [result[group] for group in groups]


def added(lists):
    return [sum(values[1:], values[0]) for values in zip(*lists)]


def joined(sections, spheres, sizes, flags, slot):
    own = [sections[slot][group] for group in range(sizes.own_groups)]
    if sizes.slots > 1:
        below = (slot + sizes.slots - 1) % sizes.slots
        above = [sections[below][group] for group in range(sizes.own_groups, sizes.section_groups)]
        upper = [jnp.where(flags[3 + below] != 0, value, 0.0) for value in above]
        lists = [spheres[slot].layer_list(group) - 1 for group in range(sizes.layer_groups)]
        own = added([own, put_columns(upper, lists, sizes.own_groups)])
    return own


def rows_of(pack, part, table, index):
    groups = len(table(0))
    halves = []
    for at in range(0, index.shape[0], 8):
        rows = slice(at, at + 8)
        place = places(index[rows], groups)
        totals = [None] * 3
        for body in range(6):
            picked = gather(table(body), place)
            for row in range(3):
                term = pack.entry(row, part, body, rows) * picked
                totals[row] = term if totals[row] is None else totals[row] + term
        halves.append(totals)
    return [jnp.concatenate([half[row] for half in halves], axis=0) for row in range(3)]


def rows_from(ref, slot, start, count):
    def rows(body):
        return [ref[slot, pl.ds(body, 1), pl.ds(start + g * LANES, LANES)] for g in range(count)]

    return rows


def cone_project(impulse_value, cone_friction):
    normal, first, second = impulse_value
    slide_norm = jnp.sqrt(first * first + second * second)
    inside_cone = slide_norm <= cone_friction * normal
    polar_cone = cone_friction * slide_norm <= -normal
    outside_both = jnp.logical_not(jnp.logical_or(inside_cone, polar_cone))
    onto_normal = (cone_friction * slide_norm + normal) / (cone_friction * cone_friction + 1.0)
    tangent_scale = cone_friction * onto_normal / jnp.where(outside_both, slide_norm, 1.0)
    scale = jnp.where(inside_cone, 1.0, jnp.where(polar_cone, 0.0, tangent_scale))
    new_normal = jnp.where(inside_cone, normal, jnp.where(polar_cone, 0.0, onto_normal))
    return [new_normal, scale * first, scale * second]


def call(body, out_shape, operands, scratch=(), space=pltpu.VMEM, room=40, out_space=pltpu.VMEM):
    return pl.pallas_call(
        body,
        out_shape=[
            jax.ShapeDtypeStruct(*shape) if isinstance(shape[0], tuple) else jax.ShapeDtypeStruct(shape, F32)
            for shape in out_shape
        ],
        in_specs=[pl.BlockSpec(memory_space=space)] * len(operands),
        out_specs=[pl.BlockSpec(memory_space=out_space)] * len(out_shape),
        scratch_shapes=list(scratch),
        compiler_params=pltpu.CompilerParams(vmem_limit_bytes=room * 1024 * 1024),
    )(*operands)


def on_device(
    velocity_free,
    inverse_mass,
    jacobian,
    impulses,
    previous_impulses,
    compliance,
    offset,
    friction,
    body_near,
    body_far,
    block_counts,
    layer_send,
    side_send,
):
    slots, cells = lax.axis_size("gz"), lax.axis_size("xy")
    sizes = Sizes(
        jacobian.shape[3], velocity_free.shape[3], layer_send.shape[2], side_send.shape[3], slots, cells
    )
    blocks, window = sizes.blocks, sizes.window
    factors = momentum_factors(ITERS)

    def flags_here():
        layer_at, cell_at = lax.axis_index("gz"), lax.axis_index("xy")
        odd = cell_at % 2
        lower, higher = cell_at > 0, cell_at < cells - 1
        places = [odd, jnp.where(odd == 0, higher, lower), jnp.where(odd == 0, lower, higher)]
        places += [(layer_at + slot) % slots != slots - 1 for slot in range(slots)]
        return [place.astype(I32) for place in places]

    def tiles(array):
        return array.reshape(-1, blocks, LANES)

    def pack_body(*refs):
        inputs, (contact_out, shared_out, sphere_out, *held, out_ref, sphere_ref, semaphores) = refs[:13], refs[13:]
        moves = list(zip([*inputs[:2], *inputs[3:]], held))
        for row in range(3):
            near, far = pl.ds(12 * row, 6), pl.ds(12 * row + 6, 6)
            moves.append((inputs[2].at[far], out_ref.at[pl.ds(6 * row, 6)]))
            moves.append((inputs[2].at[near], out_ref.at[pl.ds(NEAR_PART + 6 * row, 6)]))
        count = len(moves)
        ends = [(0, FAR), (FAR, SHARED), (NEAR_PART, NEAR), (NEAR, TILES)]
        for start, end in ends:
            moves.append((out_ref.at[pl.ds(start, end - start)], contact_out.at[pl.ds(start, end - start)]))
        for start, end in ends[:2]:
            moves.append((out_ref.at[pl.ds(start, end - start)], shared_out.at[pl.ds(start, end - start)]))
        moves.append((sphere_ref, sphere_out))
        copies = [pltpu.make_async_copy(*move, semaphores.at[at]) for at, move in enumerate(moves)]
        arrays, jacobians, out = copies[: count - 6], copies[count - 6 : count], copies[count:]
        for copy in [*jacobians, *arrays]:
            copy.start()
        for copy in arrays:
            copy.wait()
        (free_ref, mass_ref, imp_ref, prev_ref, soft_ref, off_ref, fric_ref, near_ref, far_ref,
         layer_ref, side_ref, counts) = held
        lane = lax.broadcasted_iota(I32, (1, LANES), 1)
        rows = [jnp.where(lane < counts[block], 1.0, 0.0) for block in range(blocks)]
        alive = jnp.concatenate(rows, axis=0)
        out_ref[NEAR] = near_ref[0].astype(F32)
        out_ref[FAR] = far_ref[0].astype(F32)
        out_ref[ALIVE] = alive
        out_ref[FRICTION] = fric_ref[0]
        out_ref[SOFTNESS] = soft_ref[0]
        out_ref[OFFSET] = off_ref[0]
        for row in range(3):
            current = alive * imp_ref[row]
            earlier = alive * prev_ref[row]
            out_ref[CURRENT + row] = current
            out_ref[GUESS + row] = alive * (current + factors[0] * (current - earlier))

        gap = jnp.zeros((2, LANES), F32)

        def misc(group, value):
            sphere_ref[:, pl.ds(group * LANES, LANES)] = value

        for group in range(sizes.own_groups):
            lanes = pl.ds(group * LANES, LANES)
            free = [free_ref[body, pl.ds(group, 1), :] for body in range(6)]
            misc(group, jnp.concatenate(free + [gap], axis=0))
            mass = mass_ref[:, lanes]
            linear = jnp.broadcast_to(mass[0:1], (3, LANES))
            angular = jnp.broadcast_to(mass[1:2], (3, LANES))
            misc(sizes.own_groups + group, jnp.concatenate([linear, angular, gap], axis=0))
        for group in range(sizes.layer_groups):
            lanes = pl.ds(group * LANES, LANES)
            rows = jnp.broadcast_to(layer_ref[:, lanes] + 1, (8, LANES))
            misc(sizes.layer_at + group, rows.astype(F32))
        side = side_ref[...] + 1
        if sizes.margin:
            none = jnp.zeros((1, sizes.margin), I32)
            to_lower = jnp.concatenate([none, side[0:1]], axis=1)
            to_higher = jnp.concatenate([side[1:2], none], axis=1)
            side = jnp.concatenate([to_lower, to_higher], axis=0)
        for group in range(sizes.window_groups):
            rows = jnp.concatenate([side[:, group * LANES : (group + 1) * LANES]] * 4, axis=0)
            misc(sizes.side_at + group, rows.astype(F32))
        for copy in jacobians:
            copy.wait()
        for copy in out:
            copy.start()
        for copy in out:
            copy.wait()

    loaded = [
        velocity_free[0, 0].reshape(6, sizes.own_groups, LANES),
        inverse_mass[0, 0],
        tiles(jacobian[0, 0]),
        tiles(impulses[0, 0]),
        tiles(previous_impulses[0, 0]),
        tiles(compliance[0, 0]),
        tiles(offset[0, 0]),
        tiles(friction[0, 0]),
        tiles(body_near[0, 0]),
        tiles(body_far[0, 0]),
        layer_send[0],
        side_send[0, 0],
        block_counts[0, 0],
    ]
    own_contacts, own_shared, own_spheres = call(
        pack_body,
        [(TILES, blocks, LANES), (SHARED, blocks, LANES), (8, sizes.sphere_groups * LANES)],
        loaded,
        [pltpu.VMEM(array.shape, array.dtype) for at, array in enumerate(loaded[:-1]) if at != 2]
        + [
            pltpu.SMEM(block_counts.shape[2:], I32),
            pltpu.VMEM((TILES, blocks, LANES), F32),
            pltpu.VMEM((8, sizes.sphere_groups * LANES), F32),
            pltpu.SemaphoreType.DMA((len(loaded) - 1 + 6 + 7,)),
        ],
        pl.ANY,
        62,
        pl.ANY,
    )
    to_first, to_second = pair_swaps(cells, 0), pair_swaps(cells, 1)

    def swap(first, second):
        return lax.ppermute(first, "xy", to_first), lax.ppermute(second, "xy", to_second)

    def turned(array, step):
        return lax.ppermute(array, "gz", [((i + step) % slots, i) for i in range(slots)])

    contact_arrays = [[own_contacts, *swap(own_shared, own_shared)]]
    above_contacts = [turned(own_contacts, slot) for slot in range(1, slots)]

    def views(refs):
        sets = [[Contacts(refs[3 * s + w]) for w in range(3)] for s in range(slots)]
        refs = refs[3 * slots :]
        spheres = [Spheres(ref, sizes, sizes.section_groups) for ref in refs[:slots]]
        refs = refs[slots:]
        hots = [
            [(refs[4 * s + 1 + w], refs[4 * s] if w == 0 else None) for w in range(3)] for s in range(slots)
        ]
        return sets, spheres, hots, refs[4 * slots :]

    def chosen(*arrays):
        return [array for array in arrays if array is not None]

    state_shape = (slots, 3, 3, blocks, LANES)
    section_shape, sent_shape = (slots, 8, sizes.section), (slots, sizes.sent_rows, LANES)
    hot_shape = ((LANES, sizes.contacts), BF16)

    def scratch_of(own):
        split = pltpu.VMEM((16 * blocks, LANES), F32)
        spread = [pltpu.VMEM((16 * n, sizes.contacts), BF16) for n in (sizes.section_groups, sizes.own_groups)]
        return [split, spread[0]] + ([split, spread[1]] if own else [])

    work = scratch_of(True) + scratch_of(False) * 2

    def places_of(scratch, slot, which):
        base = (slot % 2) * len(work)
        if which == 0:
            return scratch[base : base + 4]
        return [*scratch[base + 2 + 2 * which : base + 4 + 2 * which], None, None]

    def slot_sections(sets, values, maps, hots, scratch, wanted, section_ref):
        half = blocks // 2 if blocks % 16 == 0 else blocks

        def fill(s, live):
            packs = list(zip(sets[s], values[s], hots[s]))
            terms = [
                set_terms(
                    s, w, pack, value, maps, sizes, hot, places_of(scratch, s, w), wanted[s], live=live
                )
                for w, (pack, value, hot) in enumerate(packs)
            ]
            for group, total in zip(wanted[s], added(terms)):
                section_ref[s, :, pl.ds(group * LANES, LANES)] = total

        for s, groups in enumerate(wanted):
            if not groups:
                continue
            alive = [pack.tile(ALIVE)[half:] for pack in sets[s]]
            if half == blocks:
                fill(s, blocks)
                continue
            more = jnp.max(jnp.maximum(jnp.maximum(alive[0], alive[1]), alive[2])) > 0.0
            pl.when(more)(lambda s=s: fill(s, blocks))
            pl.when(jnp.logical_not(more))(lambda s=s: fill(s, half))
        return [
            {group: section_ref[s, :, pl.ds(group * LANES, LANES)] for group in groups}
            for s, groups in enumerate(wanted)
        ]

    every = list(range(sizes.section_groups))
    held_sections = pltpu.VMEM(section_shape, F32)

    def window_rows(group):
        return pl.ds(3 * blocks + 8 * group, 8)

    def put_velocities(sums, spheres, maps, flags, owns, section_ref, first_ref, second_ref):
        velocity = [
            [spheres[s].free(g) + spheres[s].weight(g) * sums[s][g] for g in range(sizes.own_groups)]
            for s in range(slots)
        ]
        for slot in range(slots):
            table = list(velocity[slot])
            for rows in maps.upper(slot):
                upper = gather(velocity[(slot + 1) % slots], places(rows - 1, sizes.own_groups))
                table.append(jnp.where(flags[3 + slot] != 0, upper, 0.0))
            for group, value in enumerate(table):
                section_ref[slot, :, pl.ds(group * LANES, LANES)] = value
            for which, sent_ref in ((1, first_ref), (2, second_ref)):
                for group, rows in enumerate(maps.side(slot, which)):
                    sent_ref[slot, window_rows(group), :] = gather(table, places(rows - 1, sizes.section_groups))
            pack = owns[slot]
            rows = rows_from(section_ref, slot, 0, sizes.own_groups)
            near = rows_of(pack, 0, rows, pack.tile(NEAR).astype(I32))
            near[0] = near[0] + pack.tile(OFFSET)
            for row in range(3):
                first_ref[slot, pl.ds(row * blocks, blocks), :] = near[row]
                second_ref[slot, pl.ds(row * blocks, blocks), :] = near[row]

    def first_terms():
        def guess_of(pack):
            return [pack.tile(GUESS + row) for row in range(3)]

        def early(own_ref, first_ref, sphere_ref, out_ref, near_hot, far_hot, first_hot, *scratch):
            flags = flags_here()
            maps = Maps([Spheres(sphere_ref, sizes)], sizes, flags)
            sets = [Contacts(own_ref), Contacts(first_ref)]
            hots = [(far_hot, near_hot), (first_hot, None)]
            sums = added(
                [
                    set_terms(
                        0, w, sets[w], guess_of(sets[w]), maps, sizes, hots[w], places_of(scratch, 0, w),
                        every, True,
                    )
                    for w in range(2)
                ]
            )
            for group, value in enumerate(sums):
                out_ref[:, pl.ds(group * LANES, LANES)] = value

        def late(part_ref, second_ref, sphere_ref, out_ref, hot_ref, *scratch):
            flags = flags_here()
            maps = Maps([Spheres(sphere_ref, sizes)], sizes, flags)
            pack = Contacts(second_ref)
            sums = set_terms(
                0, 2, pack, guess_of(pack), maps, sizes, (hot_ref, None), [*scratch, None, None], every, True
            )
            for group, value in enumerate(sums):
                lanes = pl.ds(group * LANES, LANES)
                out_ref[:, lanes] = part_ref[:, lanes] + value
            out_ref[:, pl.ds(sizes.section, sizes.sphere_groups * LANES)] = sphere_ref[...]

        own, first, second = contact_arrays[0]
        part, near_hot, far_hot, first_hot = call(
            early, [(8, sizes.section), hot_shape, hot_shape, hot_shape], [own, first, own_spheres], work[:6]
        )
        mail, second_hot = call(
            late,
            [(8, sizes.mail_groups * LANES), hot_shape],
            [part, second, own_spheres],
            work[4:6],
        )
        mail, *others = lax.optimization_barrier((mail, *above_contacts))
        for held in others:
            contact_arrays.append([held, *swap(held[:SHARED], held[:SHARED])])
        return mail, [near_hot, far_hot, first_hot, second_hot]

    def one_hots(slot, mail):
        def body(own_ref, first_ref, second_ref, mail_ref, near_hot, *hot_refs):
            flags = flags_here()
            spheres = {slot: Spheres(mail_ref, sizes, sizes.section_groups)}
            maps = Maps(spheres, sizes, flags)
            packs = [Contacts(ref) for ref in (own_ref, first_ref, second_ref)]
            lay_hot(packs[0].tile(NEAR).astype(I32), near_hot)
            for which, pack in enumerate(packs):
                lay_hot(maps.section_row(slot, which, pack.tile(FAR).astype(I32)), hot_refs[which])

        return call(body, [hot_shape] * 4, [*contact_arrays[slot], mail])

    mail, hots = first_terms()
    mails = [mail] + [turned(mail, step) for step in range(1, slots)]
    for slot in range(1, slots):
        hots = [*hots, *one_hots(slot, mails[slot])]
    inputs = [*sum(contact_arrays, []), *mails, *hots]

    def first_velocities():
        def body(*refs):
            flags = flags_here()
            mail_refs, own_refs, refs = refs[:slots], refs[slots : 2 * slots], refs[2 * slots :]
            spheres = [Spheres(ref, sizes, sizes.section_groups) for ref in mail_refs]
            maps = Maps(spheres, sizes, flags)
            sections = [[ref[:, pl.ds(group * LANES, LANES)] for group in every] for ref in mail_refs]
            sums = [joined(sections, spheres, sizes, flags, slot) for slot in range(slots)]
            put_velocities(sums, spheres, maps, flags, [Contacts(ref) for ref in own_refs], *refs)

        owns = [contact_arrays[slot][0] for slot in range(slots)]
        return call(body, [section_shape, sent_shape, sent_shape], [*mails, *owns])

    def gradients(section, sent, got, state):
        def body(section_ref, sent_first, sent_second, got_first, got_second, *refs):
            flags = flags_here()
            sets, spheres, hots, refs = views(refs)
            if state is None:
                state_ref = None
            else:
                state_ref, *refs = refs
            grad_ref, parts_ref, table_ref, *scratch = refs
            maps = Maps(spheres, sizes, flags)
            even = flags[0] == 0
            norm = soft = jnp.zeros((blocks, LANES), F32)
            lane = lax.broadcasted_iota(I32, (8, LANES), 1)
            edge = sizes.side % LANES

            values = []
            for slot in range(slots):
                low, high = [], []
                for group in range(sizes.window_groups):
                    first = jnp.where(flags[1] != 0, got_first[slot, window_rows(group), :], 0.0)
                    second = jnp.where(flags[2] != 0, got_second[slot, window_rows(group), :], 0.0)
                    low.append(jnp.where(even, second, first))
                    high.append(jnp.where(even, first, second))
                if edge:
                    extended = low[:-1] + [jnp.where(lane < edge, low[-1], high[0])] + high[1:]
                else:
                    extended = low + high
                table_ref[slot, :, pl.ds(0, sizes.section)] = section_ref[slot]
                for group, value in enumerate(extended):
                    table_ref[slot, :, pl.ds(sizes.section + group * LANES, LANES)] = value
                slot_values = []
                for which, pack in enumerate(sets[slot]):
                    far = pack.tile(FAR).astype(I32)
                    if which == 0:
                        near_ref = sent_first
                        table = rows_from(table_ref, slot, 0, sizes.total_groups)
                    else:
                        near_ref = (got_first, got_second)[which - 1]
                        listed = (sent_first, sent_second)[which - 1]
                        far = maps.window_index(far, which)

                        def table(body, listed=listed):
                            rows = [pl.ds(3 * blocks + 8 * g + body, 1) for g in range(sizes.window_groups)]
                            return [listed[slot, row, :] for row in rows]

                    contact_rows = rows_of(pack, 1, table, far)
                    alive, softness = pack.tile(ALIVE), pack.tile(SOFTNESS)
                    grad = []
                    for row in range(3):
                        guess = pack.tile(GUESS + row) if state_ref is None else state_ref[slot, which, row]
                        near = near_ref[slot, pl.ds(row * blocks, blocks), :]
                        value = alive * (near + contact_rows[row] + softness * guess)
                        grad_ref[slot, which, row] = value
                        grad.append(value)
                        if which == 0:
                            norm = norm + value * value
                            soft = soft + softness * value * value
                    slot_values.append(grad)
                values.append(slot_values)
            sections = slot_sections(sets, values, maps, hots, scratch[1:], [every] * slots, scratch[0])
            sums = [joined(sections, spheres, sizes, flags, slot) for slot in range(slots)]
            curve = jnp.sum(soft, axis=0, keepdims=True)
            norm = jnp.sum(norm, axis=0, keepdims=True)
            total = jnp.zeros((8, LANES), F32)
            for slot in range(slots):
                for group in range(sizes.own_groups):
                    value = sums[slot][group]
                    total = total + spheres[slot].weight(group) * value * value
            curve = curve + jnp.sum(total, axis=0, keepdims=True)
            half = LANES // 2
            norm = norm + pltpu.roll(norm, half, 1)
            curve = curve + pltpu.roll(curve, half, 1)
            both = jnp.where(lax.broadcasted_iota(I32, (1, LANES), 1) < half, norm, curve)
            for cell in range(cells):
                parts_ref[cell] = both

        return call(
            body,
            [state_shape, (cells, 1, LANES)],
            chosen(section, *sent, *got, *inputs, state),
            [pltpu.VMEM((slots, 8, sizes.total_groups * LANES), F32), held_sections, *work, *work],
        )

    def updates(parts, grad, state, earlier, factor):
        last = factor is None

        def body(part_ref, grad_ref, *refs):
            flags = flags_here()
            sets, spheres, hots, refs = views(refs)
            if state is not None:
                state_ref, earlier_ref, *refs = refs
            if last:
                result_ref, velocity_ref, *scratch = refs
            else:
                result_ref, guess_ref, section_ref, first_ref, second_ref, *scratch = refs
            maps = Maps(spheres, sizes, flags)
            total = part_ref[0]
            for cell in range(1, cells):
                total = total + part_ref[cell]
            lane = lax.broadcasted_iota(I32, (1, LANES), 1)
            norm = jnp.sum(jnp.where(lane < LANES // 2, total, 0.0), axis=1, keepdims=True)
            curve = jnp.sum(jnp.where(lane < LANES // 2, 0.0, total), axis=1, keepdims=True)
            step = norm / (curve + EPSILON)
            values = []
            for slot in range(slots):
                slot_values = []
                for which, pack in enumerate(sets[slot]):
                    alive = pack.tile(ALIVE)
                    moved, before = [], []
                    for row in range(3):
                        if state is None:
                            guess, old = pack.tile(GUESS + row), pack.tile(CURRENT + row)
                        else:
                            guess, old = state_ref[slot, which, row], earlier_ref[slot, which, row]
                        before.append(old)
                        moved.append(guess - step * grad_ref[slot, which, row])
                    value = [alive * v for v in cone_project(moved, pack.tile(FRICTION))]
                    if not last:
                        guess = [alive * (v + factor * (v - b)) for v, b in zip(value, before)]
                        for row in range(3):
                            result_ref[slot, which, row] = value[row]
                            guess_ref[slot, which, row] = guess[row]
                        value = guess
                    elif slot == which == 0:
                        for row in range(3):
                            result_ref[row] = value[row]
                    slot_values.append(value)
                values.append(slot_values)
            wanted = [every] * slots
            if last:
                wanted = [[] for _ in range(slots)]
                wanted[-1] = every[sizes.own_groups :]
                wanted[0] = every[: sizes.own_groups]
            sections = slot_sections(sets, values, maps, hots, scratch[1:], wanted, scratch[0])
            if last:
                total = joined(sections, spheres, sizes, flags, 0)
                for group in range(sizes.own_groups):
                    value = spheres[0].free(group) + spheres[0].weight(group) * total[group]
                    for body_row in range(6):
                        velocity_ref[body_row, pl.ds(group, 1), :] = value[body_row : body_row + 1]
            else:
                sums = [joined(sections, spheres, sizes, flags, slot) for slot in range(slots)]
                owns = [sets[slot][0] for slot in range(slots)]
                put_velocities(sums, spheres, maps, flags, owns, section_ref, first_ref, second_ref)

        if last:
            shapes = [(3, blocks, LANES), (6, sizes.own_groups, LANES)]
        else:
            shapes = [state_shape, state_shape, section_shape, sent_shape, sent_shape]
        return call(body, shapes, chosen(parts, grad, *inputs, state, earlier), [held_sections, *work, *work])

    state = earlier = None
    section, *sent = first_velocities()
    for iteration in range(ITERS):
        grad, parts = gradients(section, sent, swap(*sent), state)
        parts = lax.all_to_all(parts, "xy", 0, 0, tiled=True)
        if iteration + 1 < ITERS:
            earlier, state, section, *sent = updates(parts, grad, state, earlier, factors[iteration + 1])
    result, velocity = updates(parts, grad, state, earlier, None)
    return (
        result.reshape(1, 1, 3, sizes.contacts),
        velocity.reshape(1, 1, 6, sizes.own),
    )


def solution(mesh):
    placed = (
        P("gz", "xy", None, None),
        P("gz", "xy", None, None),
        P("gz", "xy", None, None),
        P("gz", "xy", None, None),
        P("gz", "xy", None, None),
        P("gz", "xy", None),
        P("gz", "xy", None),
        P("gz", "xy", None),
        P("gz", "xy", None),
        P("gz", "xy", None),
        P("gz", "xy", None),
        P("gz", "xy", None),
        P("gz", "xy", None, None),
    )
    return jax.shard_map(
        on_device,
        mesh=mesh,
        in_specs=placed,
        out_specs=(P("gz", "xy", None, None), P("gz", "xy", None, None)),
        check_vma=False,
    )
```

```python
import math

import jax
import jax.numpy as jnp
from jax import lax
from jax.experimental import pallas as pl
from jax.experimental.pallas import tpu as pltpu
from jax.sharding import PartitionSpec as P

ITERS = 2
EPSILON = 1e-06
THETA_START = 0.3
LANES = 128
WIDE = 256
F32 = jnp.float32
BF16 = jnp.bfloat16
I32 = jnp.int32


def theta_after(theta_value):
    return 0.5 * (
        -theta_value * theta_value + theta_value * math.sqrt(theta_value * theta_value + 4.0)
    )


def momentum_factors(iteration_count):
    thetas = [THETA_START]
    for iteration in range(iteration_count):
        thetas.append(theta_after(thetas[-1]))
    return [
        thetas[position]
        * (1.0 - thetas[position])
        / (thetas[position] * thetas[position] + thetas[position + 1])
        for position in range(iteration_count)
    ]


def pair_swaps(count, parity):
    target = list(range(count))
    for cell in range(parity, count - 1, 2):
        target[cell], target[cell + 1] = cell + 1, cell
    return list(enumerate(target))


class Sizes:
    def __init__(self, contacts, own, layer, side, slots, cells):
        self.contacts, self.own, self.layer, self.side = contacts, own, layer, side
        self.slots, self.cells = slots, cells
        self.blocks = contacts // LANES
        self.section = own + layer
        self.window = -(-side // LANES) * LANES
        self.margin = self.window - side
        self.own_groups = own // LANES
        self.layer_groups = layer // LANES
        self.section_groups = self.section // LANES
        self.total_groups = (self.section + 2 * side) // LANES
        self.window_groups = self.window // LANES
        self.layer_at = 2 * self.own_groups
        self.side_at = self.layer_at + self.layer_groups
        self.sphere_groups = self.side_at + self.window_groups
        self.mail_groups = self.section_groups + self.sphere_groups
        self.sent_rows = 3 * self.blocks + 8 * self.window_groups
        assert contacts % LANES == own % LANES == layer % LANES == 2 * side % LANES == 0
        assert self.blocks % 8 == 0


FAR, ALIVE, FRICTION, SOFTNESS, CURRENT, GUESS, NEAR_PART, NEAR, OFFSET = 18, 19, 20, 21, 22, 25, 28, 46, 47
SHARED, TILES = 28, 48


class Contacts:
    def __init__(self, ref, rest_ref=None):
        self.ref, self.rest_ref = ref, rest_ref

    def tile(self, which):
        return self.ref[which] if which < SHARED else self.rest_ref[which - SHARED]

    def entry(self, row, part, body, rows=slice(None)):
        return (self.ref if part else self.rest_ref)[6 * row + body, rows, :]


class Spheres:
    def __init__(self, ref, sizes, start=0):
        self.ref, self.sizes, self.start = ref, sizes, start

    def misc(self, group):
        return self.ref[:, pl.ds((self.start + group) * LANES, LANES)]

    def free(self, group):
        return self.misc(group)

    def weight(self, group):
        return self.misc(self.sizes.own_groups + group)

    def layer_list(self, group):
        return self.misc(self.sizes.layer_at + group)[0:1].astype(I32)

    def side_list(self, which, group):
        return self.misc(self.sizes.side_at + group)[which : which + 1].astype(I32)


def places(index, groups):
    index = jnp.broadcast_to(index, (8, LANES))
    which = index >> 7
    return index & (LANES - 1), [which == number for number in range(groups)]


def gather(groups, place):
    lane, inside = place
    out = jnp.zeros((8, LANES), groups[0].dtype)
    for group, here in zip(groups, inside):
        group = jnp.broadcast_to(group, (8, LANES))
        out = jnp.where(here, jnp.take_along_axis(group, lane, axis=1, mode="promise_in_bounds"), out)
    return out


def look_up(lists, index):
    pieces = [
        gather(lists, places(index[at : at + 8], len(lists))) for at in range(0, index.shape[0], 8)
    ]
    return jnp.concatenate(pieces, axis=0) - 1


def lay_hot(index, hot_ref):
    lane_of = (index & (LANES - 1)).astype(F32)
    row_number = lax.broadcasted_iota(I32, (LANES, LANES), 0).astype(F32).astype(BF16)
    zeros, ones = jnp.zeros((16, LANES), BF16), jnp.ones((16, LANES), BF16)
    for block in range(index.shape[0]):
        low = jnp.broadcast_to(lane_of[block : block + 1], (16, LANES)).astype(BF16)
        for piece in range(LANES // 16):
            rows = slice(piece * 16, piece * 16 + 16)
            hot = jnp.where(row_number[rows] == low, ones, zeros)
            hot_ref[pl.ds(piece * 16, 16), pl.ds(block * LANES, LANES)] = hot


def lay_terms(terms, index, groups, parts_ref, spread_ref):
    blocks = terms[0].shape[0]
    for body, term in enumerate(terms):
        upper = term.astype(BF16).astype(F32)
        parts_ref[pl.ds(body * blocks, blocks), :] = upper
        parts_ref[pl.ds((8 + body) * blocks, blocks), :] = term - upper
    gap = jnp.zeros((2 * blocks, LANES), F32)
    parts_ref[pl.ds(6 * blocks, 2 * blocks), :] = gap
    parts_ref[pl.ds(14 * blocks, 2 * blocks), :] = gap
    group_of = (index >> 7).astype(F32)
    zeros = jnp.zeros((16, LANES), BF16)
    for block in range(blocks):
        both = parts_ref[pl.ds(block, 16, stride=blocks), :].astype(BF16)
        which = jnp.broadcast_to(group_of[block : block + 1], (16, LANES)).astype(BF16)
        for at, number in enumerate(groups):
            part = jnp.where(which == jnp.asarray(number, BF16), both, zeros)
            spread_ref[pl.ds(at * 16, 16), pl.ds(block * LANES, LANES)] = part


def summed(spread, hot):
    out = lax.dot_general(spread, hot, (((1,), (1,)), ((), ())), preferred_element_type=F32)
    return [out[at : at + 8] + out[at + 8 : at + 16] for at in range(0, out.shape[0], 16)]


def put_columns(values, lists, groups):
    result = [jnp.zeros((8, LANES), F32)] * groups
    row_number = lax.broadcasted_iota(I32, (LANES, LANES), 0)
    for value, index in zip(values, lists):
        upper = value.astype(BF16).astype(F32)
        both = jnp.concatenate([upper, value - upper], axis=0)
        which = jnp.broadcast_to(index >> 7, (16, LANES))
        spread = jnp.concatenate([jnp.where(which == g, both, 0.0) for g in range(groups)], axis=0)
        low = jnp.broadcast_to(index & (LANES - 1), (LANES, LANES))
        hot = jnp.where(row_number == low, 1.0, 0.0).astype(BF16)
        result = [a + b for a, b in zip(result, summed(spread.astype(BF16), hot))]
    return result


class Maps:
    def __init__(self, spheres, sizes, flags):
        self.spheres, self.sizes, self.flags = spheres, sizes, flags

    def upper(self, slot):
        above = self.spheres[(slot + 1) % self.sizes.slots]
        return [above.layer_list(group) for group in range(self.sizes.layer_groups)]

    def side(self, slot, which):
        picks = []
        for group in range(self.sizes.window_groups):
            to_lower = self.spheres[slot].side_list(0, group)
            to_higher = self.spheres[slot].side_list(1, group)
            higher = (self.flags[0] == 0) == (which == 1)
            picks.append(jnp.where(higher, to_higher, to_lower))
        return picks

    def window_index(self, far, which):
        sizes = self.sizes
        higher = (self.flags[0] == 0) == (which == 1)
        return far - jnp.where(higher, sizes.section, sizes.section + sizes.side - sizes.margin)

    def section_row(self, slot, which, far):
        if which == 0:
            return jnp.where(far < self.sizes.section, far, -1)
        row = look_up(self.side(slot, which), self.window_index(far, which))
        return jnp.where(self.flags[which] != 0, row, -1)


def set_terms(slot, which, pack, value, maps, sizes, hots, scratch, groups, new_hots=False, live=None):
    rows = slice(0, live)
    columns = pl.ds(0, (live or sizes.blocks) * LANES)
    value = [v[rows] for v in value]
    far_hot, near_hot = hots
    parts_ref, spread_ref, near_parts, near_spread = scratch
    far = maps.section_row(slot, which, pack.tile(FAR).astype(I32))
    own = [group for group in groups if group < sizes.own_groups] if which == 0 else []
    todo = [(1, far, groups, far_hot, parts_ref, spread_ref)]
    if own:
        todo.append((0, pack.tile(NEAR).astype(I32), own, near_hot, near_parts, near_spread))
    result = {}
    for part, index, wanted, hot_ref, to_parts, to_spread in todo:
        terms = [
            pack.entry(0, part, body, rows) * value[0]
            + pack.entry(1, part, body, rows) * value[1]
            + pack.entry(2, part, body, rows) * value[2]
            for body in range(6)
        ]
        if new_hots:
            lay_hot(index, hot_ref)
        lay_terms(terms, index[rows], wanted, to_parts, to_spread)
        sums = summed(to_spread[pl.ds(0, 16 * len(wanted)), columns], hot_ref[:, columns])
        for group, total in zip(wanted, sums):
            result[group] = result[group] + total if group in result else total
    return [result[group] for group in groups]


def added(lists):
    return [sum(values[1:], values[0]) for values in zip(*lists)]


def joined(sections, spheres, sizes, flags, slot):
    own = [sections[slot][group] for group in range(sizes.own_groups)]
    if sizes.slots > 1:
        below = (slot + sizes.slots - 1) % sizes.slots
        above = [sections[below][group] for group in range(sizes.own_groups, sizes.section_groups)]
        upper = [jnp.where(flags[3 + below] != 0, value, 0.0) for value in above]
        lists = [spheres[slot].layer_list(group) - 1 for group in range(sizes.layer_groups)]
        own = added([own, put_columns(upper, lists, sizes.own_groups)])
    return own


def rows_of(pack, part, table, index):
    groups = len(table(0))
    halves = []
    for at in range(0, index.shape[0], 8):
        rows = slice(at, at + 8)
        place = places(index[rows], groups)
        totals = [None] * 3
        for body in range(6):
            picked = gather(table(body), place)
            for row in range(3):
                term = pack.entry(row, part, body, rows) * picked
                totals[row] = term if totals[row] is None else totals[row] + term
        halves.append(totals)
    return [jnp.concatenate([half[row] for half in halves], axis=0) for row in range(3)]


def rows_from(ref, slot, start, count):
    def rows(body):
        return [ref[slot, pl.ds(body, 1), pl.ds(start + g * LANES, LANES)] for g in range(count)]

    return rows


def cone_project(impulse_value, cone_friction):
    normal, first, second = impulse_value
    slide_norm = jnp.sqrt(first * first + second * second)
    inside_cone = slide_norm <= cone_friction * normal
    polar_cone = cone_friction * slide_norm <= -normal
    outside_both = jnp.logical_not(jnp.logical_or(inside_cone, polar_cone))
    onto_normal = (cone_friction * slide_norm + normal) / (cone_friction * cone_friction + 1.0)
    tangent_scale = cone_friction * onto_normal / jnp.where(outside_both, slide_norm, 1.0)
    scale = jnp.where(inside_cone, 1.0, jnp.where(polar_cone, 0.0, tangent_scale))
    new_normal = jnp.where(inside_cone, normal, jnp.where(polar_cone, 0.0, onto_normal))
    return [new_normal, scale * first, scale * second]


def call(body, out_shape, operands, scratch=(), space=pltpu.VMEM, room=40, out_space=pltpu.VMEM):
    return pl.pallas_call(
        body,
        out_shape=[
            jax.ShapeDtypeStruct(*shape) if isinstance(shape[0], tuple) else jax.ShapeDtypeStruct(shape, F32)
            for shape in out_shape
        ],
        in_specs=[pl.BlockSpec(memory_space=space)] * len(operands),
        out_specs=[pl.BlockSpec(memory_space=out_space)] * len(out_shape),
        scratch_shapes=list(scratch),
        compiler_params=pltpu.CompilerParams(vmem_limit_bytes=room * 1024 * 1024),
    )(*operands)


def on_device(
    velocity_free,
    inverse_mass,
    jacobian,
    impulses,
    previous_impulses,
    compliance,
    offset,
    friction,
    body_near,
    body_far,
    block_counts,
    layer_send,
    side_send,
):
    slots, cells = lax.axis_size("gz"), lax.axis_size("xy")
    sizes = Sizes(
        jacobian.shape[3], velocity_free.shape[3], layer_send.shape[2], side_send.shape[3], slots, cells
    )
    blocks, window = sizes.blocks, sizes.window
    factors = momentum_factors(ITERS)

    def flags_here():
        layer_at, cell_at = lax.axis_index("gz"), lax.axis_index("xy")
        odd = cell_at % 2
        lower, higher = cell_at > 0, cell_at < cells - 1
        places = [odd, jnp.where(odd == 0, higher, lower), jnp.where(odd == 0, lower, higher)]
        places += [(layer_at + slot) % slots != slots - 1 for slot in range(slots)]
        return [place.astype(I32) for place in places]

    def tiles(array):
        return array.reshape(-1, blocks, LANES)

    def pack_body(*refs):
        inputs, (shared_out, rest_out, sphere_out, *held, out_ref, sphere_ref, semaphores) = refs[:13], refs[13:]
        moves = list(zip([*inputs[:2], *inputs[3:]], held))
        for row in range(3):
            near, far = pl.ds(12 * row, 6), pl.ds(12 * row + 6, 6)
            moves.append((inputs[2].at[far], out_ref.at[pl.ds(6 * row, 6)]))
            moves.append((inputs[2].at[near], out_ref.at[pl.ds(NEAR_PART + 6 * row, 6)]))
        count = len(moves)
        for start, end in ((0, FAR), (FAR, SHARED)):
            moves.append((out_ref.at[pl.ds(start, end - start)], shared_out.at[pl.ds(start, end - start)]))
        for start, end in ((NEAR_PART, NEAR), (NEAR, TILES)):
            rows = pl.ds(start - SHARED, end - start)
            moves.append((out_ref.at[pl.ds(start, end - start)], rest_out.at[rows]))
        moves.append((sphere_ref, sphere_out))
        copies = [pltpu.make_async_copy(*move, semaphores.at[at]) for at, move in enumerate(moves)]
        arrays, jacobians, out = copies[: count - 6], copies[count - 6 : count], copies[count:]
        for copy in [*jacobians, *arrays]:
            copy.start()
        for copy in arrays:
            copy.wait()
        (free_ref, mass_ref, imp_ref, prev_ref, soft_ref, off_ref, fric_ref, near_ref, far_ref,
         layer_ref, side_ref, counts) = held
        lane = lax.broadcasted_iota(I32, (1, LANES), 1)
        rows = [jnp.where(lane < counts[block], 1.0, 0.0) for block in range(blocks)]
        alive = jnp.concatenate(rows, axis=0)
        out_ref[NEAR] = near_ref[0].astype(F32)
        out_ref[FAR] = far_ref[0].astype(F32)
        out_ref[ALIVE] = alive
        out_ref[FRICTION] = fric_ref[0]
        out_ref[SOFTNESS] = soft_ref[0]
        out_ref[OFFSET] = off_ref[0]
        for row in range(3):
            current = alive * imp_ref[row]
            earlier = alive * prev_ref[row]
            out_ref[CURRENT + row] = current
            out_ref[GUESS + row] = alive * (current + factors[0] * (current - earlier))

        gap = jnp.zeros((2, LANES), F32)

        def misc(group, value):
            sphere_ref[:, pl.ds(group * LANES, LANES)] = value

        for group in range(sizes.own_groups):
            lanes = pl.ds(group * LANES, LANES)
            free = [free_ref[body, pl.ds(group, 1), :] for body in range(6)]
            misc(group, jnp.concatenate(free + [gap], axis=0))
            mass = mass_ref[:, lanes]
            linear = jnp.broadcast_to(mass[0:1], (3, LANES))
            angular = jnp.broadcast_to(mass[1:2], (3, LANES))
            misc(sizes.own_groups + group, jnp.concatenate([linear, angular, gap], axis=0))
        for group in range(sizes.layer_groups):
            lanes = pl.ds(group * LANES, LANES)
            rows = jnp.broadcast_to(layer_ref[:, lanes] + 1, (8, LANES))
            misc(sizes.layer_at + group, rows.astype(F32))
        side = side_ref[...] + 1
        if sizes.margin:
            none = jnp.zeros((1, sizes.margin), I32)
            to_lower = jnp.concatenate([none, side[0:1]], axis=1)
            to_higher = jnp.concatenate([side[1:2], none], axis=1)
            side = jnp.concatenate([to_lower, to_higher], axis=0)
        for group in range(sizes.window_groups):
            rows = jnp.concatenate([side[:, group * LANES : (group + 1) * LANES]] * 4, axis=0)
            misc(sizes.side_at + group, rows.astype(F32))
        for copy in jacobians:
            copy.wait()
        for copy in out:
            copy.start()
        for copy in out:
            copy.wait()

    loaded = [
        velocity_free[0, 0].reshape(6, sizes.own_groups, LANES),
        inverse_mass[0, 0],
        tiles(jacobian[0, 0]),
        tiles(impulses[0, 0]),
        tiles(previous_impulses[0, 0]),
        tiles(compliance[0, 0]),
        tiles(offset[0, 0]),
        tiles(friction[0, 0]),
        tiles(body_near[0, 0]),
        tiles(body_far[0, 0]),
        layer_send[0],
        side_send[0, 0],
        block_counts[0, 0],
    ]
    own_shared, own_rest, own_spheres = call(
        pack_body,
        [(SHARED, blocks, LANES), (TILES - SHARED, blocks, LANES), (8, sizes.sphere_groups * LANES)],
        loaded,
        [pltpu.VMEM(array.shape, array.dtype) for at, array in enumerate(loaded[:-1]) if at != 2]
        + [
            pltpu.SMEM(block_counts.shape[2:], I32),
            pltpu.VMEM((TILES, blocks, LANES), F32),
            pltpu.VMEM((8, sizes.sphere_groups * LANES), F32),
            pltpu.SemaphoreType.DMA((len(loaded) - 1 + 6 + 5,)),
        ],
        pl.ANY,
        62,
        pl.ANY,
    )
    to_first, to_second = pair_swaps(cells, 0), pair_swaps(cells, 1)

    def swap(first, second):
        return lax.ppermute(first, "xy", to_first), lax.ppermute(second, "xy", to_second)

    def turned(array, step):
        return lax.ppermute(array, "gz", [((i + step) % slots, i) for i in range(slots)])

    contact_arrays = [[own_shared, own_rest, *swap(own_shared, own_shared)]]
    above_shared = [turned(own_shared, slot) for slot in range(1, slots)]
    above_rest = [turned(own_rest, slot) for slot in range(1, slots)]

    def three(refs):
        return [Contacts(refs[0], refs[1]), Contacts(refs[2]), Contacts(refs[3])]

    def views(refs):
        sets = [three(refs[4 * s : 4 * s + 4]) for s in range(slots)]
        refs = refs[4 * slots :]
        spheres = [Spheres(ref, sizes, sizes.section_groups) for ref in refs[:slots]]
        refs = refs[slots:]
        hots = [
            [(refs[4 * s + 1 + w], refs[4 * s] if w == 0 else None) for w in range(3)] for s in range(slots)
        ]
        return sets, spheres, hots, refs[4 * slots :]

    def chosen(*arrays):
        return [array for array in arrays if array is not None]

    state_shape = (slots, 3, 3, blocks, LANES)
    section_shape, sent_shape = (slots, 8, sizes.section), (slots, sizes.sent_rows, LANES)
    hot_shape = ((LANES, sizes.contacts), BF16)

    def scratch_of(own):
        split = pltpu.VMEM((16 * blocks, LANES), F32)
        spread = [pltpu.VMEM((16 * n, sizes.contacts), BF16) for n in (sizes.section_groups, sizes.own_groups)]
        return [split, spread[0]] + ([split, spread[1]] if own else [])

    work = scratch_of(True) + scratch_of(False) * 2

    def places_of(scratch, slot, which):
        base = (slot % 2) * len(work)
        if which == 0:
            return scratch[base : base + 4]
        return [*scratch[base + 2 + 2 * which : base + 4 + 2 * which], None, None]

    def slot_sections(sets, values, maps, hots, scratch, wanted, section_ref):
        half = blocks // 2 if blocks % 16 == 0 else blocks

        def fill(s, live):
            packs = list(zip(sets[s], values[s], hots[s]))
            terms = [
                set_terms(
                    s, w, pack, value, maps, sizes, hot, places_of(scratch, s, w), wanted[s], live=live
                )
                for w, (pack, value, hot) in enumerate(packs)
            ]
            for group, total in zip(wanted[s], added(terms)):
                section_ref[s, :, pl.ds(group * LANES, LANES)] = total

        for s, groups in enumerate(wanted):
            if not groups:
                continue
            alive = [pack.tile(ALIVE)[half:] for pack in sets[s]]
            if half == blocks:
                fill(s, blocks)
                continue
            more = jnp.max(jnp.maximum(jnp.maximum(alive[0], alive[1]), alive[2])) > 0.0
            pl.when(more)(lambda s=s: fill(s, blocks))
            pl.when(jnp.logical_not(more))(lambda s=s: fill(s, half))
        return [
            {group: section_ref[s, :, pl.ds(group * LANES, LANES)] for group in groups}
            for s, groups in enumerate(wanted)
        ]

    every = list(range(sizes.section_groups))
    held_sections = pltpu.VMEM(section_shape, F32)

    def window_rows(group):
        return pl.ds(3 * blocks + 8 * group, 8)

    def put_velocities(sums, spheres, maps, flags, owns, section_ref, first_ref, second_ref):
        velocity = [
            [spheres[s].free(g) + spheres[s].weight(g) * sums[s][g] for g in range(sizes.own_groups)]
            for s in range(slots)
        ]
        for slot in range(slots):
            table = list(velocity[slot])
            for rows in maps.upper(slot):
                upper = gather(velocity[(slot + 1) % slots], places(rows - 1, sizes.own_groups))
                table.append(jnp.where(flags[3 + slot] != 0, upper, 0.0))
            for group, value in enumerate(table):
                section_ref[slot, :, pl.ds(group * LANES, LANES)] = value
            for which, sent_ref in ((1, first_ref), (2, second_ref)):
                for group, rows in enumerate(maps.side(slot, which)):
                    sent_ref[slot, window_rows(group), :] = gather(table, places(rows - 1, sizes.section_groups))
            pack = owns[slot]
            rows = rows_from(section_ref, slot, 0, sizes.own_groups)
            near = rows_of(pack, 0, rows, pack.tile(NEAR).astype(I32))
            near[0] = near[0] + pack.tile(OFFSET)
            for row in range(3):
                first_ref[slot, pl.ds(row * blocks, blocks), :] = near[row]
                second_ref[slot, pl.ds(row * blocks, blocks), :] = near[row]

    def first_terms():
        def guess_of(pack):
            return [pack.tile(GUESS + row) for row in range(3)]

        def early(own_ref, rest_ref, first_ref, sphere_ref, out_ref, near_hot, far_hot, first_hot, *scratch):
            flags = flags_here()
            maps = Maps([Spheres(sphere_ref, sizes)], sizes, flags)
            sets = [Contacts(own_ref, rest_ref), Contacts(first_ref)]
            hots = [(far_hot, near_hot), (first_hot, None)]
            sums = added(
                [
                    set_terms(
                        0, w, sets[w], guess_of(sets[w]), maps, sizes, hots[w], places_of(scratch, 0, w),
                        every, True,
                    )
                    for w in range(2)
                ]
            )
            for group, value in enumerate(sums):
                out_ref[:, pl.ds(group * LANES, LANES)] = value

        def late(part_ref, second_ref, sphere_ref, out_ref, hot_ref, *scratch):
            flags = flags_here()
            maps = Maps([Spheres(sphere_ref, sizes)], sizes, flags)
            pack = Contacts(second_ref)
            sums = set_terms(
                0, 2, pack, guess_of(pack), maps, sizes, (hot_ref, None), [*scratch, None, None], every, True
            )
            for group, value in enumerate(sums):
                lanes = pl.ds(group * LANES, LANES)
                out_ref[:, lanes] = part_ref[:, lanes] + value
            out_ref[:, pl.ds(sizes.section, sizes.sphere_groups * LANES)] = sphere_ref[...]

        own, rest, first, second = contact_arrays[0]
        part, near_hot, far_hot, first_hot = call(
            early, [(8, sizes.section), hot_shape, hot_shape, hot_shape], [own, rest, first, own_spheres], work[:6]
        )
        part, *others = lax.optimization_barrier((part, *above_shared))
        for held, held_rest in zip(others, above_rest):
            contact_arrays.append([held, held_rest, *swap(held, held)])
        mail, second_hot = call(
            late,
            [(8, sizes.mail_groups * LANES), hot_shape],
            [part, second, own_spheres],
            work[4:6],
        )
        return mail, [near_hot, far_hot, first_hot, second_hot]

    def one_hots(slot, mail):
        def body(own_ref, rest_ref, first_ref, second_ref, mail_ref, near_hot, *hot_refs):
            flags = flags_here()
            spheres = {slot: Spheres(mail_ref, sizes, sizes.section_groups)}
            maps = Maps(spheres, sizes, flags)
            packs = three([own_ref, rest_ref, first_ref, second_ref])
            lay_hot(packs[0].tile(NEAR).astype(I32), near_hot)
            for which, pack in enumerate(packs):
                lay_hot(maps.section_row(slot, which, pack.tile(FAR).astype(I32)), hot_refs[which])

        return call(body, [hot_shape] * 4, [*contact_arrays[slot], mail])

    mail, hots = first_terms()
    mails = [mail] + [turned(mail, step) for step in range(1, slots)]
    for slot in range(1, slots):
        hots = [*hots, *one_hots(slot, mails[slot])]
    inputs = [*sum(contact_arrays, []), *mails, *hots]

    def first_velocities():
        def body(*refs):
            flags = flags_here()
            mail_refs, own_refs, refs = refs[:slots], refs[slots : 3 * slots], refs[3 * slots :]
            spheres = [Spheres(ref, sizes, sizes.section_groups) for ref in mail_refs]
            owns = [Contacts(*own_refs[2 * slot : 2 * slot + 2]) for slot in range(slots)]
            maps = Maps(spheres, sizes, flags)
            sections = [[ref[:, pl.ds(group * LANES, LANES)] for group in every] for ref in mail_refs]
            sums = [joined(sections, spheres, sizes, flags, slot) for slot in range(slots)]
            put_velocities(sums, spheres, maps, flags, owns, *refs)

        arrays = [array for held in contact_arrays for array in held[:2]]
        return call(body, [section_shape, sent_shape, sent_shape], [*mails, *arrays])

    def gradients(section, sent, got, state):
        def body(section_ref, sent_first, sent_second, got_first, got_second, *refs):
            flags = flags_here()
            sets, spheres, hots, refs = views(refs)
            if state is None:
                state_ref = None
            else:
                state_ref, *refs = refs
            grad_ref, parts_ref, table_ref, *scratch = refs
            maps = Maps(spheres, sizes, flags)
            even = flags[0] == 0
            norm = soft = jnp.zeros((blocks, LANES), F32)
            lane = lax.broadcasted_iota(I32, (8, LANES), 1)
            edge = sizes.side % LANES

            values = []
            for slot in range(slots):
                low, high = [], []
                for group in range(sizes.window_groups):
                    first = jnp.where(flags[1] != 0, got_first[slot, window_rows(group), :], 0.0)
                    second = jnp.where(flags[2] != 0, got_second[slot, window_rows(group), :], 0.0)
                    low.append(jnp.where(even, second, first))
                    high.append(jnp.where(even, first, second))
                if edge:
                    extended = low[:-1] + [jnp.where(lane < edge, low[-1], high[0])] + high[1:]
                else:
                    extended = low + high
                table_ref[slot, :, pl.ds(0, sizes.section)] = section_ref[slot]
                for group, value in enumerate(extended):
                    table_ref[slot, :, pl.ds(sizes.section + group * LANES, LANES)] = value
                slot_values = []
                for which, pack in enumerate(sets[slot]):
                    far = pack.tile(FAR).astype(I32)
                    if which == 0:
                        near_ref = sent_first
                        table = rows_from(table_ref, slot, 0, sizes.total_groups)
                    else:
                        near_ref = (got_first, got_second)[which - 1]
                        listed = (sent_first, sent_second)[which - 1]
                        far = maps.window_index(far, which)

                        def table(body, listed=listed):
                            rows = [pl.ds(3 * blocks + 8 * g + body, 1) for g in range(sizes.window_groups)]
                            return [listed[slot, row, :] for row in rows]

                    contact_rows = rows_of(pack, 1, table, far)
                    alive, softness = pack.tile(ALIVE), pack.tile(SOFTNESS)
                    grad = []
                    for row in range(3):
                        guess = pack.tile(GUESS + row) if state_ref is None else state_ref[slot, which, row]
                        near = near_ref[slot, pl.ds(row * blocks, blocks), :]
                        value = alive * (near + contact_rows[row] + softness * guess)
                        grad_ref[slot, which, row] = value
                        grad.append(value)
                        if which == 0:
                            norm = norm + value * value
                            soft = soft + softness * value * value
                    slot_values.append(grad)
                values.append(slot_values)
            sections = slot_sections(sets, values, maps, hots, scratch[1:], [every] * slots, scratch[0])
            sums = [joined(sections, spheres, sizes, flags, slot) for slot in range(slots)]
            curve = jnp.sum(soft, axis=0, keepdims=True)
            norm = jnp.sum(norm, axis=0, keepdims=True)
            total = jnp.zeros((8, LANES), F32)
            for slot in range(slots):
                for group in range(sizes.own_groups):
                    value = sums[slot][group]
                    total = total + spheres[slot].weight(group) * value * value
            curve = curve + jnp.sum(total, axis=0, keepdims=True)
            half = LANES // 2
            norm = norm + pltpu.roll(norm, half, 1)
            curve = curve + pltpu.roll(curve, half, 1)
            both = jnp.where(lax.broadcasted_iota(I32, (1, LANES), 1) < half, norm, curve)
            for cell in range(cells):
                parts_ref[cell] = both

        return call(
            body,
            [state_shape, (cells, 1, LANES)],
            chosen(section, *sent, *got, *inputs, state),
            [pltpu.VMEM((slots, 8, sizes.total_groups * LANES), F32), held_sections, *work, *work],
        )

    def updates(parts, grad, state, earlier, factor):
        last = factor is None

        def body(part_ref, grad_ref, *refs):
            flags = flags_here()
            sets, spheres, hots, refs = views(refs)
            if state is not None:
                state_ref, earlier_ref, *refs = refs
            if last:
                result_ref, velocity_ref, *scratch = refs
            else:
                result_ref, guess_ref, section_ref, first_ref, second_ref, *scratch = refs
            maps = Maps(spheres, sizes, flags)
            total = part_ref[0]
            for cell in range(1, cells):
                total = total + part_ref[cell]
            lane = lax.broadcasted_iota(I32, (1, LANES), 1)
            norm = jnp.sum(jnp.where(lane < LANES // 2, total, 0.0), axis=1, keepdims=True)
            curve = jnp.sum(jnp.where(lane < LANES // 2, 0.0, total), axis=1, keepdims=True)
            step = norm / (curve + EPSILON)
            values = []
            for slot in range(slots):
                slot_values = []
                for which, pack in enumerate(sets[slot]):
                    alive = pack.tile(ALIVE)
                    moved, before = [], []
                    for row in range(3):
                        if state is None:
                            guess, old = pack.tile(GUESS + row), pack.tile(CURRENT + row)
                        else:
                            guess, old = state_ref[slot, which, row], earlier_ref[slot, which, row]
                        before.append(old)
                        moved.append(guess - step * grad_ref[slot, which, row])
                    value = [alive * v for v in cone_project(moved, pack.tile(FRICTION))]
                    if not last:
                        guess = [alive * (v + factor * (v - b)) for v, b in zip(value, before)]
                        for row in range(3):
                            result_ref[slot, which, row] = value[row]
                            guess_ref[slot, which, row] = guess[row]
                        value = guess
                    elif slot == which == 0:
                        for row in range(3):
                            result_ref[row] = value[row]
                    slot_values.append(value)
                values.append(slot_values)
            wanted = [every] * slots
            if last:
                wanted = [[] for _ in range(slots)]
                wanted[-1] = every[sizes.own_groups :]
                wanted[0] = every[: sizes.own_groups]
            sections = slot_sections(sets, values, maps, hots, scratch[1:], wanted, scratch[0])
            if last:
                total = joined(sections, spheres, sizes, flags, 0)
                for group in range(sizes.own_groups):
                    value = spheres[0].free(group) + spheres[0].weight(group) * total[group]
                    for body_row in range(6):
                        velocity_ref[body_row, pl.ds(group, 1), :] = value[body_row : body_row + 1]
            else:
                sums = [joined(sections, spheres, sizes, flags, slot) for slot in range(slots)]
                owns = [sets[slot][0] for slot in range(slots)]
                put_velocities(sums, spheres, maps, flags, owns, section_ref, first_ref, second_ref)

        if last:
            shapes = [(3, blocks, LANES), (6, sizes.own_groups, LANES)]
        else:
            shapes = [state_shape, state_shape, section_shape, sent_shape, sent_shape]
        return call(body, shapes, chosen(parts, grad, *inputs, state, earlier), [held_sections, *work, *work])

    state = earlier = None
    section, *sent = first_velocities()
    for iteration in range(ITERS):
        grad, parts = gradients(section, sent, swap(*sent), state)
        parts = lax.all_to_all(parts, "xy", 0, 0, tiled=True)
        if iteration + 1 < ITERS:
            earlier, state, section, *sent = updates(parts, grad, state, earlier, factors[iteration + 1])
    result, velocity = updates(parts, grad, state, earlier, None)
    return (
        result.reshape(1, 1, 3, sizes.contacts),
        velocity.reshape(1, 1, 6, sizes.own),
    )


def solution(mesh):
    placed = (
        P("gz", "xy", None, None),
        P("gz", "xy", None, None),
        P("gz", "xy", None, None),
        P("gz", "xy", None, None),
        P("gz", "xy", None, None),
        P("gz", "xy", None),
        P("gz", "xy", None),
        P("gz", "xy", None),
        P("gz", "xy", None),
        P("gz", "xy", None),
        P("gz", "xy", None),
        P("gz", "xy", None),
        P("gz", "xy", None, None),
    )
    return jax.shard_map(
        on_device,
        mesh=mesh,
        in_specs=placed,
        out_specs=(P("gz", "xy", None, None), P("gz", "xy", None, None)),
        check_vma=False,
    )
```

```python
import math

import jax
import jax.numpy as jnp
from jax import lax
from jax.experimental import pallas as pl
from jax.experimental.pallas import tpu as pltpu
from jax.sharding import PartitionSpec as P

ITERS = 2
EPSILON = 1e-06
THETA_START = 0.3
LANES = 128
WIDE = 256
F32 = jnp.float32
BF16 = jnp.bfloat16
I32 = jnp.int32


def theta_after(theta_value):
    return 0.5 * (
        -theta_value * theta_value + theta_value * math.sqrt(theta_value * theta_value + 4.0)
    )


def momentum_factors(iteration_count):
    thetas = [THETA_START]
    for iteration in range(iteration_count):
        thetas.append(theta_after(thetas[-1]))
    return [
        thetas[position]
        * (1.0 - thetas[position])
        / (thetas[position] * thetas[position] + thetas[position + 1])
        for position in range(iteration_count)
    ]


def pair_swaps(count, parity):
    target = list(range(count))
    for cell in range(parity, count - 1, 2):
        target[cell], target[cell + 1] = cell + 1, cell
    return list(enumerate(target))


class Sizes:
    def __init__(self, contacts, own, layer, side, slots, cells):
        self.contacts, self.own, self.layer, self.side = contacts, own, layer, side
        self.slots, self.cells = slots, cells
        self.blocks = contacts // LANES
        self.section = own + layer
        self.window = -(-side // LANES) * LANES
        self.margin = self.window - side
        self.own_groups = own // LANES
        self.layer_groups = layer // LANES
        self.section_groups = self.section // LANES
        self.total_groups = (self.section + 2 * side) // LANES
        self.window_groups = self.window // LANES
        self.layer_at = 2 * self.own_groups
        self.side_at = self.layer_at + self.layer_groups
        self.sphere_groups = self.side_at + self.window_groups
        self.mail_groups = self.section_groups + self.sphere_groups
        self.sent_rows = 3 * self.blocks + 8 * self.window_groups
        assert contacts % LANES == own % LANES == layer % LANES == 2 * side % LANES == 0
        assert self.blocks % 8 == 0


FAR, ALIVE, FRICTION, SOFTNESS, CURRENT, GUESS, NEAR_PART, NEAR, OFFSET = 18, 19, 20, 21, 22, 25, 28, 46, 47
SHARED, TILES = 28, 48


class Contacts:
    def __init__(self, ref, rest_ref=None):
        self.ref, self.rest_ref = ref, rest_ref

    def tile(self, which):
        return self.ref[which] if which < SHARED else self.rest_ref[which - SHARED]

    def entry(self, row, part, body, rows=slice(None)):
        return (self.ref if part else self.rest_ref)[6 * row + body, rows, :]


class Spheres:
    def __init__(self, ref, sizes, start=0):
        self.ref, self.sizes, self.start = ref, sizes, start

    def misc(self, group):
        return self.ref[:, pl.ds((self.start + group) * LANES, LANES)]

    def free(self, group):
        return self.misc(group)

    def weight(self, group):
        return self.misc(self.sizes.own_groups + group)

    def layer_list(self, group):
        return self.misc(self.sizes.layer_at + group)[0:1].astype(I32)

    def side_list(self, which, group):
        return self.misc(self.sizes.side_at + group)[which : which + 1].astype(I32)


def places(index, groups):
    index = jnp.broadcast_to(index, (8, LANES))
    which = index >> 7
    return index & (LANES - 1), [which == number for number in range(groups)]


def gather(groups, place):
    lane, inside = place
    out = jnp.zeros((8, LANES), groups[0].dtype)
    for group, here in zip(groups, inside):
        group = jnp.broadcast_to(group, (8, LANES))
        out = jnp.where(here, jnp.take_along_axis(group, lane, axis=1, mode="promise_in_bounds"), out)
    return out


def look_up(lists, index):
    pieces = [
        gather(lists, places(index[at : at + 8], len(lists))) for at in range(0, index.shape[0], 8)
    ]
    return jnp.concatenate(pieces, axis=0) - 1


def lay_hot(index, hot_ref):
    lane_of = (index & (LANES - 1)).astype(F32)
    row_number = lax.broadcasted_iota(I32, (LANES, LANES), 0).astype(F32).astype(BF16)
    zeros, ones = jnp.zeros((16, LANES), BF16), jnp.ones((16, LANES), BF16)
    for block in range(index.shape[0]):
        low = jnp.broadcast_to(lane_of[block : block + 1], (16, LANES)).astype(BF16)
        for piece in range(LANES // 16):
            rows = slice(piece * 16, piece * 16 + 16)
            hot = jnp.where(row_number[rows] == low, ones, zeros)
            hot_ref[pl.ds(piece * 16, 16), pl.ds(block * LANES, LANES)] = hot


def lay_terms(terms, index, groups, parts_ref, spread_ref):
    blocks = terms[0].shape[0]
    for body, term in enumerate(terms):
        upper = term.astype(BF16).astype(F32)
        parts_ref[pl.ds(body * blocks, blocks), :] = upper
        parts_ref[pl.ds((8 + body) * blocks, blocks), :] = term - upper
    gap = jnp.zeros((2 * blocks, LANES), F32)
    parts_ref[pl.ds(6 * blocks, 2 * blocks), :] = gap
    parts_ref[pl.ds(14 * blocks, 2 * blocks), :] = gap
    group_of = (index >> 7).astype(F32)
    zeros = jnp.zeros((16, LANES), BF16)
    for block in range(blocks):
        both = parts_ref[pl.ds(block, 16, stride=blocks), :].astype(BF16)
        which = jnp.broadcast_to(group_of[block : block + 1], (16, LANES)).astype(BF16)
        for at, number in enumerate(groups):
            part = jnp.where(which == jnp.asarray(number, BF16), both, zeros)
            spread_ref[pl.ds(at * 16, 16), pl.ds(block * LANES, LANES)] = part


def summed(spread, hot):
    out = lax.dot_general(spread, hot, (((1,), (1,)), ((), ())), preferred_element_type=F32)
    return [out[at : at + 8] + out[at + 8 : at + 16] for at in range(0, out.shape[0], 16)]


def put_columns(values, lists, groups):
    result = [jnp.zeros((8, LANES), F32)] * groups
    row_number = lax.broadcasted_iota(I32, (LANES, LANES), 0)
    for value, index in zip(values, lists):
        upper = value.astype(BF16).astype(F32)
        both = jnp.concatenate([upper, value - upper], axis=0)
        which = jnp.broadcast_to(index >> 7, (16, LANES))
        spread = jnp.concatenate([jnp.where(which == g, both, 0.0) for g in range(groups)], axis=0)
        low = jnp.broadcast_to(index & (LANES - 1), (LANES, LANES))
        hot = jnp.where(row_number == low, 1.0, 0.0).astype(BF16)
        result = [a + b for a, b in zip(result, summed(spread.astype(BF16), hot))]
    return result


class Maps:
    def __init__(self, spheres, sizes, flags):
        self.spheres, self.sizes, self.flags = spheres, sizes, flags

    def upper(self, slot):
        above = self.spheres[(slot + 1) % self.sizes.slots]
        return [above.layer_list(group) for group in range(self.sizes.layer_groups)]

    def side(self, slot, which):
        picks = []
        for group in range(self.sizes.window_groups):
            to_lower = self.spheres[slot].side_list(0, group)
            to_higher = self.spheres[slot].side_list(1, group)
            higher = (self.flags[0] == 0) == (which == 1)
            picks.append(jnp.where(higher, to_higher, to_lower))
        return picks

    def window_index(self, far, which):
        sizes = self.sizes
        higher = (self.flags[0] == 0) == (which == 1)
        return far - jnp.where(higher, sizes.section, sizes.section + sizes.side - sizes.margin)

    def section_row(self, slot, which, far):
        if which == 0:
            return jnp.where(far < self.sizes.section, far, -1)
        row = look_up(self.side(slot, which), self.window_index(far, which))
        return jnp.where(self.flags[which] != 0, row, -1)


def set_terms(slot, which, pack, value, maps, sizes, hots, scratch, groups, new_hots=False, live=None):
    rows = slice(0, live)
    columns = pl.ds(0, (live or sizes.blocks) * LANES)
    value = [v[rows] for v in value]
    far_hot, near_hot = hots
    parts_ref, spread_ref, near_parts, near_spread = scratch
    far = maps.section_row(slot, which, pack.tile(FAR).astype(I32))
    own = [group for group in groups if group < sizes.own_groups] if which == 0 else []
    todo = [(1, far, groups, far_hot, parts_ref, spread_ref)]
    if own:
        todo.append((0, pack.tile(NEAR).astype(I32), own, near_hot, near_parts, near_spread))
    result = {}
    for part, index, wanted, hot_ref, to_parts, to_spread in todo:
        terms = [
            pack.entry(0, part, body, rows) * value[0]
            + pack.entry(1, part, body, rows) * value[1]
            + pack.entry(2, part, body, rows) * value[2]
            for body in range(6)
        ]
        if new_hots:
            lay_hot(index, hot_ref)
        lay_terms(terms, index[rows], wanted, to_parts, to_spread)
        sums = summed(to_spread[pl.ds(0, 16 * len(wanted)), columns], hot_ref[:, columns])
        for group, total in zip(wanted, sums):
            result[group] = result[group] + total if group in result else total
    return [result[group] for group in groups]


def added(lists):
    return [sum(values[1:], values[0]) for values in zip(*lists)]


def joined(sections, spheres, sizes, flags, slot):
    own = [sections[slot][group] for group in range(sizes.own_groups)]
    if sizes.slots > 1:
        below = (slot + sizes.slots - 1) % sizes.slots
        above = [sections[below][group] for group in range(sizes.own_groups, sizes.section_groups)]
        upper = [jnp.where(flags[3 + below] != 0, value, 0.0) for value in above]
        lists = [spheres[slot].layer_list(group) - 1 for group in range(sizes.layer_groups)]
        own = added([own, put_columns(upper, lists, sizes.own_groups)])
    return own


def rows_of(pack, part, table, index):
    groups = len(table(0))
    halves = []
    for at in range(0, index.shape[0], 8):
        rows = slice(at, at + 8)
        place = places(index[rows], groups)
        totals = [None] * 3
        for body in range(6):
            picked = gather(table(body), place)
            for row in range(3):
                term = pack.entry(row, part, body, rows) * picked
                totals[row] = term if totals[row] is None else totals[row] + term
        halves.append(totals)
    return [jnp.concatenate([half[row] for half in halves], axis=0) for row in range(3)]


def rows_from(ref, slot, start, count):
    def rows(body):
        return [ref[slot, pl.ds(body, 1), pl.ds(start + g * LANES, LANES)] for g in range(count)]

    return rows


def cone_project(impulse_value, cone_friction):
    normal, first, second = impulse_value
    slide_norm = jnp.sqrt(first * first + second * second)
    inside_cone = slide_norm <= cone_friction * normal
    polar_cone = cone_friction * slide_norm <= -normal
    outside_both = jnp.logical_not(jnp.logical_or(inside_cone, polar_cone))
    onto_normal = (cone_friction * slide_norm + normal) / (cone_friction * cone_friction + 1.0)
    tangent_scale = cone_friction * onto_normal / jnp.where(outside_both, slide_norm, 1.0)
    scale = jnp.where(inside_cone, 1.0, jnp.where(polar_cone, 0.0, tangent_scale))
    new_normal = jnp.where(inside_cone, normal, jnp.where(polar_cone, 0.0, onto_normal))
    return [new_normal, scale * first, scale * second]


def call(body, out_shape, operands, scratch=(), space=pltpu.VMEM, room=40, out_space=pltpu.VMEM):
    return pl.pallas_call(
        body,
        out_shape=[
            jax.ShapeDtypeStruct(*shape) if isinstance(shape[0], tuple) else jax.ShapeDtypeStruct(shape, F32)
            for shape in out_shape
        ],
        in_specs=[pl.BlockSpec(memory_space=space)] * len(operands),
        out_specs=[pl.BlockSpec(memory_space=out_space)] * len(out_shape),
        scratch_shapes=list(scratch),
        compiler_params=pltpu.CompilerParams(vmem_limit_bytes=room * 1024 * 1024),
    )(*operands)


def on_device(
    velocity_free,
    inverse_mass,
    jacobian,
    impulses,
    previous_impulses,
    compliance,
    offset,
    friction,
    body_near,
    body_far,
    block_counts,
    layer_send,
    side_send,
):
    slots, cells = lax.axis_size("gz"), lax.axis_size("xy")
    sizes = Sizes(
        jacobian.shape[3], velocity_free.shape[3], layer_send.shape[2], side_send.shape[3], slots, cells
    )
    blocks, window = sizes.blocks, sizes.window
    factors = momentum_factors(ITERS)

    def flags_here():
        layer_at, cell_at = lax.axis_index("gz"), lax.axis_index("xy")
        odd = cell_at % 2
        lower, higher = cell_at > 0, cell_at < cells - 1
        places = [odd, jnp.where(odd == 0, higher, lower), jnp.where(odd == 0, lower, higher)]
        places += [(layer_at + slot) % slots != slots - 1 for slot in range(slots)]
        return [place.astype(I32) for place in places]

    def tiles(array):
        return array.reshape(-1, blocks, LANES)

    def pack_body(*refs):
        inputs, (shared_out, rest_out, sphere_out, *held, out_ref, sphere_ref, semaphores) = refs[:13], refs[13:]
        moves = list(zip([*inputs[:2], *inputs[3:]], held))
        for row in range(3):
            near, far = pl.ds(12 * row, 6), pl.ds(12 * row + 6, 6)
            moves.append((inputs[2].at[far], out_ref.at[pl.ds(6 * row, 6)]))
            moves.append((inputs[2].at[near], out_ref.at[pl.ds(NEAR_PART + 6 * row, 6)]))
        count = len(moves)
        for start, end in ((0, FAR), (FAR, SHARED)):
            moves.append((out_ref.at[pl.ds(start, end - start)], shared_out.at[pl.ds(start, end - start)]))
        for start, end in ((NEAR_PART, NEAR), (NEAR, TILES)):
            rows = pl.ds(start - SHARED, end - start)
            moves.append((out_ref.at[pl.ds(start, end - start)], rest_out.at[rows]))
        moves.append((sphere_ref, sphere_out))
        copies = [pltpu.make_async_copy(*move, semaphores.at[at]) for at, move in enumerate(moves)]
        arrays, jacobians, out = copies[: count - 6], copies[count - 6 : count], copies[count:]
        for copy in [*jacobians, *arrays]:
            copy.start()
        for copy in arrays:
            copy.wait()
        (free_ref, mass_ref, imp_ref, prev_ref, soft_ref, off_ref, fric_ref, near_ref, far_ref,
         layer_ref, side_ref, counts) = held
        lane = lax.broadcasted_iota(I32, (1, LANES), 1)
        rows = [jnp.where(lane < counts[block], 1.0, 0.0) for block in range(blocks)]
        alive = jnp.concatenate(rows, axis=0)
        out_ref[NEAR] = near_ref[0].astype(F32)
        out_ref[FAR] = far_ref[0].astype(F32)
        out_ref[ALIVE] = alive
        out_ref[FRICTION] = fric_ref[0]
        out_ref[SOFTNESS] = soft_ref[0]
        out_ref[OFFSET] = off_ref[0]
        for row in range(3):
            current = alive * imp_ref[row]
            earlier = alive * prev_ref[row]
            out_ref[CURRENT + row] = current
            out_ref[GUESS + row] = alive * (current + factors[0] * (current - earlier))

        gap = jnp.zeros((2, LANES), F32)

        def misc(group, value):
            sphere_ref[:, pl.ds(group * LANES, LANES)] = value

        for group in range(sizes.own_groups):
            lanes = pl.ds(group * LANES, LANES)
            free = [free_ref[body, pl.ds(group, 1), :] for body in range(6)]
            misc(group, jnp.concatenate(free + [gap], axis=0))
            mass = mass_ref[:, lanes]
            linear = jnp.broadcast_to(mass[0:1], (3, LANES))
            angular = jnp.broadcast_to(mass[1:2], (3, LANES))
            misc(sizes.own_groups + group, jnp.concatenate([linear, angular, gap], axis=0))
        for group in range(sizes.layer_groups):
            lanes = pl.ds(group * LANES, LANES)
            rows = jnp.broadcast_to(layer_ref[:, lanes] + 1, (8, LANES))
            misc(sizes.layer_at + group, rows.astype(F32))
        side = side_ref[...] + 1
        if sizes.margin:
            none = jnp.zeros((1, sizes.margin), I32)
            to_lower = jnp.concatenate([none, side[0:1]], axis=1)
            to_higher = jnp.concatenate([side[1:2], none], axis=1)
            side = jnp.concatenate([to_lower, to_higher], axis=0)
        for group in range(sizes.window_groups):
            rows = jnp.concatenate([side[:, group * LANES : (group + 1) * LANES]] * 4, axis=0)
            misc(sizes.side_at + group, rows.astype(F32))
        for copy in jacobians:
            copy.wait()
        for copy in out:
            copy.start()
        for copy in out:
            copy.wait()

    loaded = [
        velocity_free[0, 0].reshape(6, sizes.own_groups, LANES),
        inverse_mass[0, 0],
        tiles(jacobian[0, 0]),
        tiles(impulses[0, 0]),
        tiles(previous_impulses[0, 0]),
        tiles(compliance[0, 0]),
        tiles(offset[0, 0]),
        tiles(friction[0, 0]),
        tiles(body_near[0, 0]),
        tiles(body_far[0, 0]),
        layer_send[0],
        side_send[0, 0],
        block_counts[0, 0],
    ]
    own_shared, own_rest, own_spheres = call(
        pack_body,
        [(SHARED, blocks, LANES), (TILES - SHARED, blocks, LANES), (8, sizes.sphere_groups * LANES)],
        loaded,
        [pltpu.VMEM(array.shape, array.dtype) for at, array in enumerate(loaded[:-1]) if at != 2]
        + [
            pltpu.SMEM(block_counts.shape[2:], I32),
            pltpu.VMEM((TILES, blocks, LANES), F32),
            pltpu.VMEM((8, sizes.sphere_groups * LANES), F32),
            pltpu.SemaphoreType.DMA((len(loaded) - 1 + 6 + 5,)),
        ],
        pl.ANY,
        62,
        pl.ANY,
    )
    to_first, to_second = pair_swaps(cells, 0), pair_swaps(cells, 1)

    def swap(first, second):
        return lax.ppermute(first, "xy", to_first), lax.ppermute(second, "xy", to_second)

    def turned(array, step):
        return lax.ppermute(array, "gz", [((i + step) % slots, i) for i in range(slots)])

    contact_arrays = [[own_shared, own_rest, *swap(own_shared, own_shared)]]
    above_shared = [turned(own_shared, slot) for slot in range(1, slots)]
    above_rest = [turned(own_rest, slot) for slot in range(1, slots)]

    def three(refs):
        return [Contacts(refs[0], refs[1]), Contacts(refs[2]), Contacts(refs[3])]

    def views(refs):
        sets = [three(refs[4 * s : 4 * s + 4]) for s in range(slots)]
        refs = refs[4 * slots :]
        spheres = [Spheres(ref, sizes, sizes.section_groups) for ref in refs[:slots]]
        refs = refs[slots:]
        hots = [
            [(refs[4 * s + 1 + w], refs[4 * s] if w == 0 else None) for w in range(3)] for s in range(slots)
        ]
        return sets, spheres, hots, refs[4 * slots :]

    def chosen(*arrays):
        return [array for array in arrays if array is not None]

    state_shape = (slots, 3, 3, blocks, LANES)
    section_shape, sent_shape = (slots, 8, sizes.section), (slots, sizes.sent_rows, LANES)
    hot_shape = ((LANES, sizes.contacts), BF16)

    def scratch_of(own):
        split = pltpu.VMEM((16 * blocks, LANES), F32)
        spread = [pltpu.VMEM((16 * n, sizes.contacts), BF16) for n in (sizes.section_groups, sizes.own_groups)]
        return [split, spread[0]] + ([split, spread[1]] if own else [])

    work = scratch_of(True) + scratch_of(False) * 2

    def places_of(scratch, slot, which):
        base = (slot % 2) * len(work)
        if which == 0:
            return scratch[base : base + 4]
        return [*scratch[base + 2 + 2 * which : base + 4 + 2 * which], None, None]

    def slot_sections(sets, values, maps, hots, scratch, wanted, section_ref):
        half = blocks // 2 if blocks % 16 == 0 else blocks

        def fill(s, live):
            packs = list(zip(sets[s], values[s], hots[s]))
            terms = [
                set_terms(
                    s, w, pack, value, maps, sizes, hot, places_of(scratch, s, w), wanted[s], live=live
                )
                for w, (pack, value, hot) in enumerate(packs)
            ]
            for group, total in zip(wanted[s], added(terms)):
                section_ref[s, :, pl.ds(group * LANES, LANES)] = total

        for s, groups in enumerate(wanted):
            if not groups:
                continue
            alive = [pack.tile(ALIVE)[half:] for pack in sets[s]]
            if half == blocks:
                fill(s, blocks)
                continue
            more = jnp.max(jnp.maximum(jnp.maximum(alive[0], alive[1]), alive[2])) > 0.0
            pl.when(more)(lambda s=s: fill(s, blocks))
            pl.when(jnp.logical_not(more))(lambda s=s: fill(s, half))
        return [
            {group: section_ref[s, :, pl.ds(group * LANES, LANES)] for group in groups}
            for s, groups in enumerate(wanted)
        ]

    every = list(range(sizes.section_groups))
    held_sections = pltpu.VMEM(section_shape, F32)

    def window_rows(group):
        return pl.ds(3 * blocks + 8 * group, 8)

    def put_velocities(sums, spheres, maps, flags, owns, section_ref, first_ref, second_ref):
        velocity = [
            [spheres[s].free(g) + spheres[s].weight(g) * sums[s][g] for g in range(sizes.own_groups)]
            for s in range(slots)
        ]
        for slot in range(slots):
            table = list(velocity[slot])
            for rows in maps.upper(slot):
                upper = gather(velocity[(slot + 1) % slots], places(rows - 1, sizes.own_groups))
                table.append(jnp.where(flags[3 + slot] != 0, upper, 0.0))
            for group, value in enumerate(table):
                section_ref[slot, :, pl.ds(group * LANES, LANES)] = value
            for which, sent_ref in ((1, first_ref), (2, second_ref)):
                for group, rows in enumerate(maps.side(slot, which)):
                    sent_ref[slot, window_rows(group), :] = gather(table, places(rows - 1, sizes.section_groups))
            pack = owns[slot]
            rows = rows_from(section_ref, slot, 0, sizes.own_groups)
            near = rows_of(pack, 0, rows, pack.tile(NEAR).astype(I32))
            near[0] = near[0] + pack.tile(OFFSET)
            for row in range(3):
                first_ref[slot, pl.ds(row * blocks, blocks), :] = near[row]
                second_ref[slot, pl.ds(row * blocks, blocks), :] = near[row]

    def first_terms():
        def guess_of(pack):
            return [pack.tile(GUESS + row) for row in range(3)]

        def early(own_ref, rest_ref, first_ref, sphere_ref, out_ref, near_hot, far_hot, first_hot, *scratch):
            flags = flags_here()
            maps = Maps([Spheres(sphere_ref, sizes)], sizes, flags)
            sets = [Contacts(own_ref, rest_ref), Contacts(first_ref)]
            hots = [(far_hot, near_hot), (first_hot, None)]
            sums = added(
                [
                    set_terms(
                        0, w, sets[w], guess_of(sets[w]), maps, sizes, hots[w], places_of(scratch, 0, w),
                        every, True,
                    )
                    for w in range(2)
                ]
            )
            for group, value in enumerate(sums):
                out_ref[:, pl.ds(group * LANES, LANES)] = value

        def late(part_ref, second_ref, sphere_ref, out_ref, hot_ref, *scratch):
            flags = flags_here()
            maps = Maps([Spheres(sphere_ref, sizes)], sizes, flags)
            pack = Contacts(second_ref)
            sums = set_terms(
                0, 2, pack, guess_of(pack), maps, sizes, (hot_ref, None), [*scratch, None, None], every, True
            )
            for group, value in enumerate(sums):
                lanes = pl.ds(group * LANES, LANES)
                out_ref[:, lanes] = part_ref[:, lanes] + value
            out_ref[:, pl.ds(sizes.section, sizes.sphere_groups * LANES)] = sphere_ref[...]

        own, rest, first, second = contact_arrays[0]
        part, near_hot, far_hot, first_hot = call(
            early, [(8, sizes.section), hot_shape, hot_shape, hot_shape], [own, rest, first, own_spheres], work[:6]
        )
        part, *others = lax.optimization_barrier((part, *above_shared))
        seconds = [lax.ppermute(held, "xy", to_second) for held in others]
        mail, second_hot = call(
            late,
            [(8, sizes.mail_groups * LANES), hot_shape],
            [part, second, own_spheres],
            work[4:6],
        )
        mail, *others = lax.optimization_barrier((mail, *others))
        for held, held_rest, got in zip(others, above_rest, seconds):
            contact_arrays.append([held, held_rest, lax.ppermute(held, "xy", to_first), got])
        return mail, [near_hot, far_hot, first_hot, second_hot]

    def one_hots(slot, mail):
        def body(own_ref, rest_ref, first_ref, second_ref, mail_ref, near_hot, *hot_refs):
            flags = flags_here()
            spheres = {slot: Spheres(mail_ref, sizes, sizes.section_groups)}
            maps = Maps(spheres, sizes, flags)
            packs = three([own_ref, rest_ref, first_ref, second_ref])
            lay_hot(packs[0].tile(NEAR).astype(I32), near_hot)
            for which, pack in enumerate(packs):
                lay_hot(maps.section_row(slot, which, pack.tile(FAR).astype(I32)), hot_refs[which])

        return call(body, [hot_shape] * 4, [*contact_arrays[slot], mail])

    mail, hots = first_terms()
    mails = [mail] + [turned(mail, step) for step in range(1, slots)]
    for slot in range(1, slots):
        hots = [*hots, *one_hots(slot, mails[slot])]
    inputs = [*sum(contact_arrays, []), *mails, *hots]

    def first_velocities():
        def body(*refs):
            flags = flags_here()
            mail_refs, own_refs, refs = refs[:slots], refs[slots : 3 * slots], refs[3 * slots :]
            spheres = [Spheres(ref, sizes, sizes.section_groups) for ref in mail_refs]
            owns = [Contacts(*own_refs[2 * slot : 2 * slot + 2]) for slot in range(slots)]
            maps = Maps(spheres, sizes, flags)
            sections = [[ref[:, pl.ds(group * LANES, LANES)] for group in every] for ref in mail_refs]
            sums = [joined(sections, spheres, sizes, flags, slot) for slot in range(slots)]
            put_velocities(sums, spheres, maps, flags, owns, *refs)

        arrays = [array for held in contact_arrays for array in held[:2]]
        return call(body, [section_shape, sent_shape, sent_shape], [*mails, *arrays])

    def gradients(section, sent, got, state):
        def body(section_ref, sent_first, sent_second, got_first, got_second, *refs):
            flags = flags_here()
            sets, spheres, hots, refs = views(refs)
            if state is None:
                state_ref = None
            else:
                state_ref, *refs = refs
            grad_ref, parts_ref, table_ref, *scratch = refs
            maps = Maps(spheres, sizes, flags)
            even = flags[0] == 0
            norm = soft = jnp.zeros((blocks, LANES), F32)
            lane = lax.broadcasted_iota(I32, (8, LANES), 1)
            edge = sizes.side % LANES

            values = []
            for slot in range(slots):
                low, high = [], []
                for group in range(sizes.window_groups):
                    first = jnp.where(flags[1] != 0, got_first[slot, window_rows(group), :], 0.0)
                    second = jnp.where(flags[2] != 0, got_second[slot, window_rows(group), :], 0.0)
                    low.append(jnp.where(even, second, first))
                    high.append(jnp.where(even, first, second))
                if edge:
                    extended = low[:-1] + [jnp.where(lane < edge, low[-1], high[0])] + high[1:]
                else:
                    extended = low + high
                table_ref[slot, :, pl.ds(0, sizes.section)] = section_ref[slot]
                for group, value in enumerate(extended):
                    table_ref[slot, :, pl.ds(sizes.section + group * LANES, LANES)] = value
                slot_values = []
                for which, pack in enumerate(sets[slot]):
                    far = pack.tile(FAR).astype(I32)
                    if which == 0:
                        near_ref = sent_first
                        table = rows_from(table_ref, slot, 0, sizes.total_groups)
                    else:
                        near_ref = (got_first, got_second)[which - 1]
                        listed = (sent_first, sent_second)[which - 1]
                        far = maps.window_index(far, which)

                        def table(body, listed=listed):
                            rows = [pl.ds(3 * blocks + 8 * g + body, 1) for g in range(sizes.window_groups)]
                            return [listed[slot, row, :] for row in rows]

                    contact_rows = rows_of(pack, 1, table, far)
                    alive, softness = pack.tile(ALIVE), pack.tile(SOFTNESS)
                    grad = []
                    for row in range(3):
                        guess = pack.tile(GUESS + row) if state_ref is None else state_ref[slot, which, row]
                        near = near_ref[slot, pl.ds(row * blocks, blocks), :]
                        value = alive * (near + contact_rows[row] + softness * guess)
                        grad_ref[slot, which, row] = value
                        grad.append(value)
                        if which == 0:
                            norm = norm + value * value
                            soft = soft + softness * value * value
                    slot_values.append(grad)
                values.append(slot_values)
            sections = slot_sections(sets, values, maps, hots, scratch[1:], [every] * slots, scratch[0])
            sums = [joined(sections, spheres, sizes, flags, slot) for slot in range(slots)]
            curve = jnp.sum(soft, axis=0, keepdims=True)
            norm = jnp.sum(norm, axis=0, keepdims=True)
            total = jnp.zeros((8, LANES), F32)
            for slot in range(slots):
                for group in range(sizes.own_groups):
                    value = sums[slot][group]
                    total = total + spheres[slot].weight(group) * value * value
            curve = curve + jnp.sum(total, axis=0, keepdims=True)
            half = LANES // 2
            norm = norm + pltpu.roll(norm, half, 1)
            curve = curve + pltpu.roll(curve, half, 1)
            both = jnp.where(lax.broadcasted_iota(I32, (1, LANES), 1) < half, norm, curve)
            for cell in range(cells):
                parts_ref[cell] = both

        return call(
            body,
            [state_shape, (cells, 1, LANES)],
            chosen(section, *sent, *got, *inputs, state),
            [pltpu.VMEM((slots, 8, sizes.total_groups * LANES), F32), held_sections, *work, *work],
        )

    def updates(parts, grad, state, earlier, factor):
        last = factor is None

        def body(part_ref, grad_ref, *refs):
            flags = flags_here()
            sets, spheres, hots, refs = views(refs)
            if state is not None:
                state_ref, earlier_ref, *refs = refs
            if last:
                result_ref, velocity_ref, *scratch = refs
            else:
                result_ref, guess_ref, section_ref, first_ref, second_ref, *scratch = refs
            maps = Maps(spheres, sizes, flags)
            total = part_ref[0]
            for cell in range(1, cells):
                total = total + part_ref[cell]
            lane = lax.broadcasted_iota(I32, (1, LANES), 1)
            norm = jnp.sum(jnp.where(lane < LANES // 2, total, 0.0), axis=1, keepdims=True)
            curve = jnp.sum(jnp.where(lane < LANES // 2, 0.0, total), axis=1, keepdims=True)
            step = norm / (curve + EPSILON)
            values = []
            for slot in range(slots):
                slot_values = []
                for which, pack in enumerate(sets[slot]):
                    alive = pack.tile(ALIVE)
                    moved, before = [], []
                    for row in range(3):
                        if state is None:
                            guess, old = pack.tile(GUESS + row), pack.tile(CURRENT + row)
                        else:
                            guess, old = state_ref[slot, which, row], earlier_ref[slot, which, row]
                        before.append(old)
                        moved.append(guess - step * grad_ref[slot, which, row])
                    value = [alive * v for v in cone_project(moved, pack.tile(FRICTION))]
                    if not last:
                        guess = [alive * (v + factor * (v - b)) for v, b in zip(value, before)]
                        for row in range(3):
                            result_ref[slot, which, row] = value[row]
                            guess_ref[slot, which, row] = guess[row]
                        value = guess
                    elif slot == which == 0:
                        for row in range(3):
                            result_ref[row] = value[row]
                    slot_values.append(value)
                values.append(slot_values)
            wanted = [every] * slots
            if last:
                wanted = [[] for _ in range(slots)]
                wanted[-1] = every[sizes.own_groups :]
                wanted[0] = every[: sizes.own_groups]
            sections = slot_sections(sets, values, maps, hots, scratch[1:], wanted, scratch[0])
            if last:
                total = joined(sections, spheres, sizes, flags, 0)
                for group in range(sizes.own_groups):
                    value = spheres[0].free(group) + spheres[0].weight(group) * total[group]
                    for body_row in range(6):
                        velocity_ref[body_row, pl.ds(group, 1), :] = value[body_row : body_row + 1]
            else:
                sums = [joined(sections, spheres, sizes, flags, slot) for slot in range(slots)]
                owns = [sets[slot][0] for slot in range(slots)]
                put_velocities(sums, spheres, maps, flags, owns, section_ref, first_ref, second_ref)

        if last:
            shapes = [(3, blocks, LANES), (6, sizes.own_groups, LANES)]
        else:
            shapes = [state_shape, state_shape, section_shape, sent_shape, sent_shape]
        return call(body, shapes, chosen(parts, grad, *inputs, state, earlier), [held_sections, *work, *work])

    state = earlier = None
    section, *sent = first_velocities()
    for iteration in range(ITERS):
        grad, parts = gradients(section, sent, swap(*sent), state)
        parts = lax.all_to_all(parts, "xy", 0, 0, tiled=True)
        if iteration + 1 < ITERS:
            earlier, state, section, *sent = updates(parts, grad, state, earlier, factors[iteration + 1])
    result, velocity = updates(parts, grad, state, earlier, None)
    return (
        result.reshape(1, 1, 3, sizes.contacts),
        velocity.reshape(1, 1, 6, sizes.own),
    )


def solution(mesh):
    placed = (
        P("gz", "xy", None, None),
        P("gz", "xy", None, None),
        P("gz", "xy", None, None),
        P("gz", "xy", None, None),
        P("gz", "xy", None, None),
        P("gz", "xy", None),
        P("gz", "xy", None),
        P("gz", "xy", None),
        P("gz", "xy", None),
        P("gz", "xy", None),
        P("gz", "xy", None),
        P("gz", "xy", None),
        P("gz", "xy", None, None),
    )
    return jax.shard_map(
        on_device,
        mesh=mesh,
        in_specs=placed,
        out_specs=(P("gz", "xy", None, None), P("gz", "xy", None, None)),
        check_vma=False,
    )
```
